32 devices in a mesh: fsdp: 8 (over z, x), tp: 4 (over y, core).
Axes of the slice: x: 2, y: 2, z: 4, core: 2. Of those that a mesh axis runs over, the one named last changes fastest.
Arguments:
- hidden: bfloat16 [8192, 1536], P(('fsdp', 'tp')), may hold values from -6 to 6
- segment_ids: int32 [8, 1024], P('fsdp'), may hold values from 0 to 4, as said below
- cotangent: bfloat16 [8192, 1536], P(('fsdp', 'tp')), may hold values from -6 to 6
- norm_gain: bfloat16 [2, 1536], P(None, ('fsdp', 'tp')), may hold values from 0.25 to 1.75
- in_zx: bfloat16 [2, 1536, 2, 3072], P(None, 'fsdp', None, 'tp'), may hold values from -0.15625 to 0.15625
- in_dt: bfloat16 [2, 1536, 48], P(None, 'fsdp', 'tp'), may hold values from -0.15625 to 0.15625
- in_bc: bfloat16 [2, 1536, 256], P(None, ('fsdp', 'tp')), may hold values from -0.15625 to 0.15625
- conv_x: bfloat16 [2, 3072, 4], P(None, 'tp'), may hold values from -3 to 3
- conv_x_bias: bfloat16 [2, 3072], P(None, 'tp'), may hold values from -3 to 3
- conv_bc: bfloat16 [2, 256, 4], P(None, ('fsdp', 'tp')), may hold values from -3 to 3
- conv_bc_bias: bfloat16 [2, 256], P(None, ('fsdp', 'tp')), may hold values from -3 to 3
- dt_bias: bfloat16 [2, 48], P(None, 'tp'), may hold values from -6 to -2
- a_log: bfloat16 [2, 48], P(None, 'tp'), may hold values from 0 to 2.765625
- skip_d: bfloat16 [2, 48], P(None, 'tp'), may hold values from 0.5 to 1.5
- gated_gain: bfloat16 [2, 3072], P(None, 'tp'), may hold values from 0.25 to 1.75
- out_wt: bfloat16 [2, 1536, 3072], P(None, 'fsdp', 'tp'), may hold values from -0.109375 to 0.109375
Outputs:
- out_hidden: float32 [8192, 1536], P(('fsdp', 'tp'))
- grad_hidden: float32 [8192, 1536], P(('fsdp', 'tp'))
- grad_norm_gain: float32 [2, 1536], P(None, ('fsdp', 'tp'))
- grad_in_zx: float32 [2, 1536, 2, 3072], P(None, 'fsdp', None, 'tp')
- grad_in_dt: float32 [2, 1536, 48], P(None, 'fsdp', 'tp')
- grad_in_bc: float32 [2, 1536, 256], P(None, ('fsdp', 'tp'))
- grad_conv_x: float32 [2, 3072, 4], P(None, 'tp')
- grad_conv_x_bias: float32 [2, 3072], P(None, 'tp')
- grad_conv_bc: float32 [2, 256, 4], P(None, ('fsdp', 'tp'))
- grad_conv_bc_bias: float32 [2, 256], P(None, ('fsdp', 'tp'))
- grad_dt_bias: float32 [2, 48], P(None, 'tp')
- grad_a_log: float32 [2, 48], P(None, 'tp')
- grad_skip_d: float32 [2, 48], P(None, 'tp')
- grad_gated_gain: float32 [2, 3072], P(None, 'tp')
- grad_out_wt: float32 [2, 1536, 3072], P(None, 'fsdp', 'tp')
The draws below stay inside these ranges and needn't reach their ends.
Inputs may be any that keep to these rules, and one draw needn't show every extreme that they name: `segment_ids`: along each sequence the ids never fall, start at 0 and end at 4; a document may span several blocks.
All inputs are finite; a program needn't handle non-finite values.
Results may differ from the reference program's by a relative error of at most 0.017.
Values may be sent and summed in bfloat16 or wider, within the bound.
No kernel may reach another device: no remote copies, remote signals or barrier semaphores. Data moves between devices by JAX's collectives and lax.ppermute only.
A program may use at most 256 MiB of HBM per device.

```python
import jax
import jax.numpy as jnp
from jax import lax

D = 1536
HEADS = 48
STATE = 128
CONV = 4
BLOCK = 256
LAYERS = 2
LENGTH = 1024
INNER = 3072
SEQS = 8
TOKENS = 8192


def draw_segment_ids(key, part):
    key = jax.random.fold_in(key, 11)
    cuts = jax.random.randint(key, (SEQS, 4), 1, LENGTH)
    places = jnp.arange(LENGTH)
    return jnp.sum((cuts[:, None, :] <= places[None, :, None]).astype(jnp.int32), -1).astype(jnp.int32)


def shard_levels(rng, extent, split, low, largest):
    def one(dim, blocks):
        steps = jax.random.uniform(jax.random.fold_in(jax.random.fold_in(rng, 6), dim), (blocks,), jnp.float32, low / len(split), largest / len(split))
        return jnp.repeat(jnp.exp(steps), extent[dim] // blocks).reshape((-1,) + (1,) * (len(extent) - dim - 1))

    gain = one(*split[0])
    for cut in split[1:]:
        gain = gain * one(*cut)
    return gain


def gaussian(stream_key, dims, scale, bound, cuts=(), kind=jnp.bfloat16):
    entries = scale * jax.random.normal(stream_key, dims, jnp.float32)
    if cuts:
        entries = entries * shard_levels(stream_key, dims, cuts, -0.22, 0.18)
    return jnp.clip(entries, -bound, bound).astype(kind)


def setup_inputs(seed: int = 0) -> dict:
    key_list = jax.random.split(jax.random.key(seed), 17)
    return {
        "hidden": gaussian(key_list[0], (TOKENS, D), 1.0, 6.0, ((0, 32),)),
        "segment_ids": draw_segment_ids(jax.random.fold_in(key_list[16], 71), 0),
        "cotangent": gaussian(key_list[2], (TOKENS, D), 1.0, 6.0, ((0, 32),)),
        "norm_gain": jnp.clip(1.0 + 0.15 * jax.random.normal(key_list[3], (LAYERS, D), jnp.float32), 0.25, 1.75).astype(jnp.bfloat16),
        "in_zx": gaussian(key_list[4], (LAYERS, D, 2, INNER), D ** -0.5, 0.15625, ((1, 8), (3, 4))),
        "in_dt": gaussian(key_list[5], (LAYERS, D, HEADS), D ** -0.5, 0.15625, ((1, 8), (2, 4))),
        "in_bc": gaussian(key_list[6], (LAYERS, D, 2 * STATE), D ** -0.5, 0.15625, ((1, 32),)),
        "conv_x": gaussian(key_list[7], (LAYERS, INNER, CONV), CONV ** -0.5, 3.0, ((1, 4),)),
        "conv_x_bias": gaussian(key_list[8], (LAYERS, INNER), 0.5, 3.0, ((1, 4),)),
        "conv_bc": gaussian(key_list[9], (LAYERS, 2 * STATE, CONV), CONV ** -0.5, 3.0, ((1, 32),)),
        "conv_bc_bias": gaussian(key_list[10], (LAYERS, 2 * STATE), 0.5, 3.0, ((1, 32),)),
        "dt_bias": jnp.clip(-6.0 + 4.0 * jax.random.uniform(key_list[11], (LAYERS, HEADS), jnp.float32) ** shard_levels(key_list[11], (LAYERS, HEADS), ((1, 4),), -0.2, 0.2), -6.0, -2.0).astype(jnp.bfloat16),
        "a_log": jnp.clip(2.765625 * jax.random.uniform(key_list[12], (LAYERS, HEADS), jnp.float32) ** shard_levels(key_list[12], (LAYERS, HEADS), ((1, 4),), -0.2, 0.2), 0.0, 2.765625).astype(jnp.bfloat16),
        "skip_d": jnp.clip(0.5 + 1.0 * jax.random.uniform(key_list[13], (LAYERS, HEADS), jnp.float32) ** shard_levels(key_list[13], (LAYERS, HEADS), ((1, 4),), -0.2, 0.2), 0.5, 1.5).astype(jnp.bfloat16),
        "gated_gain": jnp.clip(1.0 + 0.15 * jax.random.normal(key_list[14], (LAYERS, INNER), jnp.float32), 0.25, 1.75).astype(jnp.bfloat16),
        "out_wt": gaussian(key_list[15], (LAYERS, D, INNER), INNER ** -0.5, 0.109375, ((1, 8), (2, 4))),
    }


EPS = 1e-05
HIGH = lax.Precision.HIGHEST

@jax.custom_vjp
def low(v):
    return lax.optimization_barrier(v.astype(jnp.bfloat16)).astype(jnp.float32)

@jax.custom_vjp
def low_back(v):
    return v

def low_keep(v):
    return (low(v), None)

def low_pass(kept, grad):
    return (grad,)

def back_keep(v):
    return (v, None)

def back_low(kept, grad):
    return (low(grad),)
low.defvjp(low_keep, low_pass)
low_back.defvjp(back_keep, back_low)

def rms_norm(values, weight):
    return values * lax.rsqrt(lax.optimization_barrier(jnp.mean(values * values, -1, keepdims=True)) + EPS) * weight

def segment_conv(values, weight, offset_bias, segment):
    length = values.shape[0]
    kernel = weight.shape[1]
    result = jnp.zeros_like(values) + offset_bias[None, :]
    for back_by in range(kernel):
        moved = jnp.pad(values, ((back_by, 0), (0, 0)))[:length]
        moved_seg = jnp.pad(segment, (back_by, 0), constant_values=-1)[:length]
        agree = (moved_seg == segment).astype(values.dtype)
        result = result + moved * agree[:, None] * weight[None, :, kernel - 1 - back_by]
    return result

def block_scan(scaled_x, log_decay, b_rows, c_rows, segment):
    length, heads, width = scaled_x.shape
    blocks = length // BLOCK
    where_tok = jnp.arange(BLOCK)
    causal = where_tok[:, None] >= where_tok[None, :]

    def scan_step(carry, pieces):
        running, before_seg = carry
        piece_x, piece_decay, piece_b, piece_c, piece_seg = pieces
        totals = jnp.cumsum(piece_decay, 0)
        joined = (piece_seg[:, None] == piece_seg[None, :]) & causal
        spread = totals[:, None, :] - totals[None, :, :]
        weights = jnp.exp(jnp.where(joined[:, :, None], spread, 0.0)) * joined.astype(scaled_x.dtype)[:, :, None]
        scores = jnp.dot(piece_c, piece_b.T, precision=HIGH)
        inside = jnp.einsum('tsh,shp->thp', weights * scores[:, :, None], piece_x, precision=HIGH)
        carried = (piece_seg == before_seg).astype(scaled_x.dtype)
        entering = jnp.einsum('tn,hpn->thp', piece_c, running, precision=HIGH) * (jnp.exp(totals) * carried[:, None])[:, :, None]
        last_seg = piece_seg[BLOCK - 1]
        tail_rate = jnp.exp(totals[BLOCK - 1][None, :] - totals) * (piece_seg == last_seg).astype(scaled_x.dtype)[:, None]
        keep_old = jnp.exp(totals[BLOCK - 1]) * (last_seg == before_seg).astype(scaled_x.dtype)
        running = running * keep_old[:, None, None] + jnp.einsum('sh,shp,sn->hpn', tail_rate, piece_x, piece_b, precision=HIGH)
        return ((running, last_seg), inside + entering)
    initial = (jnp.zeros((heads, width, b_rows.shape[1]), scaled_x.dtype), segment[0])
    pieces = (scaled_x.reshape(blocks, BLOCK, heads, width), log_decay.reshape(blocks, BLOCK, heads), b_rows.reshape(blocks, BLOCK, -1), c_rows.reshape(blocks, BLOCK, -1), segment.reshape(blocks, BLOCK))
    finished, outputs = lax.scan(jax.checkpoint(scan_step), initial, pieces)
    return outputs.reshape(length, heads, width)

def mixer_local(gate_z, input_x, raw_dt, raw_bc, conv_w, conv_b, shared_w, shared_b, dt_shift, log_rate, skip_gain, segment=None):
    heads = dt_shift.shape[0]
    length = input_x.shape[0]
    width = input_x.shape[1] // heads
    states = shared_w.shape[0] // 2
    conv_x_out = jax.nn.silu(segment_conv(input_x, conv_w, conv_b, segment))
    conv_bc_out = jax.nn.silu(segment_conv(raw_bc, shared_w, shared_b, segment))
    step_size = jax.nn.softplus(raw_dt + dt_shift[None, :])
    log_decay = -step_size * jnp.exp(log_rate)[None, :]
    signal = conv_x_out.reshape(length, heads, width)
    scanned = block_scan(signal * step_size[:, :, None], log_decay, conv_bc_out[:, :states], conv_bc_out[:, states:], segment)
    mixed = scanned + skip_gain[None, :, None] * signal
    return mixed.reshape(length, heads * width) * jax.nn.silu(gate_z)

def mamba_block(values, segment, pre_gain, w_zx, w_dt, w_bc, conv_w, conv_b, shared_w, shared_b, dt_shift, log_rate, skip_gain, post_gain, w_out):
    normed = low(rms_norm(values, pre_gain))
    gate_input = low_back(jnp.einsum('td,dkc->tkc', normed, w_zx, precision=HIGH))
    raw_dt = low_back(jnp.dot(normed, w_dt, precision=HIGH))
    raw_bc = low_back(jnp.dot(normed, w_bc, precision=HIGH))
    mixed = mixer_local(gate_input[:, 0], gate_input[:, 1], raw_dt, raw_bc, conv_w, conv_b, shared_w, shared_b, dt_shift, log_rate, skip_gain, segment=segment)
    scaled = low(rms_norm(mixed, post_gain))
    branch = low_back(jnp.dot(scaled, w_out.T, precision=HIGH))
    return values + branch

def reference(hidden, segment_ids, cotangent, norm_gain, in_zx, in_dt, in_bc, conv_x, conv_x_bias, conv_bc, conv_bc_bias, dt_bias, a_log, skip_d, gated_gain, out_wt):
    weights = tuple((member.astype(jnp.float32) for member in (norm_gain, in_zx, in_dt, in_bc, conv_x, conv_x_bias, conv_bc, conv_bc_bias, dt_bias, a_log, skip_d, gated_gain, out_wt)))

    def forward(start_values, params):

        def one_seq(seq_pair):
            values, segment = seq_pair
            for depth_at in range(LAYERS):
                values = mamba_block(values, segment, *[member[depth_at] for member in params])
            return values
        sequences = start_values.reshape(SEQS, LENGTH, D)
        return lax.map(jax.checkpoint(one_seq), (sequences, segment_ids)).reshape(SEQS * LENGTH, D)
    output, pull_back = jax.vjp(forward, hidden.astype(jnp.float32), weights)
    grad_start, grad_weights = pull_back(cotangent.astype(jnp.float32))
    return (output, grad_start, grad_weights[0], grad_weights[1], grad_weights[2], grad_weights[3], grad_weights[4], grad_weights[5], grad_weights[6], grad_weights[7], grad_weights[8], grad_weights[9], grad_weights[10], grad_weights[11], grad_weights[12])
```

```python
import jax
import jax.numpy as jnp
from jax import lax
from jax.experimental import pallas as pl
from jax.experimental.pallas import tpu as pltpu
from jax.sharding import PartitionSpec as P

EPS = 1e-05
NEG = -1e30
F32 = jnp.float32
BF16 = jnp.bfloat16
WALK = (0, 2, 4, 6, 7, 5, 3, 1)
HEAD_ROWS = 16
VMEM = 56 * 1024 * 1024


def tp_swap(value, mask):
    size = lax.axis_size("tp")
    return lax.ppermute(value, "tp", [(at, at ^ mask) for at in range(size)])


def tp_gather(value):
    core = tp_swap(value, 1)
    across = tp_swap(value, 2)
    return [value, core, across, tp_swap(across, 1)]


def tp_reduce_own(slots):
    near = tp_swap(jnp.stack([slots[1], slots[3]]), 1)
    far = (slots[2].astype(F32) + near[1].astype(F32)).astype(slots[2].dtype)
    far = tp_swap(far, 2)
    return slots[0].astype(F32) + near[0].astype(F32) + far.astype(F32)


def tp_sum_slots(value):
    near = tp_swap(value, 1)
    value = value + jnp.stack([near[1], near[0], near[3], near[2]])
    far = tp_swap(value, 2)
    return value + jnp.stack([far[2], far[3], far[0], far[1]])


def tp_natural(slots, index):
    odd = (index & 1) == 1
    high = (index & 2) == 2
    pairs = [
        jnp.where(odd, slots[1], slots[0]),
        jnp.where(odd, slots[0], slots[1]),
        jnp.where(odd, slots[3], slots[2]),
        jnp.where(odd, slots[2], slots[3]),
    ]
    return [
        jnp.where(high, pairs[2], pairs[0]),
        jnp.where(high, pairs[3], pairs[1]),
        jnp.where(high, pairs[0], pairs[2]),
        jnp.where(high, pairs[1], pairs[3]),
    ]


def is_walk():
    return lax.axis_size("fsdp") == len(WALK)


def step_ring(value, by):
    size = len(WALK)
    return lax.ppermute(
        value, "fsdp", [(WALK[at], WALK[(at + by) % size]) for at in range(size)]
    )


def fsdp_gather(value):
    if not is_walk():
        return lax.all_gather(value, "fsdp", axis=0, tiled=False)
    half = value.shape[0] // 2
    ahead = behind = value
    slots = {0: value}
    for step in (1, 2, 3):
        behind = step_ring(behind, 1)
        ahead = step_ring(ahead, -1)
        slots[8 - step] = behind
        slots[step] = ahead
    slots[4] = jnp.concatenate(
        [step_ring(behind[:half], 1), step_ring(ahead[half:], -1)], 0
    )
    return jnp.stack([slots[at] for at in range(8)])


def fsdp_reduce(terms):
    if not is_walk():
        return lax.psum_scatter(terms, "fsdp", scatter_dimension=0, tiled=False).astype(F32)
    half = terms.shape[1] // 2
    kind = terms.dtype

    def add(left, right):
        return (left.astype(F32) + right.astype(F32)).astype(kind)

    forth = step_ring(terms[4, :half], 1)
    back = step_ring(terms[4, half:], -1)
    forth = step_ring(
        jnp.concatenate([add(terms[3, :half], forth), terms[3, half:]], 0), 1
    )
    back = step_ring(
        jnp.concatenate([terms[5, :half], add(terms[5, half:], back)], 0), -1
    )
    for step in (2, 1):
        forth = step_ring(add(terms[step], forth), 1)
        back = step_ring(add(terms[8 - step], back), -1)
    return terms[0].astype(F32) + forth.astype(F32) + back.astype(F32)


def fsdp_sum(value):
    if not is_walk():
        return lax.psum(value, "fsdp")

    def swap(item, mask):
        return lax.ppermute(item, "fsdp", [(at, at ^ mask) for at in range(8)])

    value = value + swap(value, 1)
    return value + swap(value, 2) + swap(value, 4) + swap(value, 6)


def walk_place():
    index = lax.axis_index("fsdp")
    place = jnp.zeros((), jnp.int32)
    for at, owner in enumerate(WALK):
        place = jnp.where(index == owner, at, place)
    return place


def to_walk(blocks, place):
    if not is_walk():
        return blocks
    ordered = [blocks[owner] for owner in WALK]
    for bit in (1, 2, 4):
        turn = (place & bit) == bit
        ordered = [jnp.where(turn, ordered[(at + bit) % 8], ordered[at]) for at in range(8)]
    return ordered


def from_walk(blocks, place):
    if not is_walk():
        return blocks
    for bit in (1, 2, 4):
        turn = (place & bit) == bit
        blocks = [jnp.where(turn, blocks[(at - bit) % 8], blocks[at]) for at in range(8)]
    natural = [None] * 8
    for at, owner in enumerate(WALK):
        natural[owner] = blocks[at]
    return natural


def columns_to_walk(value, place):
    count = lax.axis_size("fsdp")
    return jnp.concatenate(to_walk(jnp.split(value, count, 1), place), 1)


def columns_from_walk(value, place):
    count = lax.axis_size("fsdp")
    return jnp.concatenate(from_walk(jnp.split(value, count, 1), place), 1)


def dot(left, right):
    return jnp.dot(left, right, preferred_element_type=F32)


def dot_t(left, right):
    return lax.dot_general(left, right, (((1,), (1,)), ((), ())), preferred_element_type=F32)


def shifted_sum(value, sign):
    width = value.shape[1]
    lane = lax.broadcasted_iota(jnp.int32, value.shape, 1)
    by = 1
    while by < width:
        if sign > 0:
            value = value + jnp.where(lane >= by, pltpu.roll(value, by, 1), 0.0)
        else:
            value = value + jnp.where(lane < width - by, pltpu.roll(value, width - by, 1), 0.0)
        by *= 2
    return value


def conv_parts(cur, prev, weight, bias, marks):
    rows = cur.shape[0]
    ext = jnp.concatenate([prev, cur], 0)
    pre = bias + cur * weight[3:4]
    moved = []
    for back in (1, 2, 3):
        item = ext[8 - back : 8 - back + rows]
        moved.append(item)
        pre = pre + item * marks[back - 1] * weight[3 - back : 4 - back]
    return pre, moved


def rates(u, bias, rate, seg_rows):
    u = u + bias
    dt = jnp.maximum(u, 0.0) + jnp.log1p(jnp.exp(-jnp.abs(u)))
    log_dt = jnp.where(u < -15.0, u, jnp.log(dt))
    a = -dt * rate
    total = shifted_sum(a, 1)
    last = total[:, -1:]
    less = total - log_dt
    enter = jnp.exp(total) * seg_rows[1:2]
    tail = jnp.exp(last - less) * seg_rows[2:3]
    return u, dt, a, total, less, enter, tail


def as_columns(first, enter, tail):
    enter_hi = enter.astype(BF16).astype(F32)
    tail_hi = tail.astype(BF16).astype(F32)
    rest = jnp.zeros((128 - 5 * HEAD_ROWS, enter.shape[1]), F32)
    stacked = jnp.concatenate(
        [first, enter_hi, tail_hi, enter - enter_hi, tail - tail_hi, rest], 0
    )
    return stacked.T


def pair_masks(rows):
    lane = lax.broadcasted_iota(jnp.int32, (rows, 128), 1)
    return lane < 64, lane >= 64


def mix_forward(
    t_ref, x_ref, bc_ref, u_ref, sc_ref, sr_ref, cw_ref, cb_ref, bw_ref, bb_ref,
    db_ref, rate_ref, skip_ref, spread_ref, y_ref, state_ref, held, x_tail, bc_tail,
):
    del t_ref
    rows = x_ref.shape[1]
    pairs = x_ref.shape[2] // 128

    @pl.when(pl.program_id(0) == 0)
    def _():
        held[...] = jnp.zeros_like(held)
        x_tail[...] = jnp.zeros_like(x_tail)
        bc_tail[...] = jnp.zeros_like(bc_tail)

    sc = sc_ref[0]
    sr = sr_ref[0]
    marks = [sc[:, at : at + 1] for at in range(3)]
    x = x_ref[0]
    pre, _ = conv_parts(x, x_tail[...], cw_ref[...], cb_ref[...], marks)
    xc = pre * jax.nn.sigmoid(pre)
    x_tail[...] = x[rows - 8 :]
    raw = bc_ref[0]
    pre_bc, _ = conv_parts(raw, bc_tail[...], bw_ref[...], bb_ref[...], marks)
    bc = (pre_bc * jax.nn.sigmoid(pre_bc)).astype(BF16)
    bc_tail[...] = raw[rows - 8 :]
    states = bc.shape[1] // 2
    b_rows, c_rows = bc[:, :states], bc[:, states:]

    _, _, _, total, less, enter, tail = rates(u_ref[0], db_ref[...], rate_ref[...], sr)
    cols = as_columns(total, enter, tail)
    cols_low = cols.astype(BF16)
    enter_x = dot(cols_low, spread_ref[0])
    tail_x = dot(cols_low, spread_ref[1])

    at_t = lax.broadcasted_iota(jnp.int32, (rows, rows), 0)
    at_s = lax.broadcasted_iota(jnp.int32, (rows, rows), 1)
    bar = jnp.where((sc[:, 3:4] == sr[0:1]) & (at_t >= at_s), 0.0, NEG)
    scores = dot_t(c_rows, b_rows)
    state = held[...]
    state_ref[0] = state
    entering = dot(c_rows, state.astype(BF16)) * enter_x
    xl = xc.astype(BF16)
    low_mask, high_mask = pair_masks(rows)
    zero = jnp.zeros((rows, 128), BF16)
    for pair in range(pairs):
        span = slice(pair * 128, pair * 128 + 128)
        part = xl[:, span]
        acc = entering[:, span] + xc[:, span] * skip_ref[:, span]
        for side, mask in ((0, low_mask), (1, high_mask)):
            head = 2 * pair + side
            weights = jnp.exp(cols[:, head : head + 1] - less[head : head + 1] + bar) * scores
            acc = acc + dot(weights.astype(BF16), jnp.where(mask, part, zero))
        y_ref[0, :, span] = acc
    keep = enter_x[rows - 1 : rows]
    held[...] = state * keep + dot(
        b_rows.astype(F32).T.astype(BF16), (xc * tail_x).astype(BF16)
    )


def mix_backward(
    t_ref, x_ref, xp_ref, bc_ref, bp_ref, u_ref, sc_ref, sr_ref, y_ref, dy_ref, state_ref,
    cw_ref, cb_ref, bw_ref, bb_ref, db_ref, rate_ref, skip_ref, spread_ref, heads_ref,
    dx_ref, dbc_ref, du_ref, gx_ref, gbc_ref, gh_ref, held, x_next, bc_next,
):
    del t_ref
    rows = x_ref.shape[1]
    width = x_ref.shape[2]
    pairs = width // 128

    @pl.when(pl.program_id(0) == 0)
    def _():
        held[...] = jnp.zeros_like(held)
        x_next[...] = jnp.zeros_like(x_next)
        bc_next[...] = jnp.zeros_like(bc_next)
        gx_ref[...] = jnp.zeros_like(gx_ref)
        gbc_ref[...] = jnp.zeros_like(gbc_ref)
        gh_ref[...] = jnp.zeros_like(gh_ref)

    sc = sc_ref[0]
    sr = sr_ref[0]
    marks = [sc[:, at : at + 1] for at in range(3)]
    x = x_ref[0]
    pre, x_moved = conv_parts(x, xp_ref[0], cw_ref[...], cb_ref[...], marks)
    sig = jax.nn.sigmoid(pre)
    xc = pre * sig
    raw = bc_ref[0]
    pre_bc, bc_moved = conv_parts(raw, bp_ref[0], bw_ref[...], bb_ref[...], marks)
    sig_bc = jax.nn.sigmoid(pre_bc)
    bc = (pre_bc * sig_bc).astype(BF16)
    states = bc.shape[1] // 2
    b_rows, c_rows = bc[:, :states], bc[:, states:]

    u, dt, a, total, less, enter, tail = rates(u_ref[0], db_ref[...], rate_ref[...], sr)
    cols = as_columns(less, enter, tail)
    cols_low = cols.astype(BF16)
    enter_x = dot(cols_low, spread_ref[0])
    tail_x = dot(cols_low, spread_ref[1])
    keep = enter_x[rows - 1 : rows]

    at_s = lax.broadcasted_iota(jnp.int32, (rows, rows), 0)
    at_t = lax.broadcasted_iota(jnp.int32, (rows, rows), 1)
    bar = jnp.where((sc[:, 3:4] == sr[0:1]) & (at_t >= at_s), 0.0, NEG)
    scores = dot_t(b_rows, c_rows)

    dy = dy_ref[0]
    dyl = dy.astype(BF16)
    xl = xc.astype(BF16)
    state = state_ref[0]
    d_state = held[...]
    d_state_low = d_state.astype(BF16)
    entered = (dy * enter_x).astype(BF16)
    dc = dot_t(entered, state.astype(BF16))
    db = dot_t((xc * tail_x).astype(BF16), d_state_low)
    dx_tail = dot(b_rows, d_state_low) * tail_x
    x_round = xl.astype(F32)
    last_terms = jnp.sum(x_round * dx_tail, 0, keepdims=True) + keep * jnp.sum(
        state * d_state, 0, keepdims=True
    )
    held[...] = keep * d_state + dot(c_rows.astype(F32).T.astype(BF16), entered)

    low_mask, high_mask = pair_masks(rows)
    zero = jnp.zeros((rows, 128), BF16)
    d_scores = jnp.zeros((rows, rows), F32)
    d_scan = []
    for pair in range(pairs):
        span = slice(pair * 128, pair * 128 + 128)
        part, grad = xl[:, span], dyl[:, span]
        acc = dx_tail[:, span]
        for side, mask in ((0, low_mask), (1, high_mask)):
            head = 2 * pair + side
            decay = jnp.exp(total[head : head + 1] - cols[:, head : head + 1] + bar)
            weights = (decay * scores).astype(BF16)
            d_scores = d_scores + decay * dot_t(jnp.where(mask, part, zero), grad)
            acc = acc + dot(weights, jnp.where(mask, grad, zero))
        d_scan.append(acc)
    d_scan = jnp.concatenate(d_scan, 1)
    db = db + dot(d_scores.astype(BF16), c_rows)
    dc = dc + dot(d_scores.T.astype(BF16), b_rows)

    skip = skip_ref[...]
    from_x = x_round * d_scan
    from_t = dyl.astype(F32) * (y_ref[0] - skip * xc) - from_x
    row_at = lax.broadcasted_iota(jnp.int32, (rows, width), 0)
    from_t = from_t + jnp.where(row_at == rows - 1, last_terms, 0.0)

    def per_head(value):
        high = value.astype(BF16)
        return dot_t(heads_ref[...], high) + dot_t(
            heads_ref[...], (value - high.astype(F32)).astype(BF16)
        )

    q = per_head(from_x)
    da = shifted_sum(per_head(from_t), -1)
    slope = jax.nn.sigmoid(u)
    ratio = jnp.where(u < -15.0, 1.0, slope / dt)
    du = q * ratio - da * rate_ref[...] * slope
    du_ref[0] = du
    gh_ref[0] += jnp.sum(du, 1, keepdims=True)
    gh_ref[1] += jnp.sum(da * a, 1, keepdims=True)

    def conv_back(d_out, cur, moved, weight, carried, grads):
        grads[3:4] += jnp.sum(d_out * cur, 0, keepdims=True)
        grads[4:5] += jnp.sum(d_out, 0, keepdims=True)
        result = d_out * weight[3:4]
        for back in (1, 2, 3):
            kept = d_out * marks[back - 1]
            grads[3 - back : 4 - back] += jnp.sum(kept * moved[back - 1], 0, keepdims=True)
            ext = jnp.concatenate([kept, carried[back - 1]], 0)
            result = result + ext[back : back + rows] * weight[3 - back : 4 - back]
            carried[back - 1] = kept[:8]
        return result

    gx_ref[5:6] += jnp.sum(dy * xc, 0, keepdims=True)
    d_pre = (d_scan + skip * dy) * (sig * (1.0 + pre * (1.0 - sig)))
    dx_ref[0] = conv_back(d_pre, x, x_moved, cw_ref[...], x_next, gx_ref).astype(BF16)
    d_bc = jnp.concatenate([db, dc], 1) * (sig_bc * (1.0 + pre_bc * (1.0 - sig_bc)))
    dbc_ref[0] = conv_back(d_bc, raw, bc_moved, bw_ref[...], bc_next, gbc_ref).astype(BF16)


def whole_spec(shape):
    return pl.BlockSpec(shape, lambda at, t: (0,) * len(shape))


def run_forward(place, x, bc, u, seg_cols, seg_rows, small):
    blocks, rows, width = x.shape
    wide = bc.shape[2]
    states = wide // 2

    def slot(shape):
        return pl.BlockSpec((1,) + shape, lambda at, t: (at ^ t[0], 0, 0))

    def straight(shape):
        return pl.BlockSpec((1,) + shape, lambda at, t: (at, 0, 0))

    spec = pltpu.PrefetchScalarGridSpec(
        num_scalar_prefetch=1,
        grid=(blocks,),
        in_specs=[
            slot((rows, width)), slot((rows, wide)), slot((HEAD_ROWS, rows)),
            straight((rows, 8)), straight((8, rows)),
        ] + [whole_spec(item.shape) for item in small],
        out_specs=[slot((rows, width)), straight((states, width))],
        scratch_shapes=[
            pltpu.VMEM((states, width), F32),
            pltpu.VMEM((8, width), F32),
            pltpu.VMEM((8, wide), F32),
        ],
    )
    return pl.pallas_call(
        mix_forward,
        grid_spec=spec,
        out_shape=[
            jax.ShapeDtypeStruct((blocks, rows, width), F32),
            jax.ShapeDtypeStruct((blocks, states, width), F32),
        ],
        compiler_params=pltpu.CompilerParams(
            dimension_semantics=("arbitrary",), vmem_limit_bytes=VMEM
        ),
        cost_estimate=pl.CostEstimate(flops=3 * 10**9, bytes_accessed=10**7, transcendentals=4 * 10**6),
        name="mix_forward",
    )(place, x, bc, u, seg_cols, seg_rows, *small)


def run_backward(place, x, bc, u, seg_cols, seg_rows, y, dy, state, small, heads_of):
    blocks, rows, width = x.shape
    wide = bc.shape[2]
    states = wide // 2
    last = blocks - 1

    def slot(shape):
        return pl.BlockSpec((1,) + shape, lambda at, t: ((last - at) ^ t[0], 0, 0))

    def before(shape):
        return pl.BlockSpec(
            (1,) + shape,
            lambda at, t: (jnp.maximum(last - at - 1, 0) ^ t[0], rows // 8 - 1, 0),
        )

    def straight(shape):
        return pl.BlockSpec((1,) + shape, lambda at, t: (last - at, 0, 0))

    spec = pltpu.PrefetchScalarGridSpec(
        num_scalar_prefetch=1,
        grid=(blocks,),
        in_specs=[
            slot((rows, width)), before((8, width)), slot((rows, wide)), before((8, wide)),
            slot((HEAD_ROWS, rows)), straight((rows, 8)), straight((8, rows)),
            slot((rows, width)), slot((rows, width)), straight((states, width)),
        ] + [whole_spec(item.shape) for item in small] + [whole_spec(heads_of.shape)],
        out_specs=[
            slot((rows, width)), slot((rows, wide)), slot((HEAD_ROWS, rows)),
            whole_spec((8, width)), whole_spec((8, wide)), whole_spec((2, HEAD_ROWS, 128)),
        ],
        scratch_shapes=[
            pltpu.VMEM((states, width), F32),
            pltpu.VMEM((3, 8, width), F32),
            pltpu.VMEM((3, 8, wide), F32),
        ],
    )
    return pl.pallas_call(
        mix_backward,
        grid_spec=spec,
        out_shape=[
            jax.ShapeDtypeStruct((blocks, rows, width), BF16),
            jax.ShapeDtypeStruct((blocks, rows, wide), BF16),
            jax.ShapeDtypeStruct((blocks, HEAD_ROWS, rows), F32),
            jax.ShapeDtypeStruct((8, width), F32),
            jax.ShapeDtypeStruct((8, wide), F32),
            jax.ShapeDtypeStruct((2, HEAD_ROWS, 128), F32),
        ],
        compiler_params=pltpu.CompilerParams(
            dimension_semantics=("arbitrary",), vmem_limit_bytes=VMEM
        ),
        cost_estimate=pl.CostEstimate(flops=8 * 10**9, bytes_accessed=2 * 10**7, transcendentals=5 * 10**6),
        name="mix_backward",
    )(place, x, x, bc, bc, u, seg_cols, seg_rows, y, dy, state, *small, heads_of)


def segment_tables(segment, blocks):
    rows = segment.shape[0] // blocks
    marks = [
        jnp.concatenate([jnp.zeros((back,), F32), (segment[back:] == segment[:-back]).astype(F32)])
        for back in (1, 2, 3)
    ]
    cut = segment.reshape(blocks, rows)
    ends = cut[:, -1]
    before = jnp.concatenate([cut[:1, 0], ends[:-1]])
    carried = (cut == before[:, None]).astype(F32)
    is_last = (cut == ends[:, None]).astype(F32)
    ids = cut.astype(F32)
    nothing = jnp.zeros_like(ids)
    cols = jnp.stack(
        [item.reshape(blocks, rows) for item in marks] + [ids] + [nothing] * 4, 2
    )
    lines = jnp.stack([ids, carried, is_last] + [nothing] * 5, 1)
    return cols, lines


def head_tables(heads, width):
    owner = jnp.arange(width)[None, :] // (width // heads)
    at = jnp.arange(128)[:, None]
    spread_enter = (at == owner + HEAD_ROWS) | (at == owner + 3 * HEAD_ROWS)
    spread_tail = (at == owner + 2 * HEAD_ROWS) | (at == owner + 4 * HEAD_ROWS)
    spread = jnp.stack([spread_enter, spread_tail]).astype(BF16)
    return spread, (at[:HEAD_ROWS] == owner).astype(BF16)


def head_column(value):
    return jnp.pad(value.astype(F32), (0, HEAD_ROWS - value.shape[0]))[:, None]


def norm_scale_of(values):
    return lax.rsqrt(jnp.mean(values * values, -1, keepdims=True) + EPS)


def shards(
    hidden, segment_ids, cotangent, norm_gain, in_zx, in_dt, in_bc, conv_x, conv_x_bias,
    conv_bc, conv_bc_bias, dt_bias, a_log, skip_d, gated_gain, out_wt,
):
    layers = in_zx.shape[0]
    count = lax.axis_size("fsdp")
    tp_count = lax.axis_size("tp")
    tp_at = lax.axis_index("tp")
    place = walk_place()
    slot_at = tp_at.astype(jnp.int32)[None]
    own, features = hidden.shape
    deep = in_zx.shape[1]
    width = in_zx.shape[3]
    heads = in_dt.shape[2]
    wide = in_bc.shape[2]
    bc_deep = in_bc.shape[1]
    shared = conv_bc.shape[1]
    taps = conv_bc.shape[2]
    inner = width * tp_count

    start = columns_to_walk(hidden, place)
    all_start = jnp.stack(tp_gather(start))
    seg_cols, seg_rows = segment_tables(segment_ids[0], tp_count)
    spread, heads_of = head_tables(heads, width)

    w_x, w_z, w_o, w_dt, w_bc, gains, small = [], [], [], [], [], [], []
    for k in range(layers):
        tiny = jnp.concatenate(
            [norm_gain[k], conv_bc[k].reshape(-1), conv_bc_bias[k]], 0
        )
        tiny = jnp.pad(tiny, (0, wide - tiny.shape[0]))[None]
        pack = jnp.concatenate([in_bc[k], tiny], 0)
        x_all = fsdp_gather(in_zx[k, :, 1])
        pack_all = fsdp_gather(pack)
        dt_all = fsdp_gather(in_dt[k])
        z_all = fsdp_gather(in_zx[k, :, 0])
        o_all = fsdp_gather(out_wt[k])
        pack_all = jnp.stack(tp_natural(tp_gather(pack_all), tp_at), 1)
        w_x.append(x_all.reshape(features, width))
        w_z.append(z_all.reshape(features, width))
        w_o.append(o_all.reshape(features, width))
        w_dt.append(dt_all.reshape(features, heads))
        w_bc.append(pack_all[:, :, :bc_deep].reshape(features, wide))
        tiny = pack_all[:, :, bc_deep]
        gains.append(tiny[:, :, :bc_deep].reshape(1, features).astype(F32))
        rest = tiny[:, :, bc_deep:]
        rest = jnp.stack(from_walk([rest[at] for at in range(count)], place))
        taps_bc = rest[:, :, : shared * taps].reshape(wide, taps).astype(F32)
        bias_bc = rest[:, :, shared * taps : shared * (taps + 1)].reshape(1, wide).astype(F32)
        small.append(
            (
                conv_x[k].astype(F32).T,
                conv_x_bias[k].astype(F32)[None],
                taps_bc.T,
                bias_bc,
                head_column(dt_bias[k]),
                jnp.exp(head_column(a_log[k])),
                jnp.repeat(skip_d[k].astype(F32), width // heads)[None],
                spread,
            )
        )

    def project(rows, weight):
        return lax.dot_general(
            rows, weight, (((2,), (0,)), ((), ())), preferred_element_type=F32
        )

    def step_inputs(rows, weight):
        result = lax.dot_general(
            weight, rows, (((0,), (2,)), ((), ())), preferred_element_type=F32
        )
        result = jnp.swapaxes(result, 0, 1)
        return jnp.pad(result, ((0, 0), (0, HEAD_ROWS - heads), (0, 0)))

    running = start.astype(F32)
    saved = []
    for k in range(layers):
        if k == 0:
            wide_start = all_start.astype(F32)
            rows = (wide_start * norm_scale_of(wide_start) * gains[0]).astype(BF16)
        else:
            rows = (running * norm_scale_of(running) * gains[k]).astype(BF16)
            rows = jnp.stack(tp_gather(rows))
        raw_x = project(rows, w_x[k])
        raw_bc = project(rows, w_bc[k])
        raw_u = step_inputs(rows, w_dt[k])
        y, state = run_forward(slot_at, raw_x, raw_bc, raw_u, seg_cols, seg_rows, small[k])
        z = project(rows, w_z[k])
        v = y * jax.nn.silu(z)
        squares = jnp.sum(v * v, -1)
        gain = gated_gain[k].astype(F32)
        entry = dict(rows=rows, x=raw_x, bc=raw_bc, u=raw_u, y=y, z=z, v=v, state=state, h=running)
        partial = lax.dot_general(
            (v * gain).astype(BF16), w_o[k], (((2,), (1,)), ((), ())), preferred_element_type=F32
        ).astype(BF16)
        branch = tp_reduce_own([partial[at] for at in range(tp_count)])
        if k < layers - 1:
            scale = lax.rsqrt(tp_sum_slots(squares) / inner + EPS)
            entry["scale"] = scale
            entry["branch"] = branch
            running = running + branch * scale[0][:, None]
        else:
            entry["squares"] = squares
            entry["branch"] = branch
        saved.append(entry)

    grad_run = columns_to_walk(cotangent, place).astype(F32)
    collected = [[None] * layers for _ in range(13)]
    for k in reversed(range(layers)):
        item = saved[k]
        rows, v, z, y = item["rows"], item["v"], item["z"], item["y"]
        gain = gated_gain[k].astype(F32)
        grad_low = grad_run.astype(BF16)
        if k < layers - 1:
            cross_own = jnp.sum(grad_low.astype(F32) * item["branch"], -1)
            cross = jnp.stack(tp_gather(cross_own))
            scale = item["scale"]
        cot = jnp.stack(tp_gather(grad_low))
        d_gated = project(cot, w_o[k])
        d_unit = d_gated * gain
        if k == layers - 1:
            sums = jnp.stack([item["squares"], jnp.sum(d_unit * v, -1)], 1)
            sums = tp_sum_slots(sums)
            scale = lax.rsqrt(sums[:, 0] / inner + EPS)
            cross = sums[:, 1]
            running = running + item["branch"] * scale[0][:, None]
        gated = (v * scale[:, :, None] * gain).astype(BF16)
        d_w_o = lax.dot_general(
            cot, gated, (((0, 1), (0, 1)), ((), ())), preferred_element_type=F32
        ).astype(BF16)
        sum_o = fsdp_reduce(d_w_o.reshape(count, deep, width))
        d_gain = jnp.sum(d_gated * v * scale[:, :, None], (0, 1))
        dv = d_unit * scale[:, :, None] - v * (scale**3 * cross / inner)[:, :, None]
        sig_z = jax.nn.sigmoid(z)
        dy = dv * (z * sig_z)
        dz = (dv * y * (sig_z * (1.0 + z * (1.0 - sig_z)))).astype(BF16)

        def weight_grad(grad):
            return lax.dot_general(
                rows, grad, (((0, 1), (0, 1)), ((), ())), preferred_element_type=F32
            )

        sum_z = fsdp_reduce(weight_grad(dz).astype(BF16).reshape(count, deep, width))
        dx, dbc, du, gx, gbc, gh = run_backward(
            slot_at, item["x"], item["bc"], item["u"], seg_cols, seg_rows, y, dy,
            item["state"], small[k], heads_of,
        )
        du_low = du[:, :heads].astype(BF16)

        def back(grad, weight):
            return lax.dot_general(
                grad, weight, (((2,), (1,)), ((), ())), preferred_element_type=F32
            )

        total = back(dz, w_z[k]) + back(dx, w_x[k]) + back(dbc, w_bc[k])
        total = total + lax.dot_general(
            du_low, w_dt[k], (((1,), (1,)), ((), ())), preferred_element_type=F32
        )
        d_gain_pre = jnp.sum(total * rows.astype(F32), (0, 1)) / gains[k][0]
        total = total.astype(BF16)
        d_normed = tp_reduce_own([total[at] for at in range(tp_count)])
        sum_x = fsdp_reduce(weight_grad(dx).astype(BF16).reshape(count, deep, width))
        h = item["h"]
        inv = norm_scale_of(h)
        scaled = d_normed * gains[k]
        grad_run = (
            grad_run
            + inv * scaled
            - h * (inv**3 * (jnp.sum(scaled * h, -1, keepdims=True) / features))
        )

        d_w_bc = weight_grad(dbc).reshape(count, tp_count, bc_deep, wide)
        d_w_dt = lax.dot_general(
            rows, du_low, (((0, 1), (0, 2)), ((), ())), preferred_element_type=F32
        )
        d_tiny = jnp.concatenate(
            [
                d_gain_pre.reshape(count, tp_count, bc_deep),
                jnp.stack(
                    to_walk(
                        list(
                            jnp.concatenate(
                                [
                                    gbc[:4].T.reshape(count, tp_count, shared * taps),
                                    gbc[4].reshape(count, tp_count, shared),
                                ],
                                2,
                            )
                        ),
                        place,
                    )
                ),
            ],
            2,
        )
        d_tiny = jnp.pad(d_tiny, ((0, 0), (0, 0), (0, wide - d_tiny.shape[2])))
        d_pack = jnp.concatenate([d_w_bc, d_tiny[:, :, None]], 2)
        d_slots = tp_natural([d_pack[:, at] for at in range(tp_count)], tp_at)
        d_pack = tp_reduce_own(d_slots)
        d_pack = jnp.concatenate(
            [d_pack.reshape(count, -1), d_w_dt.reshape(count, -1)], 1
        )
        d_pack = fsdp_reduce(d_pack)
        cut = (bc_deep + 1) * wide
        sum_pack = d_pack[:cut].reshape(bc_deep + 1, wide)
        sum_dt = d_pack[cut:].reshape(deep, heads)
        tiny = sum_pack[bc_deep]
        sum_pre = tiny[:bc_deep]
        sum_bc_w = tiny[bc_deep : bc_deep + shared * taps].reshape(shared, taps)
        sum_bc_b = tiny[bc_deep + shared * taps : bc_deep + shared * (taps + 1)]

        flat = jnp.concatenate([gx[:6], d_gain[None]], 0).reshape(-1, 128)
        flat = jnp.concatenate([flat, gh[0, :, 0:1].T.repeat(8, 1), gh[1, :, 0:1].T.repeat(8, 1)], 0)
        flat = fsdp_sum(flat)
        lines = width // 128
        sums = flat[: 7 * lines].reshape(7, width)
        layer_grads = (
            sum_pre,
            jnp.stack([sum_z, sum_x], 1),
            sum_dt,
            sum_pack[:bc_deep],
            sums[:4].T,
            sums[4],
            sum_bc_w,
            sum_bc_b,
            flat[7 * lines].reshape(-1, 8)[:heads, 0],
            flat[7 * lines + 1].reshape(-1, 8)[:heads, 0],
            jnp.sum(sums[5].reshape(heads, -1), 1),
            sums[6],
            sum_o,
        )
        for at in range(13):
            collected[at][k] = layer_grads[at]
    stacked = [jnp.stack(entry, 0) for entry in collected]
    return (
        columns_from_walk(running, place),
        columns_from_walk(grad_run, place),
        *stacked,
    )


def solution(mesh):
    tokens = P(("fsdp", "tp"), None)
    split = P(None, ("fsdp", "tp"))
    rows = P(None, ("fsdp", "tp"), None)
    weights = (
        split,
        P(None, "fsdp", None, "tp"),
        P(None, "fsdp", "tp"),
        rows,
        P(None, "tp", None),
        P(None, "tp"),
        rows,
        split,
        P(None, "tp"),
        P(None, "tp"),
        P(None, "tp"),
        P(None, "tp"),
        P(None, "fsdp", "tp"),
    )
    return jax.shard_map(
        shards,
        mesh=mesh,
        in_specs=(tokens, P("fsdp", None), tokens) + weights,
        out_specs=(tokens, tokens) + weights,
        check_vma=False,
    )
```

```python
from functools import partial

import jax
import jax.numpy as jnp
import numpy as np
from jax import lax
from jax.experimental import pallas as pl
from jax.experimental.pallas import tpu as pltpu
from jax.sharding import PartitionSpec as P

EPS = 1e-05
NEG = -1e30
F32 = jnp.float32
BF16 = jnp.bfloat16
WALK = (0, 2, 4, 6, 7, 5, 3, 1)
HEAD_ROWS = 16
VMEM = 56 * 1024 * 1024


def permute(value, axis, mask):
    size = lax.axis_size(axis)
    return lax.ppermute(value, axis, [(at, at ^ mask) for at in range(size)])


def tp_gather(value):
    across = permute(value, "tp", 2)
    core = permute(value, "tp", 1)
    return [value, core, across, permute(across, "tp", 1)]


def tp_reduce(send, keep):
    near = permute(send, "tp", 1)
    far = (keep[1].astype(F32) + near[1].astype(F32)).astype(keep.dtype)
    far = permute(far, "tp", 2)
    return keep[0].astype(F32) + near[0].astype(F32) + far.astype(F32)


def tp_sum_slots(value):
    near = permute(value, "tp", 1)
    value = value + jnp.stack([near[1], near[0], near[3], near[2]])
    far = permute(value, "tp", 2)
    return value + jnp.stack([far[2], far[3], far[0], far[1]])


def is_walk():
    return lax.axis_size("fsdp") == len(WALK)


def placement(tp_at):
    size = lax.axis_size("fsdp")
    if not is_walk():
        owners = jnp.arange(size, dtype=jnp.int32)
    else:
        all_owners = [[WALK[(WALK.index(f) + k) % size] for k in range(size)] for f in range(size)]
        owners = pick(jnp.array(all_owners, jnp.int32), lax.axis_index("fsdp"), 0)
    return jnp.concatenate([tp_at[None], owners])


def step_ring(value, by):
    size = len(WALK)
    return lax.ppermute(
        value, "fsdp", [(WALK[at], WALK[(at + by) % size]) for at in range(size)]
    )


def ring_pair(behind, ahead):
    return step_ring(behind, 1), step_ring(ahead, -1)


def ring_last(behind, ahead):
    half = behind.shape[0] // 2
    return step_ring(behind[:half], 1), step_ring(ahead[half:], -1)


def walk_weight(own, steps):
    arrays = [own]
    rows = own.shape[0]
    meta = [(0, 0, rows, 0, 0, True)]
    for at, (behind, ahead) in enumerate(steps):
        arrays += [behind, ahead]
        if at < 3:
            meta.append((len(arrays) - 2, 0, rows, 7 - at, 0, True))
            meta.append((len(arrays) - 1, 0, rows, 1 + at, 0, True))
        else:
            meta.append((len(arrays) - 2, 0, rows // 2, 4, 0, True))
            meta.append((len(arrays) - 1, 0, rows // 2, 4, rows // 2, True))
    return arrays, tuple(meta)


def natural_weight(array, count, deep, stride):
    return [array], tuple((0, at * stride, deep, at, 0, False) for at in range(count))


def after(value, *earlier):
    return lax.optimization_barrier((value,) + earlier)[0]


class RingGather:
    def __init__(self, own):
        self.own = own
        self.steps = []

    def step(self, *earlier):
        if not is_walk():
            return
        behind, ahead = self.steps[-1] if self.steps else (self.own, self.own)
        if earlier:
            behind, ahead, *_ = lax.optimization_barrier((behind, ahead) + earlier)
        go = ring_last if len(self.steps) == 3 else ring_pair
        self.steps.append(go(behind, ahead))

    def last(self):
        return self.steps[-1] if self.steps else ()

    def weight(self):
        if is_walk():
            return walk_weight(self.own, self.steps)
        whole = lax.all_gather(self.own, "fsdp", axis=0, tiled=True)
        deep = self.own.shape[0]
        return natural_weight(whole, lax.axis_size("fsdp"), deep, deep)


def double(value, axis, mask, dim):
    other = permute(value, axis, mask)
    second = (lax.axis_index(axis) & mask) != 0
    low = jnp.where(second, other, value)
    high = jnp.where(second, value, other)
    return jnp.concatenate([low, high], dim)


def plus(left, right):
    return (left.astype(F32) + right.astype(F32)).astype(left.dtype)


def pick(value, at, axis):
    return lax.dynamic_index_in_dim(value, at, axis, keepdims=False, allow_negative_indices=False)


def two_parts(value):
    high = value.astype(BF16)
    return jnp.concatenate([high, (value - high.astype(F32)).astype(BF16)], 0)


def joined(parts):
    half = parts.shape[0] // 2
    return parts[:half].astype(F32) + parts[half:].astype(F32)


class SmallSum:
    def __init__(self, terms, own, vector):
        index = lax.axis_index("tp")
        self.core, self.y = index & 1, index >> 1
        self.terms = terms.reshape((terms.shape[0], 2, 2) + terms.shape[2:])
        self.own, self.vector = own, vector
        self.wide = vector.shape[1]

    def over_core(self):
        return permute(pick(self.terms, 1 - self.core, 2), "tp", 1)

    def over_y(self, got):
        self.terms = plus(pick(self.terms, self.core, 2), got)
        return permute(pick(self.terms, 1 - self.y, 1), "tp", 2)

    def over_x(self, got):
        terms = plus(pick(self.terms, self.y, 1), got)
        self.terms = terms = jnp.concatenate([terms, self.own], 1)
        self.rows = rows = terms.shape[1]
        if not is_walk():
            return ()
        index = lax.axis_index("fsdp")
        self.x, self.z = index & 1, index >> 1
        self.terms = terms = terms.reshape((4, 2) + terms.shape[1:])
        got = pick(terms, 1 - self.x, 1).reshape(4 * rows, self.wide)
        return permute(jnp.concatenate([got, two_parts(self.vector)], 0), "fsdp", 1)

    def over_z(self, got):
        if not is_walk():
            return ()
        rows, terms = self.rows, self.terms
        self.vector = self.vector + joined(got[4 * rows :])
        got = got[: 4 * rows].reshape(4, rows, self.wide)
        mine = pick(terms, self.x, 1)
        self.total = pick(mine, self.z, 0).astype(F32) + pick(got, self.z, 0).astype(F32)
        sent = two_parts(self.vector)
        parts = []
        for mask in (3, 2, 1):
            part = plus(pick(mine, self.z ^ mask, 0), pick(got, self.z ^ mask, 0))
            parts.append(permute(jnp.concatenate([part, sent], 0), "fsdp", 2 * mask))
        return tuple(parts)

    def result(self, parts):
        if not is_walk():
            own = lax.psum_scatter(self.terms, "fsdp", scatter_dimension=0, tiled=False)
            return own.astype(F32), lax.psum(self.vector, "fsdp")
        total, vector = self.total, self.vector
        for part in parts:
            total = total + part[: self.rows].astype(F32)
            vector = vector + joined(part[self.rows :])
        return total, vector


class RingSum:
    def __init__(self, terms, table):
        self.terms = terms
        self.table = table
        self.at = 0
        self.sent = ()
        self.first = 0


def ring_payload(steps, firsts, which, t_ref, *refs):
    del t_ref
    terms, refs = refs[: 2 * len(steps)], refs[2 * len(steps) :]
    forth_out, back_out = refs[-2:]
    row = 0
    for at, step in enumerate(steps):
        ahead, behind = terms[2 * at][0], terms[2 * at + 1][0]
        deep = ahead.shape[0]
        half = deep // 2
        if step == 0:
            forth_out[row : row + half] = ahead[:half]
            back_out[row : row + half] = behind[half:]
            row += half
            continue
        count = half if step == 1 else deep
        span = pl.ds(firsts[at], count)
        forth = refs[2 * which[at]][span, :].astype(F32)
        back = refs[2 * which[at] + 1][span, :].astype(F32)
        if step == 1:
            forth_out[row : row + half] = (ahead[:half].astype(F32) + forth).astype(BF16)
            forth_out[row + half : row + deep] = ahead[half:]
            back_out[row : row + half] = behind[:half]
            back_out[row + half : row + deep] = (behind[half:].astype(F32) + back).astype(BF16)
        else:
            forth_out[row : row + deep] = (ahead.astype(F32) + forth).astype(BF16)
            back_out[row : row + deep] = (behind.astype(F32) + back).astype(BF16)
        row += deep


def ring_final(firsts, which, t_ref, *refs):
    del t_ref
    count = len(firsts)
    terms, outs = refs[:count], refs[-count:]
    arrived = refs[count:-count]
    for at in range(count):
        deep = outs[at].shape[0]
        span = pl.ds(firsts[at], deep)
        outs[at][...] = (
            terms[at][0].astype(F32)
            + arrived[2 * which[at]][span, :].astype(F32)
            + arrived[2 * which[at] + 1][span, :].astype(F32)
        )


def term_spec(terms, slot):
    return pl.BlockSpec((1,) + terms.shape[1:], lambda at, t: (t[1 + slot], 0, 0))


def arrivals(rings):
    pairs, which = [], []
    for ring in rings:
        if not ring.sent:
            which.append(0)
            continue
        known = [at for at, pair in enumerate(pairs) if pair[0] is ring.sent[0]]
        which.append(known[0] if known else len(pairs))
        if not known:
            pairs.append(ring.sent)
    return [item for pair in pairs for item in pair], tuple(which)


def ring_step(rings, *earlier):
    if not is_walk():
        return ()
    arrived, which = arrivals(rings)
    if earlier and arrived:
        arrived = list(lax.optimization_barrier(tuple(arrived) + tuple(earlier))[: len(arrived)])
    table = rings[0].table
    if earlier and not arrived:
        table = after(table, *earlier)
    ins, in_specs, rows = [], [], 0
    firsts = []
    deep, width = rings[0].terms.shape[1:]
    for ring in rings:
        slots = ((4, 4), (3, 5), (2, 6), (1, 7))[ring.at]
        ins += [ring.terms, ring.terms]
        in_specs += [term_spec(ring.terms, slots[0]), term_spec(ring.terms, slots[1])]
        firsts.append(ring.first)
        ring.first = rows
        rows += deep if ring.at else deep // 2
    ins += arrived
    in_specs += [whole_spec(item.shape) for item in arrived]
    out = jax.ShapeDtypeStruct((rows, width), BF16)
    steps = tuple(ring.at for ring in rings)
    body = partial(ring_payload, steps, tuple(firsts), which)
    forth, back = call(
        body, table, 1, ins, in_specs, [out, out], [whole_spec(out.shape)] * 2, [], 10**6, "ring_payload"
    )
    sent = ring_pair(forth, back)
    for ring in rings:
        ring.sent = sent
        ring.at += 1
    return forth, back


def ring_pin(rings, *values):
    arrived, _ = arrivals(rings)
    if not arrived:
        return values
    olds = {id(item): at for at, item in enumerate(arrived)}
    done = lax.optimization_barrier(tuple(arrived) + tuple(values))
    for ring in rings:
        if ring.sent:
            ring.sent = tuple(done[olds[id(item)]] for item in ring.sent)
    return done[len(arrived) :]


def ring_results(rings):
    if not is_walk():
        return [
            lax.psum_scatter(ring.terms, "fsdp", scatter_dimension=0, tiled=False).astype(F32)
            for ring in rings
        ]
    arrived, which = arrivals(rings)
    ins = [ring.terms for ring in rings] + arrived
    in_specs = [term_spec(ring.terms, 0) for ring in rings]
    in_specs += [whole_spec(item.shape) for item in arrived]
    outs = [jax.ShapeDtypeStruct(ring.terms.shape[1:], F32) for ring in rings]
    out_specs = [whole_spec(item.shape) for item in outs]
    body = partial(ring_final, tuple(ring.first for ring in rings), which)
    return call(body, rings[0].table, 1, ins, in_specs, outs, out_specs, [], 10**6, "ring_final")


def dot(left, right):
    return jnp.dot(left, right, preferred_element_type=F32)


def dot_t(left, right):
    return lax.dot_general(left, right, (((1,), (1,)), ((), ())), preferred_element_type=F32)


def shifted_sum(value, sign):
    width = value.shape[1]
    lane = lax.broadcasted_iota(jnp.int32, value.shape, 1)
    by = 1
    while by < width:
        if sign > 0:
            value = value + jnp.where(lane >= by, pltpu.roll(value, by, 1), 0.0)
        else:
            value = value + jnp.where(lane < width - by, pltpu.roll(value, width - by, 1), 0.0)
        by *= 2
    return value


def conv_parts(cur, prev, weight, bias, marks):
    rows = cur.shape[0]
    ext = jnp.concatenate([prev, cur], 0)
    pre = bias + cur * weight[3:4]
    moved = []
    for back in (1, 2, 3):
        item = ext[8 - back : 8 - back + rows]
        moved.append(item)
        pre = pre + item * marks[back - 1] * weight[3 - back : 4 - back]
    return pre, moved


def rates(u, params, seg_rows):
    u = u + params[:, 0:1]
    rate = jnp.exp(params[:, 1:2])
    dt = jnp.maximum(u, 0.0) + jnp.log1p(jnp.exp(-jnp.abs(u)))
    log_dt = jnp.where(u < -15.0, u, jnp.log(dt))
    a = -dt * rate
    total = shifted_sum(a, 1)
    last = total[:, -1:]
    less = total - log_dt
    enter = jnp.exp(total) * seg_rows[1:2]
    tail = jnp.exp(last - less) * seg_rows[2:3]
    return u, dt, a, rate, total, less, enter, tail


def as_columns(first, enter, tail, lines):
    enter_hi = enter.astype(BF16).astype(F32)
    tail_hi = tail.astype(BF16).astype(F32)
    rest = jnp.zeros((128 - 5 * HEAD_ROWS - 8, enter.shape[1]), F32)
    stacked = jnp.concatenate(
        [first, enter_hi, tail_hi, enter - enter_hi, tail - tail_hi, lines, rest], 0
    )
    return stacked.T


SEG = 5 * HEAD_ROWS


def pair_masks(rows):
    lane = lax.broadcasted_iota(jnp.int32, (rows, 128), 1)
    return lane < 64, lane >= 64


def start_weight(arrays, meta, column, width, deep, table, goal, sems):
    copies = []
    for at, (array, source, rows, slot, first, by_walk) in enumerate(meta):
        row = slot * deep + first
        if by_walk:
            row = pl.multiple_of(table[1 + slot] * deep + first, 32)
        copy = pltpu.make_async_copy(
            arrays[array].at[pl.ds(source, rows), pl.ds(column * width, width)],
            goal.at[pl.ds(row, rows)],
            sems.at[at],
        )
        copy.start()
        copies.append(copy)
    return copies


def wait_all(copies):
    for copy in copies:
        copy.wait()


def scan_block(x, raw, raw_u, sr, cp, bp, hp, spread_ref, y_ref, state_ref, held, x_tail, bc_tail):
    rows = x.shape[0]
    pairs = x.shape[1] // 128
    _, _, _, _, total, less, enter, tail = rates(raw_u, hp, sr)
    cols = as_columns(total, enter, tail, sr)
    marks = [cols[:, SEG + at : SEG + at + 1] for at in (3, 4, 5)]
    pre, _ = conv_parts(x, x_tail[...], cp, cp[4:5], marks)
    xc = pre * jax.nn.sigmoid(pre)
    x_tail[...] = x[rows - 8 :]
    pre_bc, _ = conv_parts(raw, bc_tail[...], bp, bp[4:5], marks)
    bc = (pre_bc * jax.nn.sigmoid(pre_bc)).astype(BF16)
    bc_tail[...] = raw[rows - 8 :]
    states = bc.shape[1] // 2
    b_rows, c_rows = bc[:, :states], bc[:, states:]

    cols_low = cols.astype(BF16)
    enter_x = dot(cols_low, spread_ref[0])
    tail_x = dot(cols_low, spread_ref[1])

    at_t = lax.broadcasted_iota(jnp.int32, (rows, rows), 0)
    at_s = lax.broadcasted_iota(jnp.int32, (rows, rows), 1)
    bar = jnp.where((cols[:, SEG : SEG + 1] == sr[0:1]) & (at_t >= at_s), 0.0, NEG)
    scores = dot_t(c_rows, b_rows)
    state = held[...]
    state_ref[0] = state
    entering = dot(c_rows, state.astype(BF16)) * enter_x
    xl = xc.astype(BF16)
    low_mask, high_mask = pair_masks(rows)
    zero = jnp.zeros((rows, 128), BF16)
    for pair in range(pairs):
        span = slice(pair * 128, pair * 128 + 128)
        part = xl[:, span]
        acc = entering[:, span] + xc[:, span] * cp[5:6, span]
        for side, mask in ((0, low_mask), (1, high_mask)):
            head = 2 * pair + side
            weights = jnp.exp(cols[:, head : head + 1] - less[head : head + 1] + bar) * scores
            acc = acc + dot(weights.astype(BF16), jnp.where(mask, part, zero))
        y_ref[0, :, span] = acc
    keep = enter_x[rows - 1 : rows]
    held[...] = state * keep + dot(
        b_rows.astype(F32).T.astype(BF16), (xc * tail_x).astype(BF16)
    )


def mix_backward(is_first, t_ref, *refs):
    (
        x_ref, xp_ref, bc_ref, bcp_ref, u_ref, sr_ref, y_ref, dy_ref, state_ref,
        cp_ref, bp_ref, hp_ref, spread_ref, heads_ref,
    ) = refs[:14]
    dx_ref, dbc_ref, du_ref, *carried = refs[-9:]
    gx_ref, gbc_ref, gh_ref, held, x_next, bc_next = carried
    rows = x_ref.shape[1]
    width = x_ref.shape[2]
    pairs = width // 128

    @pl.when(pl.program_id(0) == 0)
    def _():
        for at, ref in enumerate(carried):
            if is_first:
                ref[...] = refs[14][...] if at == 0 else jnp.zeros_like(ref)
            else:
                ref[...] = refs[17 + at][...]

    sr = sr_ref[0]
    cp, bp = cp_ref[0], bp_ref[...]
    u, dt, a, rate, total, less, enter, tail = rates(u_ref[0], hp_ref[0], sr)
    cols = as_columns(less, enter, tail, sr)
    marks = [cols[:, SEG + at : SEG + at + 1] for at in (3, 4, 5)]
    x = x_ref[0].astype(F32)
    pre, x_moved = conv_parts(x, xp_ref[0][8:].astype(F32), cp, cp[4:5], marks)
    sig = jax.nn.sigmoid(pre)
    xc = pre * sig
    raw = bc_ref[0]
    pre_bc, bc_moved = conv_parts(raw, bcp_ref[0], bp, bp[4:5], marks)
    sig_bc = jax.nn.sigmoid(pre_bc)
    bc = (pre_bc * sig_bc).astype(BF16)
    states = bc.shape[1] // 2
    b_rows, c_rows = bc[:, :states], bc[:, states:]

    cols_low = cols.astype(BF16)
    enter_x = dot(cols_low, spread_ref[0])
    tail_x = dot(cols_low, spread_ref[1])
    keep = enter_x[rows - 1 : rows]

    at_s = lax.broadcasted_iota(jnp.int32, (rows, rows), 0)
    at_t = lax.broadcasted_iota(jnp.int32, (rows, rows), 1)
    bar = jnp.where((cols[:, SEG : SEG + 1] == sr[0:1]) & (at_t >= at_s), 0.0, NEG)
    scores = dot_t(b_rows, c_rows)

    dyl = dy_ref[0]
    dy = dyl.astype(F32)
    xl = xc.astype(BF16)
    state = state_ref[0]
    d_state = held[...]
    d_state_low = d_state.astype(BF16)
    entered = (dy * enter_x).astype(BF16)
    dc = dot_t(entered, state.astype(BF16))
    db = dot_t((xc * tail_x).astype(BF16), d_state_low)
    dx_tail = dot(b_rows, d_state_low) * tail_x
    x_round = xl.astype(F32)
    last_terms = jnp.sum(x_round * dx_tail, 0, keepdims=True) + keep * jnp.sum(
        state * d_state, 0, keepdims=True
    )
    held[...] = keep * d_state + dot(c_rows.astype(F32).T.astype(BF16), entered)

    low_mask, high_mask = pair_masks(rows)
    zero = jnp.zeros((rows, 128), BF16)
    d_scores = jnp.zeros((rows, rows), F32)
    d_scan = []
    for pair in range(pairs):
        span = slice(pair * 128, pair * 128 + 128)
        part, grad = xl[:, span], dyl[:, span]
        acc = dx_tail[:, span]
        for side, mask in ((0, low_mask), (1, high_mask)):
            head = 2 * pair + side
            decay = jnp.exp(total[head : head + 1] - cols[:, head : head + 1] + bar)
            weights = (decay * scores).astype(BF16)
            d_scores = d_scores + decay * dot_t(jnp.where(mask, part, zero), grad)
            acc = acc + dot(weights, jnp.where(mask, grad, zero))
        d_scan.append(acc)
    d_scan = jnp.concatenate(d_scan, 1)
    db = db + dot(d_scores.astype(BF16), c_rows)
    dc = dc + dot(d_scores.T.astype(BF16), b_rows)

    skip = cp[5:6]
    from_x = x_round * d_scan
    from_t = dy * (y_ref[0] - skip * xc) - from_x
    row_at = lax.broadcasted_iota(jnp.int32, (rows, width), 0)
    from_t = from_t + jnp.where(row_at == rows - 1, last_terms, 0.0)

    def per_head(value):
        high = value.astype(BF16)
        return dot_t(heads_ref[...], high) + dot_t(
            heads_ref[...], (value - high.astype(F32)).astype(BF16)
        )

    q = per_head(from_x)
    da = shifted_sum(per_head(from_t), -1)
    slope = jax.nn.sigmoid(u)
    ratio = jnp.where(u < -15.0, 1.0, slope / dt)
    du = q * ratio - da * rate * slope
    du_ref[0] = du
    gh_ref[0] += jnp.sum(du, 1, keepdims=True)
    gh_ref[1] += jnp.sum(da * a, 1, keepdims=True)
    both = jnp.concatenate([gh_ref[0], gh_ref[1], jnp.zeros((128 - 2 * HEAD_ROWS, 128), F32)], 0)
    gx_ref[7:8, 0:128] = both.T[0:1]

    def conv_back(d_out, cur, moved, weight, carried, grads):
        grads[3:4] += jnp.sum(d_out * cur, 0, keepdims=True)
        grads[4:5] += jnp.sum(d_out, 0, keepdims=True)
        result = d_out * weight[3:4]
        for back in (1, 2, 3):
            kept = d_out * marks[back - 1]
            grads[3 - back : 4 - back] += jnp.sum(kept * moved[back - 1], 0, keepdims=True)
            ext = jnp.concatenate([kept, carried[back - 1]], 0)
            result = result + ext[back : back + rows] * weight[3 - back : 4 - back]
            carried[back - 1] = kept[:8]
        return result

    gx_ref[5:6] += jnp.sum(dy * xc, 0, keepdims=True)
    d_pre = (d_scan + skip * dy) * (sig * (1.0 + pre * (1.0 - sig)))
    dx_ref[0] = conv_back(d_pre, x, x_moved, cp, x_next, gx_ref).astype(BF16)
    d_bc = jnp.concatenate([db, dc], 1) * (sig_bc * (1.0 + pre_bc * (1.0 - sig_bc)))
    dbc_ref[0] = conv_back(d_bc, raw, bc_moved, bp, bc_next, gbc_ref).astype(BF16)


def input_backward(n_x, meta_x, n_z, meta_z, cols_xz, t_ref, *refs):
    dx_ref, dz_ref, dbc_ref, du_ref, rows_ref, wbc_ref, wdt_ref = refs[:7]
    x_parts, z_parts = refs[7 : 7 + n_x], refs[7 + n_x : 7 + n_x + n_z]
    send_ref, keep_ref, gdt_ref, gn_ref, wx, wz, sem_x, sem_z = refs[7 + n_x + n_z :]
    step = pl.program_id(0)
    width = wx.shape[1]
    deep = wx.shape[0] // (t_ref.shape[0] - 1)

    @pl.when(step == 0)
    def _():
        copies = start_weight(x_parts, meta_x, cols_xz[0], width, deep, t_ref, wx, sem_x)
        copies += start_weight(z_parts, meta_z, cols_xz[1], width, deep, t_ref, wz, sem_z)
        wait_all(copies)
        gdt_ref[...] = jnp.zeros_like(gdt_ref)
        gn_ref[...] = jnp.zeros_like(gn_ref)

    normed = rows_ref[0]
    du = du_ref[0]
    gdt_ref[...] += dot(du.astype(BF16), normed)
    total = dot_t(dz_ref[0], wz[...]) + dot_t(dx_ref[0], wx[...]) + dot_t(dbc_ref[0], wbc_ref[...])
    du_cols = jnp.concatenate([du, jnp.zeros((128 - du.shape[0], du.shape[1]), F32)], 0).T
    total = total + dot(du_cols.astype(BF16), wdt_ref[...])
    gn_ref[...] += jnp.sum(total * normed.astype(F32), 0, keepdims=True)
    out = total.astype(BF16)

    @pl.when(step < 2)
    def _():
        send_ref[0] = out

    @pl.when(step >= 2)
    def _():
        keep_ref[0] = out


def project_scan(n_x, meta_x, col_x, with_norm, t_ref, *refs):
    slots, refs = refs[:4], refs[4:]
    gain_ref, wbc_ref, wdt_ref, sr_ref, cp_ref, bp_ref, hp_ref, spread_ref = refs[:8]
    refs = refs[8:]
    x_parts, refs = refs[:n_x], refs[n_x:]
    rows_ref, x_ref, bc_ref, u_ref, y_ref, state_ref = refs[:6]
    held, x_tail, bc_tail, wx, r_s, x_s, bc_s, u_s, sem_x = refs[6:]
    step = pl.program_id(0)
    blocks = x_s.shape[0]
    deep = wx.shape[0] // (t_ref.shape[0] - 1)

    def weights():
        return start_weight(x_parts, meta_x, col_x, wx.shape[1], deep, t_ref, wx, sem_x)

    for at in range(4):

        @pl.when(step == at)
        def _():
            copies = weights() if at == 0 else []
            value = slots[at][...]
            if with_norm:
                value = value.astype(F32)
                scale = lax.rsqrt(jnp.mean(value * value, -1, keepdims=True) + EPS)
                value = (value * scale * gain_ref[...]).astype(BF16)
            r_s[...] = value
            wait_all(copies)

    @pl.when(step < blocks)
    def _():
        value = r_s[...]
        rows_ref[0] = value
        x = dot(value, wx[...])
        bc = dot(value, wbc_ref[...])
        u = dot_t(wdt_ref[...][:HEAD_ROWS], value)
        x = x.astype(BF16)
        x_ref[0], bc_ref[0], u_ref[0] = x, bc, u
        x_s[step], bc_s[step], u_s[step] = x.astype(F32), bc, u

    @pl.when(step == blocks)
    def _():
        held[...] = jnp.zeros_like(held)
        x_tail[...] = jnp.zeros_like(x_tail)
        bc_tail[...] = jnp.zeros_like(bc_tail)

    @pl.when(step >= blocks)
    def _():
        slot = (step - blocks) ^ t_ref[0]
        scan_block(
            x_s[slot], bc_s[slot], u_s[slot], sr_ref[0], cp_ref[0], bp_ref[...], hp_ref[0], spread_ref,
            y_ref, state_ref, held, x_tail, bc_tail,
        )


def lane_columns(columns, rows):
    lane = lax.broadcasted_iota(jnp.int32, (rows, 128), 1)
    result = jnp.zeros((rows, 128), F32)
    for at, column in enumerate(columns):
        result = jnp.where(lane == at, column, result)
    return result


def three_parts(value):
    high = value.astype(BF16).astype(F32)
    rest = value - high
    middle = rest.astype(BF16).astype(F32)
    return [high, middle, rest - middle]


def gate_forward(n_z, meta_z, n_o, meta_o, cols_zo, is_last, t_ref, *refs):
    rows_ref, y_ref, gain_ref = refs[:3]
    refs = refs[3:]
    cots = ()
    if is_last:
        cots, refs = refs[:4], refs[4:]
    z_parts, refs = refs[:n_z], refs[n_z:]
    o_parts, refs = refs[:n_o], refs[n_o:]
    z_ref, send_ref, keep_ref = refs[:3]
    refs = refs[3:]
    if is_last:
        cot_ref, dg_ref, sums_ref = refs[:3]
        refs = refs[3:]
    wz, wo, sem_z, sem_o = refs
    step = pl.program_id(0)
    width = wz.shape[1]
    deep = wz.shape[0] // (t_ref.shape[0] - 1)

    @pl.when(step == 0)
    def _():
        copies = start_weight(z_parts, meta_z, cols_zo[0], width, deep, t_ref, wz, sem_z)
        copies += start_weight(o_parts, meta_o, cols_zo[1], width, deep, t_ref, wo, sem_o)
        wait_all(copies)

    z = dot(rows_ref[0], wz[...]).astype(BF16)
    z_ref[0] = z
    z = z.astype(F32)
    v = y_ref[0] * (z * jax.nn.sigmoid(z))
    gain = gain_ref[0][6:7]
    squares = jnp.sum(v * v, -1, keepdims=True)
    scaled = v * gain
    part = dot_t(scaled.astype(BF16), wo[...]).astype(BF16)
    features = wz.shape[0]
    rows = z.shape[0]

    def put(ref):
        ref[0, :, :features] = part
        if not is_last:
            ref[0, :, features:] = lane_columns(three_parts(squares), rows).astype(BF16)

    @pl.when(step < 2)
    def _():
        put(send_ref)

    @pl.when(step >= 2)
    def _():
        put(keep_ref)

    if is_last:
        for at, slot in enumerate((1, 3, 0, 2)):

            @pl.when(step == at)
            def _():
                cot_ref[0] = cots[slot][...]

        d_gated = dot(cot_ref[0], wo[...])
        dg_ref[0] = d_gated.astype(BF16)
        cross = jnp.sum(d_gated * scaled, -1, keepdims=True)
        sums_ref[0] = lane_columns([squares, cross], rows).T[:8]


def gate_backward(n_o, meta_o, col_o, is_last, inner, t_ref, *refs):
    z_ref, y_ref, gain_ref = refs[:3]
    refs = refs[3:]
    if is_last:
        dg_ref, sums_ref = refs[:2]
        refs = refs[2:]
        dy_ref, dz_ref, gated_ref, gg_ref = refs
    else:
        cots, refs = refs[:4], refs[4:]
        o_parts, refs = refs[:n_o], refs[n_o:]
        dy_ref, dz_ref, gated_ref, gg_ref, cot_ref, wo, extra_s, sem_o = refs
    step = pl.program_id(0)

    @pl.when(step == 0)
    def _():
        gg_ref[...] = jnp.zeros_like(gg_ref)
        if not is_last:
            deep = wo.shape[0] // (t_ref.shape[0] - 1)
            wait_all(
                start_weight(o_parts, meta_o, col_o, wo.shape[1], deep, t_ref, wo, sem_o)
            )

    if is_last:
        d_gated = dg_ref[0].astype(F32)
        sums = sums_ref[0]
        cols = jnp.concatenate([sums, jnp.zeros((120, sums.shape[1]), F32)], 0).T
        scale = lax.rsqrt(cols[:, 0:1] / inner + EPS)
        cross = cols[:, 1:2]
    else:
        features = wo.shape[0]
        for at in range(4):

            @pl.when(step == at)
            def _():
                cot_ref[0] = cots[at][:, :features]
                extra_s[...] = cots[at][:, features:].astype(F32)

        d_gated = dot(cot_ref[0], wo[...])
        extra = extra_s[...]
        scale = extra[:, 0:1] + extra[:, 1:2] + extra[:, 2:3]
        cross = extra[:, 3:4] + extra[:, 4:5] + extra[:, 5:6]
    z, y, gain = z_ref[0].astype(F32), y_ref[0], gain_ref[0][6:7]
    sig = jax.nn.sigmoid(z)
    silu = z * sig
    v = y * silu
    normed = v * scale
    gated_ref[0] = (normed * gain).astype(BF16)
    gg_ref[6:7] += jnp.sum(d_gated * normed, 0, keepdims=True)
    dv = d_gated * gain * scale - v * (scale * scale * scale * cross / inner)
    dy_ref[0] = (dv * silu).astype(BF16)
    dz_ref[0] = (dv * y * (sig * (1.0 + z * (1.0 - sig)))).astype(BF16)


def layer_spec(array, k):
    return pl.BlockSpec((1,) + array.shape[1:], lambda at, t: (k,) + (0,) * (array.ndim - 1))


def whole_spec(shape):
    return pl.BlockSpec(shape, lambda at, t: (0,) * len(shape))


ANY = pl.BlockSpec(memory_space=pl.ANY)


def call(body, table, grid, ins, in_specs, outs, out_specs, scratch, flops, name, aliases=None):
    size = sum(item.size * item.dtype.itemsize for item in list(ins) + list(outs))
    return pl.pallas_call(
        body,
        grid_spec=pltpu.PrefetchScalarGridSpec(
            num_scalar_prefetch=1,
            grid=(grid,),
            in_specs=in_specs,
            out_specs=out_specs,
            scratch_shapes=scratch,
        ),
        out_shape=outs,
        compiler_params=pltpu.CompilerParams(
            dimension_semantics=("arbitrary",), vmem_limit_bytes=VMEM
        ),
        cost_estimate=pl.CostEstimate(flops=flops, bytes_accessed=size, transcendentals=0),
        name=name,
        input_output_aliases=aliases or {},
    )(table, *ins)


def run_project(k, table, slots, gain, w_bc, w_dt, lines, params, bc_params, spread, weight, col, norm):
    blocks = len(slots)
    rows, features = slots[0].shape
    wide = w_bc.shape[1]
    chan, head = params
    width = chan.shape[2]
    states = wide // 2
    last = blocks - 1

    def early(shape):
        return pl.BlockSpec((1,) + shape, lambda at, t: (jnp.minimum(at, last), 0, 0))

    def block(shape):
        return pl.BlockSpec((1,) + shape, lambda at, t: (jnp.maximum(at - blocks, 0), 0, 0))

    def slot(shape):
        return pl.BlockSpec((1,) + shape, lambda at, t: (jnp.maximum(at - blocks, 0) ^ t[0], 0, 0))

    ins = [*slots, gain, w_bc, w_dt, lines, chan, bc_params, head, spread, *weight[0]]
    in_specs = [whole_spec(item.shape) for item in slots]
    in_specs += [whole_spec(item.shape) for item in (gain, w_bc, w_dt)]
    in_specs += [block((8, rows)), layer_spec(chan, k), whole_spec(bc_params.shape)]
    in_specs += [layer_spec(head, k), whole_spec(spread.shape)] + [ANY] * len(weight[0])
    outs = [
        jax.ShapeDtypeStruct((blocks, rows, features), BF16),
        jax.ShapeDtypeStruct((blocks, rows, width), BF16),
        jax.ShapeDtypeStruct((blocks, rows, wide), F32),
        jax.ShapeDtypeStruct((blocks, HEAD_ROWS, rows), F32),
        jax.ShapeDtypeStruct((blocks, rows, width), F32),
        jax.ShapeDtypeStruct((blocks, states, width), F32),
    ]
    out_specs = [
        early((rows, features)), early((rows, width)), early((rows, wide)),
        early((HEAD_ROWS, rows)), slot((rows, width)), block((states, width)),
    ]
    scratch = [
        pltpu.VMEM((states, width), F32),
        pltpu.VMEM((8, width), F32),
        pltpu.VMEM((8, wide), F32),
        pltpu.VMEM((features, width), BF16),
        pltpu.VMEM((rows, features), BF16),
        pltpu.VMEM((blocks, rows, width), F32),
        pltpu.VMEM((blocks, rows, wide), F32),
        pltpu.VMEM((blocks, HEAD_ROWS, rows), F32),
        pltpu.SemaphoreType.DMA((len(weight[1]),)),
    ]
    body = partial(project_scan, len(weight[0]), weight[1], col, norm)
    return call(body, table, 2 * blocks, ins, in_specs, outs, out_specs, scratch, 10**10, "project_scan")


def run_gate_forward(k, table, rows, y, chan, cots, w_z, w_o, cols):
    blocks, count, features = rows.shape
    width = y.shape[2]
    is_last = cots is not None
    extra = 0 if is_last else 128

    def slot(shape):
        return pl.BlockSpec((1,) + shape, lambda at, t: (2 * at + 1 - 5 * (at // 2), 0, 0))

    cots = cots or []
    ins = [rows, y, chan, *cots, *w_z[0], *w_o[0]]
    in_specs = [slot((count, features)), slot((count, width)), layer_spec(chan, k)]
    in_specs += [whole_spec(item.shape) for item in cots] + [ANY] * (len(w_z[0]) + len(w_o[0]))
    half = jax.ShapeDtypeStruct((2, count, features + extra), BF16)
    outs = [jax.ShapeDtypeStruct((blocks, count, width), BF16), half, half]
    out_specs = [
        slot((count, width)),
        pl.BlockSpec((1, count, features + extra), lambda at, t: (jnp.minimum(at, 1), 0, 0)),
        pl.BlockSpec((1, count, features + extra), lambda at, t: (jnp.maximum(at - 2, 0), 0, 0)),
    ]
    if is_last:
        outs += [
            jax.ShapeDtypeStruct((blocks, count, features), BF16),
            jax.ShapeDtypeStruct((blocks, count, width), BF16),
            jax.ShapeDtypeStruct((blocks, 8, count), F32),
        ]
        out_specs += [slot((count, features)), slot((count, width)), slot((8, count))]
    scratch = [
        pltpu.VMEM((features, width), BF16),
        pltpu.VMEM((features, width), BF16),
        pltpu.SemaphoreType.DMA((len(w_z[1]),)),
        pltpu.SemaphoreType.DMA((len(w_o[1]),)),
    ]
    body = partial(gate_forward, len(w_z[0]), w_z[1], len(w_o[0]), w_o[1], cols, is_last)
    return call(body, table, blocks, ins, in_specs, outs, out_specs, scratch, 6 * 10**9, "gate_forward")


def run_gate_backward(k, table, z, y, chan, known, cots, w_o, col, inner):
    blocks, count, width = z.shape
    is_last = cots is None

    def slot(shape):
        return pl.BlockSpec((1,) + shape, lambda at, t: (at, 0, 0))

    ins = [z, y, chan]
    in_specs = [slot((count, width)), slot((count, width)), layer_spec(chan, k)]
    outs = [
        jax.ShapeDtypeStruct((blocks, count, width), BF16),
        jax.ShapeDtypeStruct((blocks, count, width), BF16),
        jax.ShapeDtypeStruct((blocks, count, width), BF16),
        jax.ShapeDtypeStruct((8, width), F32),
    ]
    out_specs = [slot((count, width))] * 3 + [whole_spec((8, width))]
    scratch = []
    if is_last:
        ins += list(known)
        in_specs += [slot((count, width)), slot((8, count))]
    else:
        features = cots[0].shape[1] - 128
        ins += [*cots, *w_o[0]]
        in_specs += [whole_spec(item.shape) for item in cots] + [ANY] * len(w_o[0])
        outs.append(jax.ShapeDtypeStruct((blocks, count, features), BF16))
        out_specs.append(slot((count, features)))
        scratch = [
            pltpu.VMEM((features, width), BF16),
            pltpu.VMEM((count, 128), F32),
            pltpu.SemaphoreType.DMA((len(w_o[1]),)),
        ]
    body = partial(gate_backward, len(w_o[0]), w_o[1], col, is_last, inner)
    return call(body, table, blocks, ins, in_specs, outs, out_specs, scratch, 3 * 10**9, "gate_backward")


def run_mix_backward(k, table, x, bc, u, lines, y, dy, state, params, bc_params, spread, heads_of, gg, top, steps, before):
    blocks, rows, width = x.shape
    wide = bc.shape[2]
    states = wide // 2
    chan, head = params

    def slot(shape):
        return pl.BlockSpec((1,) + shape, lambda at, t: ((top - at) ^ t[0], 0, 0))

    def earlier(shape):
        return pl.BlockSpec(
            (1,) + shape,
            lambda at, t: (jnp.maximum(top - at - 1, 0) ^ t[0], rows // shape[0] - 1, 0),
        )

    def straight(shape):
        return pl.BlockSpec((1,) + shape, lambda at, t: (top - at, 0, 0))

    ins = [x, x, bc, bc, u, lines, y, dy, state, chan, bc_params, head, spread, heads_of]
    in_specs = [
        slot((rows, width)), earlier((16, width)), slot((rows, wide)), earlier((8, wide)),
        slot((HEAD_ROWS, rows)), straight((8, rows)),
        slot((rows, width)), slot((rows, width)), straight((states, width)),
        layer_spec(chan, k), whole_spec(bc_params.shape), layer_spec(head, k),
        whole_spec(spread.shape), whole_spec(heads_of.shape),
    ]
    outs = [
        jax.ShapeDtypeStruct((blocks, rows, width), BF16),
        jax.ShapeDtypeStruct((blocks, rows, wide), BF16),
        jax.ShapeDtypeStruct((blocks, HEAD_ROWS, rows), F32),
        jax.ShapeDtypeStruct((8, width), F32),
        jax.ShapeDtypeStruct((8, wide), F32),
        jax.ShapeDtypeStruct((2, HEAD_ROWS, 128), F32),
        jax.ShapeDtypeStruct((states, width), F32),
        jax.ShapeDtypeStruct((3, 8, width), F32),
        jax.ShapeDtypeStruct((3, 8, wide), F32),
    ]
    out_specs = [slot((rows, width)), slot((rows, wide)), slot((HEAD_ROWS, rows))]
    out_specs += [whole_spec(item.shape) for item in outs[3:]]
    aliases = {}
    if before:
        aliases = {1 + len(ins) + at: at for at in range(3)}
        ins += list(before)
        in_specs += [ANY] * 3 + [whole_spec(item.shape) for item in outs[3:]]
    else:
        ins.append(gg)
        in_specs.append(whole_spec(gg.shape))
    body = partial(mix_backward, not before)
    return call(body, table, steps, ins, in_specs, outs, out_specs, [], 2 * 10**9 * steps, "mix_backward", aliases)


def run_input_backward(table, dx, dz, dbc, du, normed, w_bc, w_dt, w_x, w_z, cols):
    blocks, rows, width = dx.shape
    features = normed.shape[2]
    wide = dbc.shape[2]

    def slot(shape):
        return pl.BlockSpec((1,) + shape, lambda at, t: (2 * at + 1 - 5 * (at // 2), 0, 0))

    ins = [dx, dz, dbc, du, normed, w_bc, w_dt, *w_x[0], *w_z[0]]
    in_specs = [slot((rows, width)), slot((rows, width)), slot((rows, wide)), slot((HEAD_ROWS, rows))]
    in_specs += [slot((rows, features)), whole_spec(w_bc.shape), whole_spec(w_dt.shape)]
    in_specs += [ANY] * (len(w_x[0]) + len(w_z[0]))
    half = jax.ShapeDtypeStruct((2, rows, features), BF16)
    outs = [
        half, half,
        jax.ShapeDtypeStruct((HEAD_ROWS, features), F32),
        jax.ShapeDtypeStruct((1, features), F32),
    ]
    out_specs = [
        pl.BlockSpec((1, rows, features), lambda at, t: (jnp.minimum(at, 1), 0, 0)),
        pl.BlockSpec((1, rows, features), lambda at, t: (jnp.maximum(at - 2, 0), 0, 0)),
        whole_spec((HEAD_ROWS, features)), whole_spec((1, features)),
    ]
    scratch = [
        pltpu.VMEM((features, width), BF16),
        pltpu.VMEM((features, width), BF16),
        pltpu.SemaphoreType.DMA((len(w_x[1]),)),
        pltpu.SemaphoreType.DMA((len(w_z[1]),)),
    ]
    body = partial(input_backward, len(w_x[0]), w_x[1], len(w_z[0]), w_z[1], cols)
    return call(body, table, blocks, ins, in_specs, outs, out_specs, scratch, 7 * 10**9, "input_backward")


def segment_lines(segment, blocks):
    rows = segment.shape[0] // blocks
    cut = segment.reshape(blocks, rows)
    ends = cut[:, -1:]
    before = jnp.concatenate([cut[:1, :1], ends[:-1]], 0)
    kinds = [cut.astype(F32), (cut == before).astype(F32), (cut == ends).astype(F32)]
    for back in (1, 2, 3):
        earlier = jnp.pad(segment, (back, 0), constant_values=-1)[: segment.shape[0]]
        kinds.append((segment == earlier).astype(F32).reshape(blocks, rows))
    at = jnp.arange(8)[None, :, None]
    lines = jnp.zeros((blocks, 8, rows), F32)
    for index, kind in enumerate(kinds):
        lines = jnp.where(at == index, kind[:, None], lines)
    return lines


def head_tables(heads, width):
    owner = np.arange(width)[None, :] // (width // heads)
    at = np.arange(128)[:, None]
    spread_enter = (at == owner + HEAD_ROWS) | (at == owner + 3 * HEAD_ROWS)
    spread_tail = (at == owner + 2 * HEAD_ROWS) | (at == owner + 4 * HEAD_ROWS)
    spread = np.stack([spread_enter, spread_tail]).astype(np.float32)
    owners = (at[:HEAD_ROWS] == owner).astype(np.float32)
    return jnp.asarray(spread, BF16), jnp.asarray(owners, BF16)


def norm_scale_of(values):
    return lax.rsqrt(jnp.mean(values * values, -1, keepdims=True) + EPS)


def shards(
    hidden, segment_ids, cotangent, norm_gain, in_zx, in_dt, in_bc, conv_x, conv_x_bias,
    conv_bc, conv_bc_bias, dt_bias, a_log, skip_d, gated_gain, out_wt,
):
    layers = in_zx.shape[0]
    count = lax.axis_size("fsdp")
    tp_count = lax.axis_size("tp")
    tp_at = lax.axis_index("tp").astype(jnp.int32)
    own, features = hidden.shape
    deep = in_zx.shape[1]
    width = in_zx.shape[3]
    heads = in_dt.shape[2]
    wide = in_bc.shape[2]
    bc_deep = in_bc.shape[1]
    shared = conv_bc.shape[1]
    taps = conv_bc.shape[2]
    inner = width * tp_count
    dt_lines = -(-deep * heads // wide)
    dt_rest = dt_lines * wide - deep * heads
    lines = -(-(bc_deep + dt_lines + 1) // 16) * 16
    table = placement(tp_at)

    packs, weights, wholes = [], [], []
    for k in range(layers):
        tiny = [conv_bc[k].reshape(-1), conv_bc_bias[k]]
        tiny = jnp.concatenate(tiny + ([norm_gain.reshape(-1)] if k == 0 else []))
        tiny = jnp.pad(tiny, (0, wide - tiny.shape[0]))[None]
        dt = jnp.pad(in_dt[k].T.reshape(-1), (0, dt_rest)).reshape(dt_lines, wide)
        pack = jnp.concatenate([in_bc[k], dt, tiny], 0)
        packs.append(jnp.pad(pack, ((0, lines - pack.shape[0]), (0, 0))))

    ring_x = RingGather(in_zx[0, :, 1])
    over = permute(hidden, "tp", 2)
    beside = permute(hidden, "tp", 1)
    ring_x.step()
    walk = is_walk()
    pack = double(packs[0][None, None, None, None, None], "tp", 2, 3)
    for k in range(1, layers):
        whole = lax.all_gather(packs[k], ("fsdp", "tp"), axis=0, tiled=False)
        packs[k] = whole.reshape((count, tp_count) + packs[k].shape)

    def whole_of(k, source, out):
        return jnp.concatenate([source[k, :, 1], source[k, :, 0], out[k]], 1)

    if walk:
        steps = ring_x.steps
        in_zx_late, out_wt_late, *steps[0] = lax.optimization_barrier((in_zx, out_wt) + tuple(steps[0]))
        ring_zo = RingGather(jnp.concatenate([in_zx_late[0, :, 0], out_wt_late[0]], 1))
        ring_x.step(pack)
        pack = double(after(pack, *steps[0]), "fsdp", 4, 0)
        ring_x.step(pack)
        ring_zo.step(*steps[1])
        pack = double(after(pack, *steps[1]), "fsdp", 2, 1)
        ring_x.step(pack)
        pack = double(after(pack, *steps[2]), "fsdp", 1, 2)
        ring_zo.step(pack, *steps[3])
        over = after(over, pack)
    else:
        in_zx_late, out_wt_late = in_zx, out_wt
        ring_zo = RingGather(jnp.concatenate([in_zx[0, :, 0], out_wt[0]], 1))
        pack = lax.all_gather(pack[0], "fsdp", axis=0, tiled=False)[:, None]
    packs[0] = pack = double(pack, "tp", 1, 4).reshape(count, tp_count, lines, wide)
    slots = [hidden, beside, over, permute(over, "tp", 1)]
    cot_over = permute(after(cotangent, pack), "tp", 2)
    cot_beside = permute(after(cotangent, pack), "tp", 1)
    table = after(table, pack, *ring_zo.last())
    ring_zo.step(table)

    lines_of = segment_lines(segment_ids[0], tp_count)
    spread, heads_of = head_tables(heads, width)
    w_bc, w_dt, gains, bc_params = [], [], [], []
    skips = jnp.repeat(skip_d, width // heads, axis=1)
    chan = jnp.stack([conv_x_bias, skips, gated_gain], 1)
    chan = jnp.concatenate([jnp.swapaxes(conv_x, 1, 2), chan], 1)
    chan = jnp.pad(chan, ((0, 0), (0, 1), (0, 0))).astype(F32)
    head = jnp.pad(jnp.stack([dt_bias, a_log], 2), ((0, 0), (0, HEAD_ROWS - heads), (0, 126)))
    params = (chan, head.astype(F32))

    def unpack(k):
        part = packs[k]
        w_bc.append(part[:, :, :bc_deep].reshape(features, wide))
        dt = pick(part[:, :, bc_deep : bc_deep + dt_lines], tp_at, 1)
        dt = dt.reshape(count, -1)[:, : heads * deep]
        dt = dt.reshape(count, heads, deep).swapaxes(0, 1).reshape(heads, features)
        w_dt.append(jnp.pad(dt, ((0, 128 - heads), (0, 0))))
        tiny = part[:, :, bc_deep + dt_lines]
        if k == 0:
            first = shared * (taps + 1)
            every = tiny[:, :, first : first + layers * bc_deep]
            every = every.reshape(features // bc_deep, layers, bc_deep).swapaxes(0, 1)
            gains.extend(every.reshape(layers, 1, features).astype(F32))
        taps_bc = tiny[:, :, : shared * taps].reshape(wide, taps).astype(F32)
        bias_bc = tiny[:, :, shared * taps : shared * (taps + 1)].reshape(1, wide).astype(F32)
        bc_params.append(jnp.pad(jnp.concatenate([taps_bc.T, bias_bc], 0), ((0, 3), (0, 0))))

    running = hidden.astype(F32)
    saved = []
    for k in range(layers):
        if k:
            normed = (running * norm_scale_of(running) * gains[k]).astype(BF16)
            over = permute(normed, "tp", 2)
            beside = permute(normed, "tp", 1)
            if walk:
                ring_all.step(normed)
                over, *ring_all.steps[2] = lax.optimization_barrier((over,) + tuple(ring_all.steps[2]))
                ring_all.step()
            slots = [normed, beside, over, permute(over, "tp", 1)]
        unpack(k)
        w_x = ring_x.weight() if k == 0 else ring_all.weight()
        rows, x, bc, u, y, state = run_project(
            k, table, slots, gains[k], w_bc[k], w_dt[k], lines_of, params, bc_params[k], spread, w_x, 0, k == 0
        )
        if k == 0:
            y, cot_over, *_ = lax.optimization_barrier((y, cot_over) + tuple(ring_zo.last()))
            ring_zo.step(y)
            cots_last = [cotangent, cot_beside, cot_over, permute(cot_over, "tp", 1)]
            w_zo, cols_zo = ring_zo.weight(), (0, 1)
        else:
            w_zo, cols_zo = w_x, (1, 2)
        weights.append((w_x, w_zo, cols_zo))
        entry = dict(rows=rows, x=x, bc=bc, u=u, y=y, state=state, h=running)
        is_last = k == layers - 1
        if not is_last:
            next_ring = RingGather(whole_of(k + 1, in_zx_late, out_wt_late))
            next_ring.step(*(ring_zo.last() if k == 0 else (y,)))
        z, send, keep, *more = run_gate_forward(
            k, table, rows, y, chan, cots_last if is_last else None, w_zo, w_zo, cols_zo
        )
        if not is_last and walk:
            send, z, *next_ring.steps[0] = lax.optimization_barrier((send, z) + tuple(next_ring.steps[0]))
        entry["z"] = z
        entry["near"] = near = permute(send, "tp", 1)
        if not is_last:
            ring_all = next_ring
            going = plus(keep[1], near[1])
            far = permute(going, "tp", 2)
            if walk:
                ring_all.step(going)
                far, *ring_all.steps[1] = lax.optimization_barrier((far,) + tuple(ring_all.steps[1]))
        else:
            cot, d_gated, sums = more
            sums = tp_sum_slots(sums)
            far = permute(plus(keep[1], near[1]), "tp", 2)
            entry.update(cot=cot, d_gated=d_gated, sums=sums, far=far, parts=keep[0].astype(F32) + near[0].astype(F32))
        if not is_last:
            branch = keep[0].astype(F32) + near[0].astype(F32) + far.astype(F32)
            squares = jnp.sum(branch[:, features:], -1, keepdims=True)
            branch = branch[:, :features]
            scale = lax.rsqrt(squares / inner + EPS)
            entry.update(branch=branch, scale=scale)
            running = running + branch * scale
        saved.append(entry)

    grad_run = cotangent.astype(F32)
    parts = [None] * layers

    def small_sum(parts):
        d_bc, g_norm, gbc, g_dt, gx = (jnp.stack(item) for item in zip(*parts))
        room = (layers, count, tp_count)
        d_norm = (g_norm / jnp.stack(gains)).reshape(room + (bc_deep,))
        d_conv = gbc[:, : taps + 1].reshape((layers, taps + 1) + room[1:] + (shared,))
        d_conv = d_conv.transpose(0, 2, 3, 1, 4).reshape(room + ((taps + 1) * shared,))
        d_tiny = jnp.concatenate([d_norm, d_conv], 3).astype(BF16)
        d_tiny = jnp.pad(d_tiny, ((0, 0), (0, 0), (0, 0), (0, wide - d_tiny.shape[3])))
        d_pack = jnp.concatenate([d_bc.reshape(room + (bc_deep, wide)), d_tiny[:, :, :, None]], 3)
        d_pack = d_pack.transpose(1, 2, 0, 3, 4).reshape(count, tp_count, -1, wide)
        d_dt = g_dt[:, :heads].reshape(layers, heads, count, deep).transpose(2, 0, 1, 3)
        d_dt = jnp.pad(d_dt.reshape(count, layers, -1), ((0, 0), (0, 0), (0, dt_rest))).astype(BF16)
        return SmallSum(d_pack, d_dt.reshape(count, -1, wide), gx.reshape(-1, wide))

    sums_of = [None] * layers
    for k in reversed(range(layers)):
        item = saved[k]
        rows, z, y = item["rows"], item["z"], item["y"]
        w_x, w_zo, cols_zo = weights[k]
        if k == layers - 1:
            cot = item["cot"]
            dy, dz, gated, g_gain = run_gate_backward(
                k, table, z, y, chan, (item["d_gated"], item["sums"]), None, w_zo, cols_zo[1], inner
            )
        else:
            low = grad_run.astype(BF16)
            cross = jnp.sum(low.astype(F32) * item["branch"], -1, keepdims=True)
            extra = three_parts(item["scale"]) + three_parts(cross)
            extra = jnp.concatenate(extra, 1).astype(BF16)
            low = jnp.concatenate([low, jnp.pad(extra, ((0, 0), (0, 128 - 6)))], 1)
            cots = tp_gather(low)
            if walk:
                later_rings = sums_of[k + 1]
                (low_now,) = ring_pin(later_rings, low)
                sums_of[k + 1] = later_rings[:2] + (ring_results(later_rings[:2]), later_rings[2])
                last_x = later_rings[2]
                ring_step([last_x], low_now)
                (cots[2],) = ring_pin([last_x], cots[2])
                ring_step([last_x])
            dy, dz, gated, g_gain, cot = run_gate_backward(
                k, table, z, y, chan, None, cots, w_zo, cols_zo[1], inner
            )
            if walk:
                (dy,) = ring_pin([last_x], dy)

        def weight_grad(left, right):
            result = lax.dot_general(
                left, right, (((0, 1), (0, 1)), ((), ())), preferred_element_type=F32
            )
            return result.astype(BF16)

        ring_o = RingSum(weight_grad(cot, gated).reshape(count, deep, width), table)
        ring_z = RingSum(weight_grad(rows, dz).reshape(count, deep, width), table)
        early = [ring_o, ring_z]
        dy = after(dy, *ring_step(early, dy), ring_o.terms, ring_z.terms)
        if k == layers - 1:
            dy = after(dy, saved[k]["near"])
        splits = (tp_count // 2, tp_count - tp_count // 2)
        done, top = None, tp_count - 1
        for steps in splits:
            done = run_mix_backward(
                k, table, item["x"], item["bc"], item["u"], lines_of, y, dy, item["state"], params,
                bc_params[k], spread, heads_of, g_gain, top, steps, done,
            )
            top -= steps
            if top >= 0:
                done = list(done)
                (done[6],) = ring_pin(early, done[6])
                done[6] = after(done[6], *ring_step(early))
        dx, dbc, du, gx, gbc, gh = done[:6]
        (dx,) = ring_pin(early, dx)
        if k == layers - 1:
            dx, far = lax.optimization_barrier((dx, item["far"]))
            scale = lax.rsqrt(item["sums"][0, 0] / inner + EPS)[:, None]
            running = running + (item["parts"] + far.astype(F32)) * scale
        every = [ring_o, ring_z]
        if k == 0:
            ring_x = RingSum(weight_grad(rows, dx).reshape(count, deep, width), table)
            every.append(ring_x)
            sent = ring_step(every)
            dx_now = after(dx, *sent) if walk else dx
        else:
            dx_now = dx
        send, keep, g_dt, g_norm = run_input_backward(
            table, dx_now, dz, dbc, du, rows, w_bc[k], w_dt[k], w_x, w_zo, (0, cols_zo[0])
        )
        parts[k] = [weight_grad(rows, dbc), g_norm, gbc, g_dt, gx]
        if k == 0:
            (send,) = ring_pin(every, send)
            near = permute(send, "tp", 1)
            small = small_sum(parts)
            near, small.terms = lax.optimization_barrier((near, small.terms))
            going = plus(keep[1], near[1])
            far = permute(going, "tp", 2)
            ring_step(every, going)
            got = small.over_core()
            got, far = ring_pin(every, got, far)
            ring_step([ring_x], far)
            got = small.over_y(got)
            (got,) = ring_pin([ring_x], got)
            ring_step([ring_x])
            got = small.over_x(got)
            if walk:
                (got,) = ring_pin([ring_x], got)
            got = small.over_z(got)
        else:
            near = permute(send, "tp", 1)
            ring_x = RingSum(weight_grad(rows, dx).reshape(count, deep, width), table)
            every.append(ring_x)
            going, ring_x.terms = lax.optimization_barrier((plus(keep[1], near[1]), ring_x.terms))
            far = permute(going, "tp", 2)
            ring_step(every, going)
            (far,) = ring_pin(every, far)
            ring_step(every, far)
        sums_of[k] = (ring_o, ring_z, ring_x)
        if k == 0 or not walk:
            sums_of[k] = (ring_o, ring_z, ring_results([ring_o, ring_z]), ring_x)
        d_normed = keep[0].astype(F32) + near[0].astype(F32) + far.astype(F32)
        h = item["h"]
        inv = norm_scale_of(h)
        scaled = d_normed * gains[k]
        grad_run = (
            grad_run
            + inv * scaled
            - h * (inv**3 * (jnp.sum(scaled * h, -1, keepdims=True) / features))
        )

    d_pack, vector = small.result(got)
    d_dt = d_pack[layers * (bc_deep + 1) :].reshape(layers, -1)[:, : heads * deep]
    d_pack = d_pack[: layers * (bc_deep + 1)].reshape(layers, -1, wide)
    vector = vector.reshape(layers, 8, width)
    tiny = d_pack[:, bc_deep]
    conv = tiny[:, bc_deep : bc_deep + (taps + 1) * shared].reshape(layers, taps + 1, shared)
    zx, out = [], []
    for k in range(layers):
        _, _, (sum_o, sum_z), last_x = sums_of[k]
        zx.append(jnp.stack([sum_z, ring_results([last_x])[0]], 1))
        out.append(sum_o)
    return (
        running,
        grad_run,
        tiny[:, :bc_deep],
        jnp.stack(zx),
        d_dt.reshape(layers, heads, deep).swapaxes(1, 2),
        d_pack[:, :bc_deep],
        vector[:, :taps].swapaxes(1, 2),
        vector[:, taps],
        conv[:, :taps].swapaxes(1, 2),
        conv[:, taps],
        vector[:, 7, :heads],
        vector[:, 7, HEAD_ROWS : HEAD_ROWS + heads],
        jnp.sum(vector[:, 5].reshape(layers, heads, -1), 2),
        vector[:, 6],
        jnp.stack(out),
    )


def solution(mesh):
    tokens = P(("fsdp", "tp"), None)
    split = P(None, ("fsdp", "tp"))
    rows = P(None, ("fsdp", "tp"), None)
    weights = (
        split,
        P(None, "fsdp", None, "tp"),
        P(None, "fsdp", "tp"),
        rows,
        P(None, "tp", None),
        P(None, "tp"),
        rows,
        split,
        P(None, "tp"),
        P(None, "tp"),
        P(None, "tp"),
        P(None, "tp"),
        P(None, "fsdp", "tp"),
    )
    return jax.shard_map(
        shards,
        mesh=mesh,
        in_specs=(tokens, P("fsdp", None), tokens) + weights,
        out_specs=(tokens, tokens) + weights,
        check_vma=False,
    )
```

```python
from functools import partial

import jax
import jax.numpy as jnp
import numpy as np
from jax import lax
from jax.experimental import pallas as pl
from jax.experimental.pallas import tpu as pltpu
from jax.sharding import PartitionSpec as P

EPS = 1e-05
NEG = -1e30
F32 = jnp.float32
BF16 = jnp.bfloat16
WALK = (0, 2, 4, 6, 7, 5, 3, 1)
HEAD_ROWS = 16
VMEM = 56 * 1024 * 1024


def permute(value, axis, mask):
    size = lax.axis_size(axis)
    return lax.ppermute(value, axis, [(at, at ^ mask) for at in range(size)])


def tp_gather(value):
    across = permute(value, "tp", 2)
    core = permute(value, "tp", 1)
    return [value, core, across, permute(across, "tp", 1)]


def tp_reduce(send, keep):
    near = permute(send, "tp", 1)
    far = (keep[1].astype(F32) + near[1].astype(F32)).astype(keep.dtype)
    far = permute(far, "tp", 2)
    return keep[0].astype(F32) + near[0].astype(F32) + far.astype(F32)


def tp_sum_slots(value):
    near = permute(value, "tp", 1)
    value = value + jnp.stack([near[1], near[0], near[3], near[2]])
    far = permute(value, "tp", 2)
    return value + jnp.stack([far[2], far[3], far[0], far[1]])


def is_walk():
    return lax.axis_size("fsdp") == len(WALK)


def placement(tp_at):
    size = lax.axis_size("fsdp")
    if not is_walk():
        owners = jnp.arange(size, dtype=jnp.int32)
    else:
        all_owners = [[WALK[(WALK.index(f) + k) % size] for k in range(size)] for f in range(size)]
        owners = pick(jnp.array(all_owners, jnp.int32), lax.axis_index("fsdp"), 0)
    return jnp.concatenate([tp_at[None], owners])


def step_ring(value, by):
    size = len(WALK)
    return lax.ppermute(
        value, "fsdp", [(WALK[at], WALK[(at + by) % size]) for at in range(size)]
    )


def ring_pair(behind, ahead):
    return step_ring(behind, 1), step_ring(ahead, -1)


def ring_last(behind, ahead):
    half = behind.shape[0] // 2
    return step_ring(behind[:half], 1), step_ring(ahead[half:], -1)


def walk_weight(own, steps, lack=0):
    arrays = [own]
    rows = own.shape[0]
    meta = [(0, 0, rows, 0, 0, True, 0)]
    for at, (behind, ahead) in enumerate(steps):
        arrays += [behind, ahead]
        if at < 3:
            meta.append((len(arrays) - 2, 0, rows, 7 - at, 0, True, 0))
            meta.append((len(arrays) - 1, 0, rows, 1 + at, 0, True, 0))
        else:
            meta.append((len(arrays) - 2, 0, rows // 2, 4, 0, True, lack))
            meta.append((len(arrays) - 1, 0, rows // 2, 4, rows // 2, True, lack))
    return arrays, tuple(meta)


def natural_weight(array, count, deep, stride):
    return [array], tuple((0, at * stride, deep, at, 0, False, 0) for at in range(count))


def after(value, *earlier):
    return lax.optimization_barrier((value,) + earlier)[0]


class RingGather:
    def __init__(self, own):
        self.own = own
        self.steps = []

    def step(self, *earlier):
        if not is_walk():
            return
        behind, ahead = self.steps[-1] if self.steps else (self.own, self.own)
        if earlier:
            behind, ahead, *_ = lax.optimization_barrier((behind, ahead) + earlier)
        go = ring_last if len(self.steps) == 3 else ring_pair
        self.steps.append(go(behind, ahead))

    def last(self):
        return self.steps[-1] if self.steps else ()

    def weight(self):
        if is_walk():
            return walk_weight(self.own, self.steps)
        whole = lax.all_gather(self.own, "fsdp", axis=0, tiled=True)
        deep = self.own.shape[0]
        return natural_weight(whole, lax.axis_size("fsdp"), deep, deep)


def double(value, axis, mask, dim):
    other = permute(value, axis, mask)
    second = (lax.axis_index(axis) & mask) != 0
    low = jnp.where(second, other, value)
    high = jnp.where(second, value, other)
    return jnp.concatenate([low, high], dim)


def plus(left, right):
    return (left.astype(F32) + right.astype(F32)).astype(left.dtype)


def pick(value, at, axis):
    return lax.dynamic_index_in_dim(value, at, axis, keepdims=False, allow_negative_indices=False)


def two_parts(value):
    high = value.astype(BF16)
    return jnp.concatenate([high, (value - high.astype(F32)).astype(BF16)], 0)


def joined(parts):
    half = parts.shape[0] // 2
    return parts[:half].astype(F32) + parts[half:].astype(F32)


class SmallSum:
    def __init__(self, terms, own, vector):
        index = lax.axis_index("tp")
        self.core, self.y = index & 1, index >> 1
        self.terms = terms.reshape((terms.shape[0], 2, 2) + terms.shape[2:])
        self.own, self.vector = own, vector
        self.wide = vector.shape[1]

    def over_core(self):
        return permute(pick(self.terms, 1 - self.core, 2), "tp", 1)

    def over_y(self, got):
        self.terms = plus(pick(self.terms, self.core, 2), got)
        return permute(pick(self.terms, 1 - self.y, 1), "tp", 2)

    def over_x(self, got):
        terms = plus(pick(self.terms, self.y, 1), got)
        self.terms = terms = jnp.concatenate([terms, self.own], 1)
        self.rows = rows = terms.shape[1]
        if not is_walk():
            return ()
        index = lax.axis_index("fsdp")
        self.x, self.z = index & 1, index >> 1
        self.terms = terms = terms.reshape((4, 2) + terms.shape[1:])
        got = pick(terms, 1 - self.x, 1).reshape(4 * rows, self.wide)
        return permute(jnp.concatenate([got, two_parts(self.vector)], 0), "fsdp", 1)

    def over_z(self, got):
        if not is_walk():
            return ()
        rows, terms = self.rows, self.terms
        self.vector = self.vector + joined(got[4 * rows :])
        got = got[: 4 * rows].reshape(4, rows, self.wide)
        mine = pick(terms, self.x, 1)
        self.total = pick(mine, self.z, 0).astype(F32) + pick(got, self.z, 0).astype(F32)
        sent = two_parts(self.vector)
        parts = []
        for mask in (3, 2, 1):
            part = plus(pick(mine, self.z ^ mask, 0), pick(got, self.z ^ mask, 0))
            parts.append(permute(jnp.concatenate([part, sent], 0), "fsdp", 2 * mask))
        return tuple(parts)

    def result(self, parts):
        if not is_walk():
            own = lax.psum_scatter(self.terms, "fsdp", scatter_dimension=0, tiled=False)
            return own.astype(F32), lax.psum(self.vector, "fsdp")
        total, vector = self.total, self.vector
        for part in parts:
            total = total + part[: self.rows].astype(F32)
            vector = vector + joined(part[self.rows :])
        return total, vector


class RingSum:
    def __init__(self, terms, table):
        self.terms = terms
        self.table = table
        self.at = 0
        self.sent = ()
        self.first = 0


def ring_payload(steps, firsts, which, t_ref, *refs):
    del t_ref
    terms, refs = refs[: 2 * len(steps)], refs[2 * len(steps) :]
    forth_out, back_out = refs[-2:]
    row = 0
    for at, step in enumerate(steps):
        ahead, behind = terms[2 * at][0], terms[2 * at + 1][0]
        deep = ahead.shape[0]
        half = deep // 2
        if step == 0:
            forth_out[row : row + half] = ahead[:half]
            back_out[row : row + half] = behind[half:]
            row += half
            continue
        count = half if step == 1 else deep
        span = pl.ds(firsts[at], count)
        forth = refs[2 * which[at]][span, :].astype(F32)
        back = refs[2 * which[at] + 1][span, :].astype(F32)
        if step == 1:
            forth_out[row : row + half] = (ahead[:half].astype(F32) + forth).astype(BF16)
            forth_out[row + half : row + deep] = ahead[half:]
            back_out[row : row + half] = behind[:half]
            back_out[row + half : row + deep] = (behind[half:].astype(F32) + back).astype(BF16)
        else:
            forth_out[row : row + deep] = (ahead.astype(F32) + forth).astype(BF16)
            back_out[row : row + deep] = (behind.astype(F32) + back).astype(BF16)
        row += deep


def ring_final(firsts, which, t_ref, *refs):
    del t_ref
    count = len(firsts)
    terms, (zx_ref, out_ref) = refs[:count], refs[-2:]
    arrived = refs[count:-2]
    deep = out_ref.shape[1]
    for at in range(count):
        span = pl.ds(firsts[at], deep)
        total = (
            terms[at][0].astype(F32)
            + arrived[2 * which[at]][span, :].astype(F32)
            + arrived[2 * which[at] + 1][span, :].astype(F32)
        )
        if at % 3 == 0:
            out_ref[at // 3] = total
        else:
            zx_ref[at // 3, :, at % 3 - 1, :] = total


def term_spec(terms, slot):
    return pl.BlockSpec((1,) + terms.shape[1:], lambda at, t: (t[1 + slot], 0, 0))


def arrivals(rings):
    pairs, which = [], []
    for ring in rings:
        if not ring.sent:
            which.append(0)
            continue
        known = [at for at, pair in enumerate(pairs) if pair[0] is ring.sent[0]]
        which.append(known[0] if known else len(pairs))
        if not known:
            pairs.append(ring.sent)
    return [item for pair in pairs for item in pair], tuple(which)


def ring_step(rings, *earlier):
    if not is_walk():
        return ()
    arrived, which = arrivals(rings)
    if earlier and arrived:
        arrived = list(lax.optimization_barrier(tuple(arrived) + tuple(earlier))[: len(arrived)])
    table = rings[0].table
    if earlier and not arrived:
        table = after(table, *earlier)
    ins, in_specs, rows = [], [], 0
    firsts = []
    deep, width = rings[0].terms.shape[1:]
    for ring in rings:
        slots = ((4, 4), (3, 5), (2, 6), (1, 7))[ring.at]
        ins += [ring.terms, ring.terms]
        in_specs += [term_spec(ring.terms, slots[0]), term_spec(ring.terms, slots[1])]
        firsts.append(ring.first)
        ring.first = rows
        rows += deep if ring.at else deep // 2
    ins += arrived
    in_specs += [whole_spec(item.shape) for item in arrived]
    out = jax.ShapeDtypeStruct((rows, width), BF16)
    steps = tuple(ring.at for ring in rings)
    body = partial(ring_payload, steps, tuple(firsts), which)
    forth, back = call(
        body, table, 1, ins, in_specs, [out, out], [whole_spec(out.shape)] * 2, [], 10**6, "ring_payload"
    )
    sent = ring_pair(forth, back)
    for ring in rings:
        ring.sent = sent
        ring.at += 1
    return forth, back


def ring_pin(rings, *values):
    arrived, _ = arrivals(rings)
    if not arrived:
        return values
    olds = {id(item): at for at, item in enumerate(arrived)}
    done = lax.optimization_barrier(tuple(arrived) + tuple(values))
    for ring in rings:
        if ring.sent:
            ring.sent = tuple(done[olds[id(item)]] for item in ring.sent)
    return done[len(arrived) :]


def ring_results(rings):
    layers = len(rings) // 3
    deep, width = rings[0].terms.shape[1:]
    if not is_walk():
        sums = [
            lax.psum_scatter(ring.terms, "fsdp", scatter_dimension=0, tiled=False).astype(F32)
            for ring in rings
        ]
        zx = [jnp.stack(sums[3 * k + 1 : 3 * k + 3], 1) for k in range(layers)]
        return jnp.stack(zx), jnp.stack(sums[::3])
    arrived, which = arrivals(rings)
    ins = [ring.terms for ring in rings] + arrived
    in_specs = [term_spec(ring.terms, 0) for ring in rings]
    in_specs += [whole_spec(item.shape) for item in arrived]
    outs = [
        jax.ShapeDtypeStruct((layers, deep, 2, width), F32),
        jax.ShapeDtypeStruct((layers, deep, width), F32),
    ]
    out_specs = [whole_spec(item.shape) for item in outs]
    body = partial(ring_final, tuple(ring.first for ring in rings), which)
    return call(body, rings[0].table, 1, ins, in_specs, outs, out_specs, [], 10**6, "ring_final")


def dot(left, right):
    return jnp.dot(left, right, preferred_element_type=F32)


def dot_t(left, right):
    return lax.dot_general(left, right, (((1,), (1,)), ((), ())), preferred_element_type=F32)


def shifted_sum(value, sign):
    width = value.shape[1]
    lane = lax.broadcasted_iota(jnp.int32, value.shape, 1)
    by = 1
    while by < width:
        if sign > 0:
            value = value + jnp.where(lane >= by, pltpu.roll(value, by, 1), 0.0)
        else:
            value = value + jnp.where(lane < width - by, pltpu.roll(value, width - by, 1), 0.0)
        by *= 2
    return value


def conv_parts(cur, prev, weight, bias, marks):
    rows = cur.shape[0]
    ext = jnp.concatenate([prev, cur], 0)
    pre = bias + cur * weight[3:4]
    moved = []
    for back in (1, 2, 3):
        item = ext[8 - back : 8 - back + rows]
        moved.append(item)
        pre = pre + item * marks[back - 1] * weight[3 - back : 4 - back]
    return pre, moved


def rates(u, params, seg_rows):
    u = u + params[:, 0:1]
    rate = jnp.exp(params[:, 1:2])
    dt = jnp.maximum(u, 0.0) + jnp.log1p(jnp.exp(-jnp.abs(u)))
    log_dt = jnp.where(u < -15.0, u, jnp.log(dt))
    a = -dt * rate
    total = shifted_sum(a, 1)
    last = total[:, -1:]
    less = total - log_dt
    enter = jnp.exp(total) * seg_rows[1:2]
    tail = jnp.exp(last - less) * seg_rows[2:3]
    return u, dt, a, rate, total, less, enter, tail


def as_columns(first, enter, tail, lines):
    enter_hi = enter.astype(BF16).astype(F32)
    tail_hi = tail.astype(BF16).astype(F32)
    rest = jnp.zeros((128 - 5 * HEAD_ROWS - 8, enter.shape[1]), F32)
    stacked = jnp.concatenate(
        [first, enter_hi, tail_hi, enter - enter_hi, tail - tail_hi, lines, rest], 0
    )
    return stacked.T


SEG = 5 * HEAD_ROWS


def pair_masks(rows):
    lane = lax.broadcasted_iota(jnp.int32, (rows, 128), 1)
    return lane < 64, lane >= 64


def weight_copies(arrays, meta, column, width, deep, table, goal, sems):
    copies = []
    for at, (array, source, rows, slot, first, by_walk, lack) in enumerate(meta):
        row = slot * deep + first
        if by_walk:
            row = pl.multiple_of(table[1 + slot] * deep + first, 32)
        copy = pltpu.make_async_copy(
            arrays[array].at[pl.ds(source, rows), pl.ds(column * width - lack, width)],
            goal.at[pl.ds(row, rows)],
            sems.at[at],
        )
        copies.append(copy)
    return copies


def start_weight(*where):
    copies = weight_copies(*where)
    for copy in copies:
        copy.start()
    return copies


def wait_weight(*where):
    wait_all(weight_copies(*where))


def wait_all(copies):
    for copy in copies:
        copy.wait()


def scan_block(x, raw, raw_u, sr, cp, bp, hp, spread_ref, y_ref, state_ref, held, x_tail, bc_tail):
    rows = x.shape[0]
    pairs = x.shape[1] // 128
    _, _, _, _, total, less, enter, tail = rates(raw_u, hp, sr)
    cols = as_columns(total, enter, tail, sr)
    marks = [cols[:, SEG + at : SEG + at + 1] for at in (3, 4, 5)]
    pre, _ = conv_parts(x, x_tail[...], cp, cp[4:5], marks)
    xc = pre * jax.nn.sigmoid(pre)
    x_tail[...] = x[rows - 8 :]
    pre_bc, _ = conv_parts(raw, bc_tail[...], bp, bp[4:5], marks)
    bc = (pre_bc * jax.nn.sigmoid(pre_bc)).astype(BF16)
    bc_tail[...] = raw[rows - 8 :]
    states = bc.shape[1] // 2
    b_rows, c_rows = bc[:, :states], bc[:, states:]

    cols_low = cols.astype(BF16)
    enter_x = dot(cols_low, spread_ref[0])
    tail_x = dot(cols_low, spread_ref[1])

    at_t = lax.broadcasted_iota(jnp.int32, (rows, rows), 0)
    at_s = lax.broadcasted_iota(jnp.int32, (rows, rows), 1)
    bar = jnp.where((cols[:, SEG : SEG + 1] == sr[0:1]) & (at_t >= at_s), 0.0, NEG)
    scores = dot_t(c_rows, b_rows)
    state = held[...]
    state_ref[0] = state
    entering = dot(c_rows, state.astype(BF16)) * enter_x
    xl = xc.astype(BF16)
    low_mask, high_mask = pair_masks(rows)
    zero = jnp.zeros((rows, 128), BF16)
    for pair in range(pairs):
        span = slice(pair * 128, pair * 128 + 128)
        part = xl[:, span]
        acc = entering[:, span] + xc[:, span] * cp[5:6, span]
        for side, mask in ((0, low_mask), (1, high_mask)):
            head = 2 * pair + side
            weights = jnp.exp(cols[:, head : head + 1] - less[head : head + 1] + bar) * scores
            acc = acc + dot(weights.astype(BF16), jnp.where(mask, part, zero))
        y_ref[0, :, span] = acc
    keep = enter_x[rows - 1 : rows]
    held[...] = state * keep + dot(
        b_rows.astype(F32).T.astype(BF16), (xc * tail_x).astype(BF16)
    )


def mix_backward(is_first, t_ref, *refs):
    (
        x_ref, xp_ref, bc_ref, bcp_ref, u_ref, sr_ref, y_ref, dy_ref, state_ref,
        cp_ref, bp_ref, hp_ref, spread_ref, heads_ref,
    ) = refs[:14]
    dx_ref, dbc_ref, du_ref, *carried = refs[-9:]
    gx_ref, gbc_ref, gh_ref, held, x_next, bc_next = carried
    rows = x_ref.shape[1]
    width = x_ref.shape[2]
    pairs = width // 128

    @pl.when(pl.program_id(0) == 0)
    def _():
        for at, ref in enumerate(carried):
            if is_first:
                ref[...] = refs[14][...] if at == 0 else jnp.zeros_like(ref)
            else:
                ref[...] = refs[17 + at][...]

    sr = sr_ref[0]
    cp, bp = cp_ref[0], bp_ref[...]
    u, dt, a, rate, total, less, enter, tail = rates(u_ref[0], hp_ref[0], sr)
    cols = as_columns(less, enter, tail, sr)
    marks = [cols[:, SEG + at : SEG + at + 1] for at in (3, 4, 5)]
    x = x_ref[0].astype(F32)
    pre, x_moved = conv_parts(x, xp_ref[0][8:].astype(F32), cp, cp[4:5], marks)
    sig = jax.nn.sigmoid(pre)
    xc = pre * sig
    raw = bc_ref[0]
    pre_bc, bc_moved = conv_parts(raw, bcp_ref[0], bp, bp[4:5], marks)
    sig_bc = jax.nn.sigmoid(pre_bc)
    bc = (pre_bc * sig_bc).astype(BF16)
    states = bc.shape[1] // 2
    b_rows, c_rows = bc[:, :states], bc[:, states:]

    cols_low = cols.astype(BF16)
    enter_x = dot(cols_low, spread_ref[0])
    tail_x = dot(cols_low, spread_ref[1])
    keep = enter_x[rows - 1 : rows]

    at_s = lax.broadcasted_iota(jnp.int32, (rows, rows), 0)
    at_t = lax.broadcasted_iota(jnp.int32, (rows, rows), 1)
    bar = jnp.where((cols[:, SEG : SEG + 1] == sr[0:1]) & (at_t >= at_s), 0.0, NEG)
    scores = dot_t(b_rows, c_rows)

    dyl = dy_ref[0]
    dy = dyl.astype(F32)
    xl = xc.astype(BF16)
    state = state_ref[0]
    d_state = held[...]
    d_state_low = d_state.astype(BF16)
    entered = (dy * enter_x).astype(BF16)
    dc = dot_t(entered, state.astype(BF16))
    db = dot_t((xc * tail_x).astype(BF16), d_state_low)
    dx_tail = dot(b_rows, d_state_low) * tail_x
    x_round = xl.astype(F32)
    last_terms = jnp.sum(x_round * dx_tail, 0, keepdims=True) + keep * jnp.sum(
        state * d_state, 0, keepdims=True
    )
    held[...] = keep * d_state + dot(c_rows.astype(F32).T.astype(BF16), entered)

    low_mask, high_mask = pair_masks(rows)
    zero = jnp.zeros((rows, 128), BF16)
    d_scores = jnp.zeros((rows, rows), F32)
    d_scan = []
    for pair in range(pairs):
        span = slice(pair * 128, pair * 128 + 128)
        part, grad = xl[:, span], dyl[:, span]
        acc = dx_tail[:, span]
        for side, mask in ((0, low_mask), (1, high_mask)):
            head = 2 * pair + side
            decay = jnp.exp(total[head : head + 1] - cols[:, head : head + 1] + bar)
            weights = (decay * scores).astype(BF16)
            d_scores = d_scores + decay * dot_t(jnp.where(mask, part, zero), grad)
            acc = acc + dot(weights, jnp.where(mask, grad, zero))
        d_scan.append(acc)
    d_scan = jnp.concatenate(d_scan, 1)
    db = db + dot(d_scores.astype(BF16), c_rows)
    dc = dc + dot(d_scores.T.astype(BF16), b_rows)

    skip = cp[5:6]
    from_x = x_round * d_scan
    from_t = dy * (y_ref[0] - skip * xc) - from_x
    row_at = lax.broadcasted_iota(jnp.int32, (rows, width), 0)
    from_t = from_t + jnp.where(row_at == rows - 1, last_terms, 0.0)

    def per_head(value):
        high = value.astype(BF16)
        return dot_t(heads_ref[...], high) + dot_t(
            heads_ref[...], (value - high.astype(F32)).astype(BF16)
        )

    q = per_head(from_x)
    da = shifted_sum(per_head(from_t), -1)
    slope = jax.nn.sigmoid(u)
    ratio = jnp.where(u < -15.0, 1.0, slope / dt)
    du = q * ratio - da * rate * slope
    du_ref[0] = du
    gh_ref[0] += jnp.sum(du, 1, keepdims=True)
    gh_ref[1] += jnp.sum(da * a, 1, keepdims=True)
    both = jnp.concatenate([gh_ref[0], gh_ref[1], jnp.zeros((128 - 2 * HEAD_ROWS, 128), F32)], 0)
    gx_ref[7:8, 0:128] = both.T[0:1]

    def conv_back(d_out, cur, moved, weight, carried, grads):
        grads[3:4] += jnp.sum(d_out * cur, 0, keepdims=True)
        grads[4:5] += jnp.sum(d_out, 0, keepdims=True)
        result = d_out * weight[3:4]
        for back in (1, 2, 3):
            kept = d_out * marks[back - 1]
            grads[3 - back : 4 - back] += jnp.sum(kept * moved[back - 1], 0, keepdims=True)
            ext = jnp.concatenate([kept, carried[back - 1]], 0)
            result = result + ext[back : back + rows] * weight[3 - back : 4 - back]
            carried[back - 1] = kept[:8]
        return result

    gx_ref[5:6] += jnp.sum(dy * xc, 0, keepdims=True)
    d_pre = (d_scan + skip * dy) * (sig * (1.0 + pre * (1.0 - sig)))
    dx_ref[0] = conv_back(d_pre, x, x_moved, cp, x_next, gx_ref).astype(BF16)
    d_bc = jnp.concatenate([db, dc], 1) * (sig_bc * (1.0 + pre_bc * (1.0 - sig_bc)))
    dbc_ref[0] = conv_back(d_bc, raw, bc_moved, bp, bc_next, gbc_ref).astype(BF16)


def input_backward(n_x, meta_x, n_z, meta_z, cols_xz, t_ref, *refs):
    dx_ref, dz_ref, dbc_ref, du_ref, rows_ref, wbc_ref, wdt_ref = refs[:7]
    x_parts, z_parts = refs[7 : 7 + n_x], refs[7 + n_x : 7 + n_x + n_z]
    send_ref, keep_ref, gdt_ref, gn_ref, wx, wz, sem_x, sem_z = refs[7 + n_x + n_z :]
    step = pl.program_id(0)
    width = wx.shape[1]
    deep = wx.shape[0] // (t_ref.shape[0] - 1)

    @pl.when(step == 0)
    def _():
        copies = start_weight(z_parts, meta_z, cols_xz[1], width, deep, t_ref, wz, sem_z)
        start_weight(x_parts, meta_x, cols_xz[0], width, deep, t_ref, wx, sem_x)
        wait_all(copies)
        gdt_ref[...] = jnp.zeros_like(gdt_ref)
        gn_ref[...] = jnp.zeros_like(gn_ref)

    normed = rows_ref[0]
    du = du_ref[0]
    gdt_ref[...] += dot(du.astype(BF16), normed)
    total = dot_t(dz_ref[0], wz[...]) + dot_t(dbc_ref[0], wbc_ref[...])

    @pl.when(step == 0)
    def _():
        wait_weight(x_parts, meta_x, cols_xz[0], width, deep, t_ref, wx, sem_x)

    total = total + dot_t(dx_ref[0], wx[...])
    du_cols = jnp.concatenate([du, jnp.zeros((128 - du.shape[0], du.shape[1]), F32)], 0).T
    total = total + dot(du_cols.astype(BF16), wdt_ref[...])
    gn_ref[...] += jnp.sum(total * normed.astype(F32), 0, keepdims=True)
    out = total.astype(BF16)

    @pl.when(step < 2)
    def _():
        send_ref[0] = out

    @pl.when(step >= 2)
    def _():
        keep_ref[0] = out


def project_scan(n_x, meta_x, col_x, with_norm, t_ref, *refs):
    slots, refs = refs[:4], refs[4:]
    gain_ref, wbc_ref, wdt_ref, sr_ref, cp_ref, bp_ref, hp_ref, spread_ref = refs[:8]
    refs = refs[8:]
    x_parts, refs = refs[:n_x], refs[n_x:]
    rows_ref, x_ref, bc_ref, u_ref, y_ref, state_ref = refs[:6]
    held, x_tail, bc_tail, wx, r_s, x_s, bc_s, u_s, sem_x = refs[6:]
    step = pl.program_id(0)
    blocks = x_s.shape[0]
    deep = wx.shape[0] // (t_ref.shape[0] - 1)

    def weights():
        return start_weight(x_parts, meta_x, col_x, wx.shape[1], deep, t_ref, wx, sem_x)

    for at in range(4):

        @pl.when(step == at)
        def _():
            copies = weights() if at == 0 else []
            value = slots[at][...]
            if with_norm:
                value = value.astype(F32)
                scale = lax.rsqrt(jnp.mean(value * value, -1, keepdims=True) + EPS)
                value = (value * scale * gain_ref[...]).astype(BF16)
            r_s[...] = value
            wait_all(copies)

    @pl.when(step < blocks)
    def _():
        value = r_s[...]
        rows_ref[0] = value
        x = dot(value, wx[...])
        bc = dot(value, wbc_ref[...])
        u = dot_t(wdt_ref[...][:HEAD_ROWS], value)
        x = x.astype(BF16)
        x_ref[0], bc_ref[0], u_ref[0] = x, bc, u
        x_s[step], bc_s[step], u_s[step] = x.astype(F32), bc, u

    @pl.when(step == blocks)
    def _():
        held[...] = jnp.zeros_like(held)
        x_tail[...] = jnp.zeros_like(x_tail)
        bc_tail[...] = jnp.zeros_like(bc_tail)

    @pl.when(step >= blocks)
    def _():
        slot = (step - blocks) ^ t_ref[0]
        scan_block(
            x_s[slot], bc_s[slot], u_s[slot], sr_ref[0], cp_ref[0], bp_ref[...], hp_ref[0], spread_ref,
            y_ref, state_ref, held, x_tail, bc_tail,
        )


def lane_columns(columns, rows):
    lane = lax.broadcasted_iota(jnp.int32, (rows, 128), 1)
    result = jnp.zeros((rows, 128), F32)
    for at, column in enumerate(columns):
        result = jnp.where(lane == at, column, result)
    return result


def three_parts(value):
    high = value.astype(BF16).astype(F32)
    rest = value - high
    middle = rest.astype(BF16).astype(F32)
    return [high, middle, rest - middle]


def gate_forward(n_z, meta_z, n_o, meta_o, cols_zo, is_last, t_ref, *refs):
    rows_ref, y_ref, gain_ref = refs[:3]
    refs = refs[3:]
    cots = ()
    if is_last:
        cots, refs = refs[:4], refs[4:]
    z_parts, refs = refs[:n_z], refs[n_z:]
    o_parts, refs = refs[:n_o], refs[n_o:]
    z_ref, send_ref, keep_ref = refs[:3]
    refs = refs[3:]
    if is_last:
        cot_ref, dg_ref, sums_ref = refs[:3]
        refs = refs[3:]
    wz, wo, sem_z, sem_o = refs
    step = pl.program_id(0)
    width = wz.shape[1]
    deep = wz.shape[0] // (t_ref.shape[0] - 1)

    @pl.when(step == 0)
    def _():
        copies = start_weight(z_parts, meta_z, cols_zo[0], width, deep, t_ref, wz, sem_z)
        start_weight(o_parts, meta_o, cols_zo[1], width, deep, t_ref, wo, sem_o)
        wait_all(copies)

    z = dot(rows_ref[0], wz[...]).astype(BF16)

    @pl.when(step == 0)
    def _():
        wait_weight(o_parts, meta_o, cols_zo[1], width, deep, t_ref, wo, sem_o)

    z_ref[0] = z
    z = z.astype(F32)
    v = y_ref[0] * (z * jax.nn.sigmoid(z))
    gain = gain_ref[0][6:7]
    squares = jnp.sum(v * v, -1, keepdims=True)
    scaled = v * gain
    part = dot_t(scaled.astype(BF16), wo[...]).astype(BF16)
    features = wz.shape[0]
    rows = z.shape[0]

    def put(ref):
        ref[0, :, :features] = part
        if not is_last:
            ref[0, :, features:] = lane_columns(three_parts(squares), rows).astype(BF16)

    @pl.when(step < 2)
    def _():
        put(send_ref)

    @pl.when(step >= 2)
    def _():
        put(keep_ref)

    if is_last:
        for at, slot in enumerate((1, 3, 0, 2)):

            @pl.when(step == at)
            def _():
                cot_ref[0] = cots[slot][...]

        d_gated = dot(cot_ref[0], wo[...])
        dg_ref[0] = d_gated.astype(BF16)
        cross = jnp.sum(d_gated * scaled, -1, keepdims=True)
        sums_ref[0] = lane_columns([squares, cross], rows).T[:8]


def gate_backward(n_o, meta_o, col_o, is_last, inner, t_ref, *refs):
    z_ref, y_ref, gain_ref = refs[:3]
    refs = refs[3:]
    if is_last:
        dg_ref, sums_ref = refs[:2]
        refs = refs[2:]
        dy_ref, dz_ref, gated_ref, gg_ref = refs
    else:
        cots, refs = refs[:4], refs[4:]
        o_parts, refs = refs[:n_o], refs[n_o:]
        dy_ref, dz_ref, gated_ref, gg_ref, cot_ref, wo, extra_s, sem_o = refs
    step = pl.program_id(0)

    @pl.when(step == 0)
    def _():
        gg_ref[...] = jnp.zeros_like(gg_ref)
        if not is_last:
            deep = wo.shape[0] // (t_ref.shape[0] - 1)
            wait_all(
                start_weight(o_parts, meta_o, col_o, wo.shape[1], deep, t_ref, wo, sem_o)
            )

    if is_last:
        d_gated = dg_ref[0].astype(F32)
        sums = sums_ref[0]
        cols = jnp.concatenate([sums, jnp.zeros((120, sums.shape[1]), F32)], 0).T
        scale = lax.rsqrt(cols[:, 0:1] / inner + EPS)
        cross = cols[:, 1:2]
    else:
        features = wo.shape[0]
        for at in range(4):

            @pl.when(step == at)
            def _():
                cot_ref[0] = cots[at][:, :features]
                extra_s[...] = cots[at][:, features:].astype(F32)

        d_gated = dot(cot_ref[0], wo[...])
        extra = extra_s[...]
        scale = extra[:, 0:1] + extra[:, 1:2] + extra[:, 2:3]
        cross = extra[:, 3:4] + extra[:, 4:5] + extra[:, 5:6]
    z, y, gain = z_ref[0].astype(F32), y_ref[0], gain_ref[0][6:7]
    sig = jax.nn.sigmoid(z)
    silu = z * sig
    v = y * silu
    normed = v * scale
    gated_ref[0] = (normed * gain).astype(BF16)
    gg_ref[6:7] += jnp.sum(d_gated * normed, 0, keepdims=True)
    dv = d_gated * gain * scale - v * (scale * scale * scale * cross / inner)
    dy_ref[0] = (dv * silu).astype(BF16)
    dz_ref[0] = (dv * y * (sig * (1.0 + z * (1.0 - sig)))).astype(BF16)


def layer_spec(array, k):
    return pl.BlockSpec((1,) + array.shape[1:], lambda at, t: (k,) + (0,) * (array.ndim - 1))


def whole_spec(shape):
    return pl.BlockSpec(shape, lambda at, t: (0,) * len(shape))


ANY = pl.BlockSpec(memory_space=pl.ANY)


def call(body, table, grid, ins, in_specs, outs, out_specs, scratch, flops, name, aliases=None):
    size = sum(item.size * item.dtype.itemsize for item in list(ins) + list(outs))
    return pl.pallas_call(
        body,
        grid_spec=pltpu.PrefetchScalarGridSpec(
            num_scalar_prefetch=1,
            grid=(grid,),
            in_specs=in_specs,
            out_specs=out_specs,
            scratch_shapes=scratch,
        ),
        out_shape=outs,
        compiler_params=pltpu.CompilerParams(
            dimension_semantics=("arbitrary",), vmem_limit_bytes=VMEM
        ),
        cost_estimate=pl.CostEstimate(flops=flops, bytes_accessed=size, transcendentals=0),
        name=name,
        input_output_aliases=aliases or {},
    )(table, *ins)


def run_project(k, table, slots, gain, w_bc, w_dt, lines, params, bc_params, spread, weight, col, norm):
    blocks = len(slots)
    rows, features = slots[0].shape
    wide = w_bc.shape[1]
    chan, head = params
    width = chan.shape[2]
    states = wide // 2
    last = blocks - 1

    def early(shape):
        return pl.BlockSpec((1,) + shape, lambda at, t: (jnp.minimum(at, last), 0, 0))

    def block(shape):
        return pl.BlockSpec((1,) + shape, lambda at, t: (jnp.maximum(at - blocks, 0), 0, 0))

    def slot(shape):
        return pl.BlockSpec((1,) + shape, lambda at, t: (jnp.maximum(at - blocks, 0) ^ t[0], 0, 0))

    ins = [*slots, gain, w_bc, w_dt, lines, chan, bc_params, head, spread, *weight[0]]
    in_specs = [whole_spec(item.shape) for item in slots]
    in_specs += [whole_spec(item.shape) for item in (gain, w_bc, w_dt)]
    in_specs += [block((8, rows)), layer_spec(chan, k), whole_spec(bc_params.shape)]
    in_specs += [layer_spec(head, k), whole_spec(spread.shape)] + [ANY] * len(weight[0])
    outs = [
        jax.ShapeDtypeStruct((blocks, rows, features), BF16),
        jax.ShapeDtypeStruct((blocks, rows, width), BF16),
        jax.ShapeDtypeStruct((blocks, rows, wide), F32),
        jax.ShapeDtypeStruct((blocks, HEAD_ROWS, rows), F32),
        jax.ShapeDtypeStruct((blocks, rows, width), F32),
        jax.ShapeDtypeStruct((blocks, states, width), F32),
    ]
    out_specs = [
        early((rows, features)), early((rows, width)), early((rows, wide)),
        early((HEAD_ROWS, rows)), slot((rows, width)), block((states, width)),
    ]
    scratch = [
        pltpu.VMEM((states, width), F32),
        pltpu.VMEM((8, width), F32),
        pltpu.VMEM((8, wide), F32),
        pltpu.VMEM((features, width), BF16),
        pltpu.VMEM((rows, features), BF16),
        pltpu.VMEM((blocks, rows, width), F32),
        pltpu.VMEM((blocks, rows, wide), F32),
        pltpu.VMEM((blocks, HEAD_ROWS, rows), F32),
        pltpu.SemaphoreType.DMA((len(weight[1]),)),
    ]
    body = partial(project_scan, len(weight[0]), weight[1], col, norm)
    return call(body, table, 2 * blocks, ins, in_specs, outs, out_specs, scratch, 10**10, "project_scan")


def run_gate_forward(k, table, rows, y, chan, cots, w_z, w_o, cols):
    blocks, count, features = rows.shape
    width = y.shape[2]
    is_last = cots is not None
    extra = 0 if is_last else 128

    def slot(shape):
        return pl.BlockSpec((1,) + shape, lambda at, t: (2 * at + 1 - 5 * (at // 2), 0, 0))

    cots = cots or []
    ins = [rows, y, chan, *cots, *w_z[0], *w_o[0]]
    in_specs = [slot((count, features)), slot((count, width)), layer_spec(chan, k)]
    in_specs += [whole_spec(item.shape) for item in cots] + [ANY] * (len(w_z[0]) + len(w_o[0]))
    half = jax.ShapeDtypeStruct((2, count, features + extra), BF16)
    outs = [jax.ShapeDtypeStruct((blocks, count, width), BF16), half, half]
    out_specs = [
        slot((count, width)),
        pl.BlockSpec((1, count, features + extra), lambda at, t: (jnp.minimum(at, 1), 0, 0)),
        pl.BlockSpec((1, count, features + extra), lambda at, t: (jnp.maximum(at - 2, 0), 0, 0)),
    ]
    if is_last:
        outs += [
            jax.ShapeDtypeStruct((blocks, count, features), BF16),
            jax.ShapeDtypeStruct((blocks, count, width), BF16),
            jax.ShapeDtypeStruct((blocks, 8, count), F32),
        ]
        out_specs += [slot((count, features)), slot((count, width)), slot((8, count))]
    scratch = [
        pltpu.VMEM((features, width), BF16),
        pltpu.VMEM((features, width), BF16),
        pltpu.SemaphoreType.DMA((len(w_z[1]),)),
        pltpu.SemaphoreType.DMA((len(w_o[1]),)),
    ]
    body = partial(gate_forward, len(w_z[0]), w_z[1], len(w_o[0]), w_o[1], cols, is_last)
    return call(body, table, blocks, ins, in_specs, outs, out_specs, scratch, 6 * 10**9, "gate_forward")


def run_gate_backward(k, table, z, y, chan, known, cots, w_o, col, inner):
    blocks, count, width = z.shape
    is_last = cots is None

    def slot(shape):
        return pl.BlockSpec((1,) + shape, lambda at, t: (at, 0, 0))

    ins = [z, y, chan]
    in_specs = [slot((count, width)), slot((count, width)), layer_spec(chan, k)]
    outs = [
        jax.ShapeDtypeStruct((blocks, count, width), BF16),
        jax.ShapeDtypeStruct((blocks, count, width), BF16),
        jax.ShapeDtypeStruct((blocks, count, width), BF16),
        jax.ShapeDtypeStruct((8, width), F32),
    ]
    out_specs = [slot((count, width))] * 3 + [whole_spec((8, width))]
    scratch = []
    if is_last:
        ins += list(known)
        in_specs += [slot((count, width)), slot((8, count))]
    else:
        features = cots[0].shape[1] - 128
        ins += [*cots, *w_o[0]]
        in_specs += [whole_spec(item.shape) for item in cots] + [ANY] * len(w_o[0])
        outs.append(jax.ShapeDtypeStruct((blocks, count, features), BF16))
        out_specs.append(slot((count, features)))
        scratch = [
            pltpu.VMEM((features, width), BF16),
            pltpu.VMEM((count, 128), F32),
            pltpu.SemaphoreType.DMA((len(w_o[1]),)),
        ]
    body = partial(gate_backward, len(w_o[0]), w_o[1], col, is_last, inner)
    return call(body, table, blocks, ins, in_specs, outs, out_specs, scratch, 3 * 10**9, "gate_backward")


def run_mix_backward(k, table, x, bc, u, lines, y, dy, state, params, bc_params, spread, heads_of, gg, top, steps, before):
    blocks, rows, width = x.shape
    wide = bc.shape[2]
    states = wide // 2
    chan, head = params

    def slot(shape):
        return pl.BlockSpec((1,) + shape, lambda at, t: ((top - at) ^ t[0], 0, 0))

    def earlier(shape):
        return pl.BlockSpec(
            (1,) + shape,
            lambda at, t: (jnp.maximum(top - at - 1, 0) ^ t[0], rows // shape[0] - 1, 0),
        )

    def straight(shape):
        return pl.BlockSpec((1,) + shape, lambda at, t: (top - at, 0, 0))

    ins = [x, x, bc, bc, u, lines, y, dy, state, chan, bc_params, head, spread, heads_of]
    in_specs = [
        slot((rows, width)), earlier((16, width)), slot((rows, wide)), earlier((8, wide)),
        slot((HEAD_ROWS, rows)), straight((8, rows)),
        slot((rows, width)), slot((rows, width)), straight((states, width)),
        layer_spec(chan, k), whole_spec(bc_params.shape), layer_spec(head, k),
        whole_spec(spread.shape), whole_spec(heads_of.shape),
    ]
    outs = [
        jax.ShapeDtypeStruct((blocks, rows, width), BF16),
        jax.ShapeDtypeStruct((blocks, rows, wide), BF16),
        jax.ShapeDtypeStruct((blocks, HEAD_ROWS, rows), F32),
        jax.ShapeDtypeStruct((8, width), F32),
        jax.ShapeDtypeStruct((8, wide), F32),
        jax.ShapeDtypeStruct((2, HEAD_ROWS, 128), F32),
        jax.ShapeDtypeStruct((states, width), F32),
        jax.ShapeDtypeStruct((3, 8, width), F32),
        jax.ShapeDtypeStruct((3, 8, wide), F32),
    ]
    out_specs = [slot((rows, width)), slot((rows, wide)), slot((HEAD_ROWS, rows))]
    out_specs += [whole_spec(item.shape) for item in outs[3:]]
    aliases = {}
    if before:
        aliases = {1 + len(ins) + at: at for at in range(3)}
        ins += list(before)
        in_specs += [ANY] * 3 + [whole_spec(item.shape) for item in outs[3:]]
    else:
        ins.append(gg)
        in_specs.append(whole_spec(gg.shape))
    body = partial(mix_backward, not before)
    return call(body, table, steps, ins, in_specs, outs, out_specs, [], 2 * 10**9 * steps, "mix_backward", aliases)


def run_input_backward(table, dx, dz, dbc, du, normed, w_bc, w_dt, w_x, w_z, cols):
    blocks, rows, width = dx.shape
    features = normed.shape[2]
    wide = dbc.shape[2]

    def slot(shape):
        return pl.BlockSpec((1,) + shape, lambda at, t: (2 * at + 1 - 5 * (at // 2), 0, 0))

    ins = [dx, dz, dbc, du, normed, w_bc, w_dt, *w_x[0], *w_z[0]]
    in_specs = [slot((rows, width)), slot((rows, width)), slot((rows, wide)), slot((HEAD_ROWS, rows))]
    in_specs += [slot((rows, features)), whole_spec(w_bc.shape), whole_spec(w_dt.shape)]
    in_specs += [ANY] * (len(w_x[0]) + len(w_z[0]))
    half = jax.ShapeDtypeStruct((2, rows, features), BF16)
    outs = [
        half, half,
        jax.ShapeDtypeStruct((HEAD_ROWS, features), F32),
        jax.ShapeDtypeStruct((1, features), F32),
    ]
    out_specs = [
        pl.BlockSpec((1, rows, features), lambda at, t: (jnp.minimum(at, 1), 0, 0)),
        pl.BlockSpec((1, rows, features), lambda at, t: (jnp.maximum(at - 2, 0), 0, 0)),
        whole_spec((HEAD_ROWS, features)), whole_spec((1, features)),
    ]
    scratch = [
        pltpu.VMEM((features, width), BF16),
        pltpu.VMEM((features, width), BF16),
        pltpu.SemaphoreType.DMA((len(w_x[1]),)),
        pltpu.SemaphoreType.DMA((len(w_z[1]),)),
    ]
    body = partial(input_backward, len(w_x[0]), w_x[1], len(w_z[0]), w_z[1], cols)
    return call(body, table, blocks, ins, in_specs, outs, out_specs, scratch, 7 * 10**9, "input_backward")


def segment_lines(segment, blocks):
    rows = segment.shape[0] // blocks
    cut = segment.reshape(blocks, rows)
    ends = cut[:, -1:]
    before = jnp.concatenate([cut[:1, :1], ends[:-1]], 0)
    kinds = [cut.astype(F32), (cut == before).astype(F32), (cut == ends).astype(F32)]
    for back in (1, 2, 3):
        earlier = jnp.pad(segment, (back, 0), constant_values=-1)[: segment.shape[0]]
        kinds.append((segment == earlier).astype(F32).reshape(blocks, rows))
    at = jnp.arange(8)[None, :, None]
    lines = jnp.zeros((blocks, 8, rows), F32)
    for index, kind in enumerate(kinds):
        lines = jnp.where(at == index, kind[:, None], lines)
    return lines


def head_tables(heads, width):
    owner = np.arange(width)[None, :] // (width // heads)
    at = np.arange(128)[:, None]
    spread_enter = (at == owner + HEAD_ROWS) | (at == owner + 3 * HEAD_ROWS)
    spread_tail = (at == owner + 2 * HEAD_ROWS) | (at == owner + 4 * HEAD_ROWS)
    spread = np.stack([spread_enter, spread_tail]).astype(np.float32)
    owners = (at[:HEAD_ROWS] == owner).astype(np.float32)
    return jnp.asarray(spread, BF16), jnp.asarray(owners, BF16)


def norm_scale_of(values):
    return lax.rsqrt(jnp.mean(values * values, -1, keepdims=True) + EPS)


def shards(
    hidden, segment_ids, cotangent, norm_gain, in_zx, in_dt, in_bc, conv_x, conv_x_bias,
    conv_bc, conv_bc_bias, dt_bias, a_log, skip_d, gated_gain, out_wt,
):
    layers = in_zx.shape[0]
    count = lax.axis_size("fsdp")
    tp_count = lax.axis_size("tp")
    tp_at = lax.axis_index("tp").astype(jnp.int32)
    own, features = hidden.shape
    deep = in_zx.shape[1]
    width = in_zx.shape[3]
    heads = in_dt.shape[2]
    wide = in_bc.shape[2]
    bc_deep = in_bc.shape[1]
    shared = conv_bc.shape[1]
    taps = conv_bc.shape[2]
    inner = width * tp_count
    dt_lines = -(-deep * heads // wide)
    dt_rest = dt_lines * wide - deep * heads
    lines = -(-(bc_deep + dt_lines + 1) // 16) * 16
    table = placement(tp_at)

    packs, weights, wholes = [], [], []
    for k in range(layers):
        tiny = [conv_bc[k].reshape(-1), conv_bc_bias[k]]
        tiny = jnp.concatenate(tiny + ([norm_gain.reshape(-1)] if k == 0 else []))
        tiny = jnp.pad(tiny, (0, wide - tiny.shape[0]))[None]
        dt = jnp.pad(in_dt[k].T.reshape(-1), (0, dt_rest)).reshape(dt_lines, wide)
        pack = jnp.concatenate([in_bc[k], dt, tiny], 0)
        packs.append(jnp.pad(pack, ((0, lines - pack.shape[0]), (0, 0))))

    ring_x = RingGather(in_zx[0, :, 1])
    over = permute(hidden, "tp", 2)
    beside = permute(hidden, "tp", 1)
    ring_x.step()
    walk = is_walk()
    pack = double(packs[0][None, None, None, None, None], "tp", 2, 3)
    for k in range(1, layers):
        whole = lax.all_gather(packs[k], ("fsdp", "tp"), axis=0, tiled=False)
        packs[k] = whole.reshape((count, tp_count) + packs[k].shape)

    def whole_of(k, source, out):
        return jnp.concatenate([source[k, :, 1], source[k, :, 0], out[k]], 1)

    if walk:
        steps = ring_x.steps
        in_zx_late, out_wt_late, *steps[0] = lax.optimization_barrier((in_zx, out_wt) + tuple(steps[0]))
        ring_zo = RingGather(jnp.concatenate([in_zx_late[0, :, 0], out_wt_late[0]], 1))
        ring_x.step(pack)
        pack = double(after(pack, *steps[0]), "fsdp", 4, 0)
        ring_x.step(pack)
        ring_zo.step(*steps[1])
        pack = double(after(pack, *steps[1]), "fsdp", 2, 1)
        ring_x.step(pack)
        pack = double(after(pack, *steps[2]), "fsdp", 1, 2)
        ring_zo.step(pack, *steps[3])
        over = after(over, pack)
    else:
        in_zx_late, out_wt_late = in_zx, out_wt
        ring_zo = RingGather(jnp.concatenate([in_zx[0, :, 0], out_wt[0]], 1))
        pack = lax.all_gather(pack[0], "fsdp", axis=0, tiled=False)[:, None]
    packs[0] = pack = double(pack, "tp", 1, 4).reshape(count, tp_count, lines, wide)
    slots = [hidden, beside, over, permute(over, "tp", 1)]
    cot_over = permute(after(cotangent, pack), "tp", 2)
    cot_beside = permute(after(cotangent, pack), "tp", 1)
    table = after(table, pack, *ring_zo.last())
    ring_zo.step(table)

    lines_of = segment_lines(segment_ids[0], tp_count)
    spread, heads_of = head_tables(heads, width)
    w_bc, w_dt, gains, bc_params = [], [], [], []
    skips = jnp.repeat(skip_d, width // heads, axis=1)
    chan = jnp.stack([conv_x_bias, skips, gated_gain], 1)
    chan = jnp.concatenate([jnp.swapaxes(conv_x, 1, 2), chan], 1)
    chan = jnp.pad(chan, ((0, 0), (0, 1), (0, 0))).astype(F32)
    head = jnp.pad(jnp.stack([dt_bias, a_log], 2), ((0, 0), (0, HEAD_ROWS - heads), (0, 126)))
    params = (chan, head.astype(F32))

    def unpack(k):
        part = packs[k]
        w_bc.append(part[:, :, :bc_deep].reshape(features, wide))
        dt = pick(part[:, :, bc_deep : bc_deep + dt_lines], tp_at, 1)
        dt = dt.reshape(count, -1)[:, : heads * deep]
        dt = dt.reshape(count, heads, deep).swapaxes(0, 1).reshape(heads, features)
        w_dt.append(jnp.pad(dt, ((0, 128 - heads), (0, 0))))
        tiny = part[:, :, bc_deep + dt_lines]
        if k == 0:
            first = shared * (taps + 1)
            every = tiny[:, :, first : first + layers * bc_deep]
            every = every.reshape(features // bc_deep, layers, bc_deep).swapaxes(0, 1)
            gains.extend(every.reshape(layers, 1, features).astype(F32))
        taps_bc = tiny[:, :, : shared * taps].reshape(wide, taps).astype(F32)
        bias_bc = tiny[:, :, shared * taps : shared * (taps + 1)].reshape(1, wide).astype(F32)
        bc_params.append(jnp.pad(jnp.concatenate([taps_bc.T, bias_bc], 0), ((0, 3), (0, 0))))

    unpack(0)
    running = hidden.astype(F32)
    saved = []
    for k in range(layers):
        if k:
            normed = (running * norm_scale_of(running) * gains[k]).astype(BF16)
            over = permute(normed, "tp", 2)
            beside = permute(normed, "tp", 1)
            if walk:
                ring_all.step(normed)
                over, *ring_all.steps[2] = lax.optimization_barrier((over,) + tuple(ring_all.steps[2]))
                behind, ahead = ring_all.steps[2]
                last_x = ring_last(behind[:, :width], ahead[:, :width])
                last_zo = ring_last(behind[:, width:], ahead[:, width:])
            slots = [normed, beside, over, permute(over, "tp", 1)]
        if k == 0:
            w_x = ring_x.weight()
        elif walk:
            w_x = walk_weight(ring_all.own, ring_all.steps[:3] + [last_x])
        else:
            w_x = ring_all.weight()
        rows, x, bc, u, y, state = run_project(
            k, table, slots, gains[k], w_bc[k], w_dt[k], lines_of, params, bc_params[k], spread, w_x, 0, k == 0
        )
        if k == 0:
            y, cot_over, *_ = lax.optimization_barrier((y, cot_over) + tuple(ring_zo.last()))
            ring_zo.step(y)
            cots_last = [cotangent, cot_beside, cot_over, permute(cot_over, "tp", 1)]
            w_zo, cols_zo = ring_zo.weight(), (0, 1)
        else:
            w_zo, cols_zo = w_x, (1, 2)
            if walk:
                y, *last_zo = lax.optimization_barrier((y,) + tuple(last_zo))
                w_zo = walk_weight(ring_all.own, ring_all.steps[:3] + [tuple(last_zo)], width)
        weights.append((w_x, w_zo, cols_zo))
        entry = dict(rows=rows, x=x, bc=bc, u=u, y=y, state=state, h=running)
        is_last = k == layers - 1
        if not is_last:
            next_ring = RingGather(whole_of(k + 1, in_zx_late, out_wt_late))
            next_ring.step(*(ring_zo.last() if k == 0 else (y,)))
        z, send, keep, *more = run_gate_forward(
            k, table, rows, y, chan, cots_last if is_last else None, w_zo, w_zo, cols_zo
        )
        if not is_last and walk:
            send, z, packs[k + 1], *next_ring.steps[0] = lax.optimization_barrier(
                (send, z, packs[k + 1]) + tuple(next_ring.steps[0])
            )
        entry["z"] = z
        entry["near"] = near = permute(send, "tp", 1)
        if not is_last:
            ring_all = next_ring
            going = plus(keep[1], near[1])
            far = permute(going, "tp", 2)
            unpack(k + 1)
            far = after(far, w_bc[k + 1], w_dt[k + 1], bc_params[k + 1])
            if walk:
                ring_all.step(going)
                far, *ring_all.steps[1] = lax.optimization_barrier((far,) + tuple(ring_all.steps[1]))
        else:
            cot, d_gated, sums = more
            sums = tp_sum_slots(sums)
            far = permute(plus(keep[1], near[1]), "tp", 2)
            entry.update(cot=cot, d_gated=d_gated, sums=sums, far=far, parts=keep[0].astype(F32) + near[0].astype(F32))
        if not is_last:
            branch = keep[0].astype(F32) + near[0].astype(F32) + far.astype(F32)
            squares = jnp.sum(branch[:, features:], -1, keepdims=True)
            branch = branch[:, :features]
            scale = lax.rsqrt(squares / inner + EPS)
            entry.update(branch=branch, scale=scale)
            running = running + branch * scale
        saved.append(entry)

    grad_run = cotangent.astype(F32)
    parts = [None] * layers

    def small_sum(parts):
        d_bc, g_norm, gbc, g_dt, gx = (jnp.stack(item) for item in zip(*parts))
        room = (layers, count, tp_count)
        d_norm = (g_norm / jnp.stack(gains)).reshape(room + (bc_deep,))
        d_conv = gbc[:, : taps + 1].reshape((layers, taps + 1) + room[1:] + (shared,))
        d_conv = d_conv.transpose(0, 2, 3, 1, 4).reshape(room + ((taps + 1) * shared,))
        d_tiny = jnp.concatenate([d_norm, d_conv], 3).astype(BF16)
        d_tiny = jnp.pad(d_tiny, ((0, 0), (0, 0), (0, 0), (0, wide - d_tiny.shape[3])))
        d_pack = jnp.concatenate([d_bc.reshape(room + (bc_deep, wide)), d_tiny[:, :, :, None]], 3)
        d_pack = d_pack.transpose(1, 2, 0, 3, 4).reshape(count, tp_count, -1, wide)
        d_dt = g_dt[:, :heads].reshape(layers, heads, count, deep).transpose(2, 0, 1, 3)
        d_dt = jnp.pad(d_dt.reshape(count, layers, -1), ((0, 0), (0, 0), (0, dt_rest))).astype(BF16)
        return SmallSum(d_pack, d_dt.reshape(count, -1, wide), gx.reshape(-1, wide))

    sums_of = [None] * layers
    for k in reversed(range(layers)):
        item = saved[k]
        rows, z, y = item["rows"], item["z"], item["y"]
        w_x, w_zo, cols_zo = weights[k]
        if k == layers - 1:
            cot = item["cot"]
            dy, dz, gated, g_gain = run_gate_backward(
                k, table, z, y, chan, (item["d_gated"], item["sums"]), None, w_zo, cols_zo[1], inner
            )
        else:
            low = grad_run.astype(BF16)
            cross = jnp.sum(low.astype(F32) * item["branch"], -1, keepdims=True)
            extra = three_parts(item["scale"]) + three_parts(cross)
            extra = jnp.concatenate(extra, 1).astype(BF16)
            low = jnp.concatenate([low, jnp.pad(extra, ((0, 0), (0, 128 - 6)))], 1)
            over, beside = permute(low, "tp", 2), permute(low, "tp", 1)
            if walk:
                last_x = sums_of[k + 1][2]
                over = after(over, *ring_step(sums_of[k + 1], low))
                (over,) = ring_pin(sums_of[k + 1], over)
                ring_step([last_x], over)
            cots = [low, beside, over, permute(over, "tp", 1)]
            dy, dz, gated, g_gain, cot = run_gate_backward(
                k, table, z, y, chan, None, cots, w_zo, cols_zo[1], inner
            )
            if walk:
                (dy,) = ring_pin([last_x], dy)

        def weight_grad(left, right):
            result = lax.dot_general(
                left, right, (((0, 1), (0, 1)), ((), ())), preferred_element_type=F32
            )
            return result.astype(BF16)

        ring_o = RingSum(weight_grad(cot, gated).reshape(count, deep, width), table)
        ring_z = RingSum(weight_grad(rows, dz).reshape(count, deep, width), table)
        early = [ring_o, ring_z]
        rounds = early + ([last_x] if k < layers - 1 and walk else [])
        dy = after(dy, *ring_step(rounds, dy), ring_o.terms, ring_z.terms)
        if k == layers - 1:
            dy = after(dy, saved[k]["near"])
        splits = (tp_count,) if k else (tp_count // 2, tp_count - tp_count // 2)
        done, top = None, tp_count - 1
        for steps in splits:
            done = run_mix_backward(
                k, table, item["x"], item["bc"], item["u"], lines_of, y, dy, item["state"], params,
                bc_params[k], spread, heads_of, g_gain, top, steps, done,
            )
            top -= steps
            if top >= 0:
                done = list(done)
                (done[6],) = ring_pin(rounds, done[6])
                done[6] = after(done[6], *ring_step(rounds))
        dx, dbc, du, gx, gbc, gh = done[:6]
        (dx,) = ring_pin(rounds, dx)
        if k == layers - 1:
            dx, far = lax.optimization_barrier((dx, item["far"]))
            scale = lax.rsqrt(item["sums"][0, 0] / inner + EPS)[:, None]
            running = running + (item["parts"] + far.astype(F32)) * scale
        every = [ring_o, ring_z]
        if k == 0:
            ring_x = RingSum(weight_grad(rows, dx).reshape(count, deep, width), table)
            every.append(ring_x)
            sent = ring_step(every)
            dx_now = after(dx, *sent) if walk else dx
        else:
            sent = ring_step(every)
            dx_now = after(dx, *sent) if walk else dx
        send, keep, g_dt, g_norm = run_input_backward(
            table, dx_now, dz, dbc, du, rows, w_bc[k], w_dt[k], w_x, w_zo, (0, cols_zo[0])
        )
        parts[k] = [weight_grad(rows, dbc) if k else None, g_norm, gbc, g_dt, gx]
        if k == 0:
            (send,) = ring_pin(every, send)
            near = permute(send, "tp", 1)
            going = plus(keep[1], near[1])
            far = permute(going, "tp", 2)
            ring_step(every, going)
            (far,) = ring_pin(every, far)
            ring_step([ring_x], far)
            parts[k][0] = weight_grad(rows, after(dbc, far))
            small = small_sum(parts)
            got = small.over_core()
            (got,) = ring_pin([ring_x], got)
            last_sent = ring_step([ring_x])
            if walk:
                got = after(got, *last_sent)
                far = after(far, *last_sent)
            got = small.over_z(small.over_x(small.over_y(got)))
        else:
            (send,) = ring_pin(every, send)
            near = permute(send, "tp", 1)
            going = plus(keep[1], near[1])
            far = permute(going, "tp", 2)
            ring_step(every, going)
            ring_x = RingSum(weight_grad(rows, after(dx, going)).reshape(count, deep, width), table)
            far, ring_x.terms, parts[k][0] = ring_pin(every, far, ring_x.terms, parts[k][0])
        sums_of[k] = (ring_o, ring_z, ring_x)
        d_normed = keep[0].astype(F32) + near[0].astype(F32) + far.astype(F32)
        h = item["h"]
        inv = norm_scale_of(h)
        scaled = d_normed * gains[k]
        grad_run = (
            grad_run
            + inv * scaled
            - h * (inv**3 * (jnp.sum(scaled * h, -1, keepdims=True) / features))
        )

    d_pack, vector = small.result(got)
    d_dt = d_pack[layers * (bc_deep + 1) :].reshape(layers, -1)[:, : heads * deep]
    d_pack = d_pack[: layers * (bc_deep + 1)].reshape(layers, -1, wide)
    vector = vector.reshape(layers, 8, width)
    tiny = d_pack[:, bc_deep]
    conv = tiny[:, bc_deep : bc_deep + (taps + 1) * shared].reshape(layers, taps + 1, shared)
    zx, out = ring_results([ring for rings in sums_of for ring in rings])
    return (
        running,
        grad_run,
        tiny[:, :bc_deep],
        zx,
        d_dt.reshape(layers, heads, deep).swapaxes(1, 2),
        d_pack[:, :bc_deep],
        vector[:, :taps].swapaxes(1, 2),
        vector[:, taps],
        conv[:, :taps].swapaxes(1, 2),
        conv[:, taps],
        vector[:, 7, :heads],
        vector[:, 7, HEAD_ROWS : HEAD_ROWS + heads],
        jnp.sum(vector[:, 5].reshape(layers, heads, -1), 2),
        vector[:, 6],
        out,
    )


def solution(mesh):
    tokens = P(("fsdp", "tp"), None)
    split = P(None, ("fsdp", "tp"))
    rows = P(None, ("fsdp", "tp"), None)
    weights = (
        split,
        P(None, "fsdp", None, "tp"),
        P(None, "fsdp", "tp"),
        rows,
        P(None, "tp", None),
        P(None, "tp"),
        rows,
        split,
        P(None, "tp"),
        P(None, "tp"),
        P(None, "tp"),
        P(None, "tp"),
        P(None, "fsdp", "tp"),
    )
    return jax.shard_map(
        shards,
        mesh=mesh,
        in_specs=(tokens, P("fsdp", None), tokens) + weights,
        out_specs=(tokens, tokens) + weights,
        check_vma=False,
    )
```

```python
from functools import partial

import jax
import jax.numpy as jnp
import numpy as np
from jax import lax
from jax.experimental import pallas as pl
from jax.experimental.pallas import tpu as pltpu
from jax.sharding import PartitionSpec as P

EPS = 1e-05
NEG = -1e30
F32 = jnp.float32
BF16 = jnp.bfloat16
WALK = (0, 2, 4, 6, 7, 5, 3, 1)
HEAD_ROWS = 16
VMEM = 48 * 1024 * 1024


def permute(value, axis, mask):
    size = lax.axis_size(axis)
    return lax.ppermute(value, axis, [(at, at ^ mask) for at in range(size)])


def tp_gather(value):
    across = permute(value, "tp", 2)
    core = permute(value, "tp", 1)
    return [value, core, across, permute(across, "tp", 1)]


def tp_reduce(send, keep):
    near = permute(send, "tp", 1)
    far = (keep[1].astype(F32) + near[1].astype(F32)).astype(keep.dtype)
    far = permute(far, "tp", 2)
    return keep[0].astype(F32) + near[0].astype(F32) + far.astype(F32)


def tp_sum_slots(value):
    near = permute(value, "tp", 1)
    value = value + jnp.stack([near[1], near[0], near[3], near[2]])
    far = permute(value, "tp", 2)
    return value + jnp.stack([far[2], far[3], far[0], far[1]])


def is_walk():
    return lax.axis_size("fsdp") == len(WALK)


def placement(tp_at):
    size = lax.axis_size("fsdp")
    if not is_walk():
        owners = jnp.arange(size, dtype=jnp.int32)
    else:
        all_owners = [[WALK[(WALK.index(f) + k) % size] for k in range(size)] for f in range(size)]
        owners = pick(jnp.array(all_owners, jnp.int32), lax.axis_index("fsdp"), 0)
    return jnp.concatenate([tp_at[None], owners])


def step_ring(value, by):
    size = len(WALK)
    return lax.ppermute(
        value, "fsdp", [(WALK[at], WALK[(at + by) % size]) for at in range(size)]
    )


def ring_pair(behind, ahead):
    return step_ring(behind, 1), step_ring(ahead, -1)


def ring_last(behind, ahead):
    half = behind.shape[0] // 2
    return step_ring(behind[:half], 1), step_ring(ahead[half:], -1)


def walk_weight(own, steps, lack=0):
    arrays = [own]
    rows = own.shape[0]
    meta = [(0, 0, rows, 0, 0, True, 0)]
    for at, (behind, ahead) in enumerate(steps):
        arrays += [behind, ahead]
        if at < 3:
            meta.append((len(arrays) - 2, 0, rows, 7 - at, 0, True, 0))
            meta.append((len(arrays) - 1, 0, rows, 1 + at, 0, True, 0))
        else:
            meta.append((len(arrays) - 2, 0, rows // 2, 4, 0, True, lack))
            meta.append((len(arrays) - 1, 0, rows // 2, 4, rows // 2, True, lack))
    return arrays, tuple(meta)


def natural_weight(array, count, deep, stride):
    return [array], tuple((0, at * stride, deep, at, 0, False, 0) for at in range(count))


def after(value, *earlier):
    return lax.optimization_barrier((value,) + earlier)[0]


class RingGather:
    def __init__(self, own):
        self.own = own
        self.steps = []

    def step(self, *earlier):
        if not is_walk():
            return
        behind, ahead = self.steps[-1] if self.steps else (self.own, self.own)
        if earlier:
            behind, ahead, *_ = lax.optimization_barrier((behind, ahead) + earlier)
        go = ring_last if len(self.steps) == 3 else ring_pair
        self.steps.append(go(behind, ahead))

    def last(self):
        return self.steps[-1] if self.steps else ()

    def weight(self):
        if is_walk():
            return walk_weight(self.own, self.steps)
        whole = lax.all_gather(self.own, "fsdp", axis=0, tiled=True)
        deep = self.own.shape[0]
        return natural_weight(whole, lax.axis_size("fsdp"), deep, deep)


def double(value, axis, mask, dim):
    other = permute(value, axis, mask)
    second = (lax.axis_index(axis) & mask) != 0
    low = jnp.where(second, other, value)
    high = jnp.where(second, value, other)
    return jnp.concatenate([low, high], dim)


def plus(left, right):
    return (left.astype(F32) + right.astype(F32)).astype(left.dtype)


def pick(value, at, axis):
    return lax.dynamic_index_in_dim(value, at, axis, keepdims=False, allow_negative_indices=False)


def two_parts(value):
    high = value.astype(BF16)
    return jnp.concatenate([high, (value - high.astype(F32)).astype(BF16)], 0)


def joined(parts):
    half = parts.shape[0] // 2
    return parts[:half].astype(F32) + parts[half:].astype(F32)


class SmallSum:
    def __init__(self, terms, own, vector):
        index = lax.axis_index("tp")
        self.core, self.y = index & 1, index >> 1
        self.terms = terms.reshape((terms.shape[0], 2, 2) + terms.shape[2:])
        self.own, self.vector = own, vector
        self.wide = vector.shape[1]

    def over_core(self):
        return permute(pick(self.terms, 1 - self.core, 2), "tp", 1)

    def over_y(self, got):
        self.terms = plus(pick(self.terms, self.core, 2), got)
        return permute(pick(self.terms, 1 - self.y, 1), "tp", 2)

    def over_x(self, got):
        terms = plus(pick(self.terms, self.y, 1), got)
        self.terms = terms = jnp.concatenate([terms, self.own], 1)
        self.rows = rows = terms.shape[1]
        if not is_walk():
            return ()
        index = lax.axis_index("fsdp")
        self.x, self.z = index & 1, index >> 1
        self.terms = terms = terms.reshape((4, 2) + terms.shape[1:])
        got = pick(terms, 1 - self.x, 1).reshape(4 * rows, self.wide)
        return permute(jnp.concatenate([got, two_parts(self.vector)], 0), "fsdp", 1)

    def over_z(self, got):
        if not is_walk():
            return ()
        rows, terms = self.rows, self.terms
        self.vector = self.vector + joined(got[4 * rows :])
        got = got[: 4 * rows].reshape(4, rows, self.wide)
        mine = pick(terms, self.x, 1)
        self.total = pick(mine, self.z, 0).astype(F32) + pick(got, self.z, 0).astype(F32)
        sent = two_parts(self.vector)
        parts = []
        for mask in (3, 2, 1):
            part = plus(pick(mine, self.z ^ mask, 0), pick(got, self.z ^ mask, 0))
            parts.append(permute(jnp.concatenate([part, sent], 0), "fsdp", 2 * mask))
        return tuple(parts)

    def result(self, parts):
        if not is_walk():
            own = lax.psum_scatter(self.terms, "fsdp", scatter_dimension=0, tiled=False)
            return own.astype(F32), lax.psum(self.vector, "fsdp")
        total, vector = self.total, self.vector
        for part in parts:
            total = total + part[: self.rows].astype(F32)
            vector = vector + joined(part[self.rows :])
        return total, vector


class RingSum:
    def __init__(self, terms, table):
        self.terms = terms
        self.table = table
        self.at = 0
        self.sent = ()
        self.first = 0


def ring_payload(steps, firsts, which, t_ref, *refs):
    del t_ref
    terms, refs = refs[: 2 * len(steps)], refs[2 * len(steps) :]
    forth_out, back_out = refs[-2:]
    row = 0
    for at, step in enumerate(steps):
        ahead, behind = terms[2 * at][0], terms[2 * at + 1][0]
        deep = ahead.shape[0]
        half = deep // 2
        if step == 0:
            forth_out[row : row + half] = ahead[:half]
            back_out[row : row + half] = behind[half:]
            row += half
            continue
        count = half if step == 1 else deep
        span = pl.ds(firsts[at], count)
        forth = refs[2 * which[at]][span, :].astype(F32)
        back = refs[2 * which[at] + 1][span, :].astype(F32)
        if step == 1:
            forth_out[row : row + half] = (ahead[:half].astype(F32) + forth).astype(BF16)
            forth_out[row + half : row + deep] = ahead[half:]
            back_out[row : row + half] = behind[:half]
            back_out[row + half : row + deep] = (behind[half:].astype(F32) + back).astype(BF16)
        else:
            forth_out[row : row + deep] = (ahead.astype(F32) + forth).astype(BF16)
            back_out[row : row + deep] = (behind.astype(F32) + back).astype(BF16)
        row += deep


def ring_final(firsts, which, t_ref, *refs):
    del t_ref
    count = len(firsts)
    terms, (zx_ref, out_ref) = refs[:count], refs[-2:]
    arrived = refs[count:-2]
    deep = out_ref.shape[1]
    for at in range(count):
        span = pl.ds(firsts[at], deep)
        total = (
            terms[at][0].astype(F32)
            + arrived[2 * which[at]][span, :].astype(F32)
            + arrived[2 * which[at] + 1][span, :].astype(F32)
        )
        if at % 3 == 0:
            out_ref[at // 3] = total
        else:
            zx_ref[at // 3, :, at % 3 - 1, :] = total


def term_spec(terms, slot):
    return pl.BlockSpec((1,) + terms.shape[1:], lambda at, t: (t[1 + slot], 0, 0))


def arrivals(rings):
    pairs, which = [], []
    for ring in rings:
        if not ring.sent:
            which.append(0)
            continue
        known = [at for at, pair in enumerate(pairs) if pair[0] is ring.sent[0]]
        which.append(known[0] if known else len(pairs))
        if not known:
            pairs.append(ring.sent)
    return [item for pair in pairs for item in pair], tuple(which)


def ring_step(rings, *earlier):
    if not is_walk():
        return ()
    arrived, which = arrivals(rings)
    if earlier and arrived:
        arrived = list(lax.optimization_barrier(tuple(arrived) + tuple(earlier))[: len(arrived)])
    table = rings[0].table
    if earlier and not arrived:
        table = after(table, *earlier)
    ins, in_specs, rows = [], [], 0
    firsts = []
    deep, width = rings[0].terms.shape[1:]
    for ring in rings:
        slots = ((4, 4), (3, 5), (2, 6), (1, 7))[ring.at]
        ins += [ring.terms, ring.terms]
        in_specs += [term_spec(ring.terms, slots[0]), term_spec(ring.terms, slots[1])]
        firsts.append(ring.first)
        ring.first = rows
        rows += deep if ring.at else deep // 2
    ins += arrived
    in_specs += [whole_spec(item.shape) for item in arrived]
    out = jax.ShapeDtypeStruct((rows, width), BF16)
    steps = tuple(ring.at for ring in rings)
    body = partial(ring_payload, steps, tuple(firsts), which)
    forth, back = call(
        body, table, 1, ins, in_specs, [out, out], [whole_spec(out.shape)] * 2, [], 10**6, "ring_payload"
    )
    sent = ring_pair(forth, back)
    for ring in rings:
        ring.sent = sent
        ring.at += 1
    return forth, back


def ring_pin(rings, *values):
    arrived, _ = arrivals(rings)
    if not arrived:
        return values
    olds = {id(item): at for at, item in enumerate(arrived)}
    done = lax.optimization_barrier(tuple(arrived) + tuple(values))
    for ring in rings:
        if ring.sent:
            ring.sent = tuple(done[olds[id(item)]] for item in ring.sent)
    return done[len(arrived) :]


def ring_results(rings):
    layers = len(rings) // 3
    deep, width = rings[0].terms.shape[1:]
    if not is_walk():
        sums = [
            lax.psum_scatter(ring.terms, "fsdp", scatter_dimension=0, tiled=False).astype(F32)
            for ring in rings
        ]
        zx = [jnp.stack(sums[3 * k + 1 : 3 * k + 3], 1) for k in range(layers)]
        return jnp.stack(zx), jnp.stack(sums[::3])
    arrived, which = arrivals(rings)
    ins = [ring.terms for ring in rings] + arrived
    in_specs = [term_spec(ring.terms, 0) for ring in rings]
    in_specs += [whole_spec(item.shape) for item in arrived]
    outs = [
        jax.ShapeDtypeStruct((layers, deep, 2, width), F32),
        jax.ShapeDtypeStruct((layers, deep, width), F32),
    ]
    out_specs = [whole_spec(item.shape) for item in outs]
    body = partial(ring_final, tuple(ring.first for ring in rings), which)
    return call(body, rings[0].table, 1, ins, in_specs, outs, out_specs, [], 10**6, "ring_final")


def dot(left, right):
    return jnp.dot(left, right, preferred_element_type=F32)


def dot_t(left, right):
    return lax.dot_general(left, right, (((1,), (1,)), ((), ())), preferred_element_type=F32)


def shifted_sum(value, sign):
    width = value.shape[1]
    lane = lax.broadcasted_iota(jnp.int32, value.shape, 1)
    by = 1
    while by < width:
        if sign > 0:
            value = value + jnp.where(lane >= by, pltpu.roll(value, by, 1), 0.0)
        else:
            value = value + jnp.where(lane < width - by, pltpu.roll(value, width - by, 1), 0.0)
        by *= 2
    return value


def conv_parts(cur, prev, weight, bias, marks):
    rows = cur.shape[0]
    ext = jnp.concatenate([prev, cur], 0)
    pre = bias + cur * weight[3:4]
    moved = []
    for back in (1, 2, 3):
        item = ext[8 - back : 8 - back + rows]
        moved.append(item)
        pre = pre + item * marks[back - 1] * weight[3 - back : 4 - back]
    return pre, moved


def rates(u, params, seg_rows):
    u = u + params[:, 0:1]
    rate = jnp.exp(params[:, 1:2])
    dt = jnp.maximum(u, 0.0) + jnp.log1p(jnp.exp(-jnp.abs(u)))
    log_dt = jnp.where(u < -15.0, u, jnp.log(dt))
    a = -dt * rate
    total = shifted_sum(a, 1)
    last = total[:, -1:]
    less = total - log_dt
    enter = jnp.exp(total) * seg_rows[1:2]
    tail = jnp.exp(last - less) * seg_rows[2:3]
    return u, dt, a, rate, total, less, enter, tail


def as_columns(first, enter, tail, lines):
    enter_hi = enter.astype(BF16).astype(F32)
    tail_hi = tail.astype(BF16).astype(F32)
    rest = jnp.zeros((128 - 5 * HEAD_ROWS - 8, enter.shape[1]), F32)
    stacked = jnp.concatenate(
        [first, enter_hi, tail_hi, enter - enter_hi, tail - tail_hi, lines, rest], 0
    )
    return stacked.T


SEG = 5 * HEAD_ROWS


def pair_masks(rows):
    lane = lax.broadcasted_iota(jnp.int32, (rows, 128), 1)
    return lane < 64, lane >= 64


def weight_copies(arrays, meta, column, width, deep, table, goal, sems):
    copies = []
    for at, (array, source, rows, slot, first, by_walk, lack) in enumerate(meta):
        row = slot * deep + first
        if by_walk:
            row = pl.multiple_of(table[1 + slot] * deep + first, 32)
        copy = pltpu.make_async_copy(
            arrays[array].at[pl.ds(source, rows), pl.ds(column * width - lack, width)],
            goal.at[pl.ds(row, rows)],
            sems.at[at],
        )
        copies.append(copy)
    return copies


def start_weight(*where):
    copies = weight_copies(*where)
    for copy in copies:
        copy.start()
    return copies


def wait_weight(*where):
    wait_all(weight_copies(*where))


def wait_all(copies):
    for copy in copies:
        copy.wait()


def scan_block(x, raw, raw_u, sr, cp, bp, hp, spread_ref, y_ref, state_ref, held, x_tail, bc_tail):
    rows = x.shape[0]
    pairs = x.shape[1] // 128
    _, _, _, _, total, less, enter, tail = rates(raw_u, hp, sr)
    cols = as_columns(total, enter, tail, sr)
    marks = [cols[:, SEG + at : SEG + at + 1] for at in (3, 4, 5)]
    pre, _ = conv_parts(x, x_tail[...], cp, cp[4:5], marks)
    xc = pre * jax.nn.sigmoid(pre)
    x_tail[...] = x[rows - 8 :]
    pre_bc, _ = conv_parts(raw, bc_tail[...], bp, bp[4:5], marks)
    bc = (pre_bc * jax.nn.sigmoid(pre_bc)).astype(BF16)
    bc_tail[...] = raw[rows - 8 :]
    states = bc.shape[1] // 2
    b_rows, c_rows = bc[:, :states], bc[:, states:]

    cols_low = cols.astype(BF16)
    enter_x = dot(cols_low, spread_ref[0])
    tail_x = dot(cols_low, spread_ref[1])

    at_t = lax.broadcasted_iota(jnp.int32, (rows, rows), 0)
    at_s = lax.broadcasted_iota(jnp.int32, (rows, rows), 1)
    bar = jnp.where((cols[:, SEG : SEG + 1] == sr[0:1]) & (at_t >= at_s), 0.0, NEG)
    scores = dot_t(c_rows, b_rows)
    state = held[...]
    state_ref[0] = state
    entering = dot(c_rows, state.astype(BF16)) * enter_x
    half = rows // 2
    xl = xc.astype(BF16)
    low_mask, high_mask = pair_masks(rows)
    zero = jnp.zeros((rows, 128), BF16)
    for pair in range(pairs):
        span = slice(pair * 128, pair * 128 + 128)
        part = xl[:, span]
        acc = entering[:, span] + xc[:, span] * cp[5:6, span]
        early, late = acc[:half], acc[half:]
        for side, mask in ((0, low_mask), (1, high_mask)):
            head = 2 * pair + side
            column, line = cols[:, head : head + 1], less[head : head + 1]
            own = jnp.where(mask, part, zero)
            first = jnp.exp(column[:half] - line[:, :half] + bar[:half, :half]) * scores[:half, :half]
            second = jnp.exp(column[half:] - line + bar[half:]) * scores[half:]
            early = early + dot(first.astype(BF16), own[:half])
            late = late + dot(second.astype(BF16), own)
        acc = jnp.concatenate([early, late], 0)
        y_ref[0, :, span] = acc
    keep = enter_x[rows - 1 : rows]
    held[...] = state * keep + dot(
        b_rows.astype(F32).T.astype(BF16), (xc * tail_x).astype(BF16)
    )


def mix_backward(is_first, t_ref, *refs):
    (
        x_ref, xp_ref, bc_ref, bcp_ref, u_ref, sr_ref, y_ref, dy_ref, state_ref,
        cp_ref, bp_ref, hp_ref, spread_ref, heads_ref,
    ) = refs[:14]
    dx_ref, dbc_ref, du_ref, *carried = refs[-9:]
    gx_ref, gbc_ref, gh_ref, held, x_next, bc_next = carried
    rows = x_ref.shape[1]
    width = x_ref.shape[2]
    pairs = width // 128

    @pl.when(pl.program_id(0) == 0)
    def _():
        for at, ref in enumerate(carried):
            if is_first:
                ref[...] = refs[14][...] if at == 0 else jnp.zeros_like(ref)
            else:
                ref[...] = refs[17 + at][...]

    sr = sr_ref[0]
    cp, bp = cp_ref[0], bp_ref[...]
    u, dt, a, rate, total, less, enter, tail = rates(u_ref[0], hp_ref[0], sr)
    cols = as_columns(less, enter, tail, sr)
    marks = [cols[:, SEG + at : SEG + at + 1] for at in (3, 4, 5)]
    x = x_ref[0].astype(F32)
    pre, x_moved = conv_parts(x, xp_ref[0][8:].astype(F32), cp, cp[4:5], marks)
    sig = jax.nn.sigmoid(pre)
    xc = pre * sig
    raw = bc_ref[0]
    pre_bc, bc_moved = conv_parts(raw, bcp_ref[0], bp, bp[4:5], marks)
    sig_bc = jax.nn.sigmoid(pre_bc)
    bc = (pre_bc * sig_bc).astype(BF16)
    states = bc.shape[1] // 2
    b_rows, c_rows = bc[:, :states], bc[:, states:]

    cols_low = cols.astype(BF16)
    enter_x = dot(cols_low, spread_ref[0])
    tail_x = dot(cols_low, spread_ref[1])
    keep = enter_x[rows - 1 : rows]

    at_s = lax.broadcasted_iota(jnp.int32, (rows, rows), 0)
    at_t = lax.broadcasted_iota(jnp.int32, (rows, rows), 1)
    bar = jnp.where((cols[:, SEG : SEG + 1] == sr[0:1]) & (at_t >= at_s), 0.0, NEG)
    scores = dot_t(b_rows, c_rows)

    dyl = dy_ref[0]
    dy = dyl.astype(F32)
    xl = xc.astype(BF16)
    state = state_ref[0]
    d_state = held[...]
    d_state_low = d_state.astype(BF16)
    entered = (dy * enter_x).astype(BF16)
    dc = dot_t(entered, state.astype(BF16))
    db = dot_t((xc * tail_x).astype(BF16), d_state_low)
    dx_tail = dot(b_rows, d_state_low) * tail_x
    x_round = xl.astype(F32)
    last_terms = jnp.sum(x_round * dx_tail, 0, keepdims=True) + keep * jnp.sum(
        state * d_state, 0, keepdims=True
    )
    held[...] = keep * d_state + dot(c_rows.astype(F32).T.astype(BF16), entered)

    low_mask, high_mask = pair_masks(rows)
    zero = jnp.zeros((rows, 128), BF16)
    half = rows // 2
    d_first = jnp.zeros((half, rows), F32)
    d_second = jnp.zeros((half, half), F32)
    d_scan = []
    for pair in range(pairs):
        span = slice(pair * 128, pair * 128 + 128)
        part, grad = xl[:, span], dyl[:, span]
        acc = dx_tail[:, span]
        early, late = acc[:half], acc[half:]
        for side, mask in ((0, low_mask), (1, high_mask)):
            head = 2 * pair + side
            column, line = cols[:, head : head + 1], total[head : head + 1]
            own, own_grad = jnp.where(mask, part, zero), jnp.where(mask, grad, zero)
            first = jnp.exp(line - column[:half] + bar[:half])
            second = jnp.exp(line[:, half:] - column[half:] + bar[half:, half:])
            d_first = d_first + first * dot_t(own[:half], grad)
            d_second = d_second + second * dot_t(own[half:], grad[half:])
            early = early + dot((first * scores[:half]).astype(BF16), own_grad)
            late = late + dot((second * scores[half:, half:]).astype(BF16), own_grad[half:])
        d_scan.append(jnp.concatenate([early, late], 0))
    d_scores = jnp.concatenate([jnp.zeros((half, half), F32), d_second], 1)
    d_scores = jnp.concatenate([d_first, d_scores], 0)
    d_scan = jnp.concatenate(d_scan, 1)
    db = db + dot(d_scores.astype(BF16), c_rows)
    dc = dc + dot(d_scores.T.astype(BF16), b_rows)

    skip = cp[5:6]
    from_x = x_round * d_scan
    from_t = dy * (y_ref[0] - skip * xc) - from_x
    row_at = lax.broadcasted_iota(jnp.int32, (rows, width), 0)
    from_t = from_t + jnp.where(row_at == rows - 1, last_terms, 0.0)

    def per_head(value):
        high = value.astype(BF16)
        return dot_t(heads_ref[...], high) + dot_t(
            heads_ref[...], (value - high.astype(F32)).astype(BF16)
        )

    q = per_head(from_x)
    da = shifted_sum(per_head(from_t), -1)
    slope = jax.nn.sigmoid(u)
    ratio = jnp.where(u < -15.0, 1.0, slope / dt)
    du = q * ratio - da * rate * slope
    du_ref[0] = du
    gh_ref[0] += jnp.sum(du, 1, keepdims=True)
    gh_ref[1] += jnp.sum(da * a, 1, keepdims=True)
    both = jnp.concatenate([gh_ref[0], gh_ref[1], jnp.zeros((128 - 2 * HEAD_ROWS, 128), F32)], 0)
    gx_ref[7:8, 0:128] = both.T[0:1]

    def conv_back(d_out, cur, moved, weight, carried, grads):
        grads[3:4] += jnp.sum(d_out * cur, 0, keepdims=True)
        grads[4:5] += jnp.sum(d_out, 0, keepdims=True)
        result = d_out * weight[3:4]
        for back in (1, 2, 3):
            kept = d_out * marks[back - 1]
            grads[3 - back : 4 - back] += jnp.sum(kept * moved[back - 1], 0, keepdims=True)
            ext = jnp.concatenate([kept, carried[back - 1]], 0)
            result = result + ext[back : back + rows] * weight[3 - back : 4 - back]
            carried[back - 1] = kept[:8]
        return result

    gx_ref[5:6] += jnp.sum(dy * xc, 0, keepdims=True)
    d_pre = (d_scan + skip * dy) * (sig * (1.0 + pre * (1.0 - sig)))
    dx_ref[0] = conv_back(d_pre, x, x_moved, cp, x_next, gx_ref).astype(BF16)
    d_bc = jnp.concatenate([db, dc], 1) * (sig_bc * (1.0 + pre_bc * (1.0 - sig_bc)))
    dbc_ref[0] = conv_back(d_bc, raw, bc_moved, bp, bc_next, gbc_ref).astype(BF16)


def input_backward(n_x, meta_x, n_z, meta_z, cols_xz, t_ref, *refs):
    dx_ref, dz_ref, dbc_ref, du_ref, rows_ref, wbc_ref, wdt_ref = refs[:7]
    x_parts, z_parts = refs[7 : 7 + n_x], refs[7 + n_x : 7 + n_x + n_z]
    send_ref, keep_ref, gdt_ref, gn_ref, wx, wz, sem_x, sem_z = refs[7 + n_x + n_z :]
    step = pl.program_id(0)
    width = wx.shape[1]
    deep = wx.shape[0] // (t_ref.shape[0] - 1)

    @pl.when(step == 0)
    def _():
        copies = start_weight(z_parts, meta_z, cols_xz[1], width, deep, t_ref, wz, sem_z)
        start_weight(x_parts, meta_x, cols_xz[0], width, deep, t_ref, wx, sem_x)
        wait_all(copies)
        gdt_ref[...] = jnp.zeros_like(gdt_ref)
        gn_ref[...] = jnp.zeros_like(gn_ref)

    normed = rows_ref[0]
    du = du_ref[0]
    gdt_ref[...] += dot(du.astype(BF16), normed)
    total = dot_t(dz_ref[0], wz[...]) + dot_t(dbc_ref[0], wbc_ref[...])

    @pl.when(step == 0)
    def _():
        wait_weight(x_parts, meta_x, cols_xz[0], width, deep, t_ref, wx, sem_x)

    total = total + dot_t(dx_ref[0], wx[...])
    du_cols = jnp.concatenate([du, jnp.zeros((128 - du.shape[0], du.shape[1]), F32)], 0).T
    total = total + dot(du_cols.astype(BF16), wdt_ref[...])
    gn_ref[...] += jnp.sum(total * normed.astype(F32), 0, keepdims=True)
    out = total.astype(BF16)

    @pl.when(step < 2)
    def _():
        send_ref[0] = out

    @pl.when(step >= 2)
    def _():
        keep_ref[0] = out


def project_scan(n_x, meta_x, col_x, with_norm, t_ref, *refs):
    slots, refs = refs[:4], refs[4:]
    gain_ref, wbc_ref, wdt_ref, sr_ref, cp_ref, bp_ref, hp_ref, spread_ref = refs[:8]
    refs = refs[8:]
    x_parts, refs = refs[:n_x], refs[n_x:]
    rows_ref, x_ref, bc_ref, u_ref, y_ref, state_ref = refs[:6]
    held, x_tail, bc_tail, wx, r_s, x_s, bc_s, u_s, sem_x = refs[6:]
    step = pl.program_id(0)
    blocks = x_s.shape[0]
    deep = wx.shape[0] // (t_ref.shape[0] - 1)

    def weights():
        return start_weight(x_parts, meta_x, col_x, wx.shape[1], deep, t_ref, wx, sem_x)

    for at in range(4):

        @pl.when(step == at)
        def _():
            copies = weights() if at == 0 else []
            value = slots[at][...]
            if with_norm:
                value = value.astype(F32)
                scale = lax.rsqrt(jnp.mean(value * value, -1, keepdims=True) + EPS)
                value = (value * scale * gain_ref[...]).astype(BF16)
            r_s[...] = value
            wait_all(copies)

    @pl.when(step < blocks)
    def _():
        value = r_s[...]
        rows_ref[0] = value
        x = dot(value, wx[...])
        bc = dot(value, wbc_ref[...])
        u = dot_t(wdt_ref[...][:HEAD_ROWS], value)
        x = x.astype(BF16)
        x_ref[0], bc_ref[0], u_ref[0] = x, bc, u
        x_s[step], bc_s[step], u_s[step] = x.astype(F32), bc, u

    @pl.when(step == blocks)
    def _():
        held[...] = jnp.zeros_like(held)
        x_tail[...] = jnp.zeros_like(x_tail)
        bc_tail[...] = jnp.zeros_like(bc_tail)

    @pl.when(step >= blocks)
    def _():
        slot = (step - blocks) ^ t_ref[0]
        scan_block(
            x_s[slot], bc_s[slot], u_s[slot], sr_ref[0], cp_ref[0], bp_ref[...], hp_ref[0], spread_ref,
            y_ref, state_ref, held, x_tail, bc_tail,
        )


def lane_columns(columns, rows):
    lane = lax.broadcasted_iota(jnp.int32, (rows, 128), 1)
    result = jnp.zeros((rows, 128), F32)
    for at, column in enumerate(columns):
        result = jnp.where(lane == at, column, result)
    return result


def three_parts(value):
    high = value.astype(BF16).astype(F32)
    rest = value - high
    middle = rest.astype(BF16).astype(F32)
    return [high, middle, rest - middle]


def gate_forward(n_z, meta_z, n_o, meta_o, cols_zo, is_last, t_ref, *refs):
    rows_ref, y_ref, gain_ref = refs[:3]
    refs = refs[3:]
    cots = ()
    if is_last:
        cots, refs = refs[:4], refs[4:]
    z_parts, refs = refs[:n_z], refs[n_z:]
    o_parts, refs = refs[:n_o], refs[n_o:]
    z_ref, send_ref, keep_ref = refs[:3]
    refs = refs[3:]
    if is_last:
        cot_ref, dg_ref, sums_ref = refs[:3]
        refs = refs[3:]
    wz, wo, sem_z, sem_o = refs
    step = pl.program_id(0)
    width = wz.shape[1]
    deep = wz.shape[0] // (t_ref.shape[0] - 1)

    @pl.when(step == 0)
    def _():
        copies = start_weight(z_parts, meta_z, cols_zo[0], width, deep, t_ref, wz, sem_z)
        start_weight(o_parts, meta_o, cols_zo[1], width, deep, t_ref, wo, sem_o)
        wait_all(copies)

    z = dot(rows_ref[0], wz[...]).astype(BF16)

    @pl.when(step == 0)
    def _():
        wait_weight(o_parts, meta_o, cols_zo[1], width, deep, t_ref, wo, sem_o)

    z_ref[0] = z
    z = z.astype(F32)
    v = y_ref[0] * (z * jax.nn.sigmoid(z))
    gain = gain_ref[0][6:7]
    squares = jnp.sum(v * v, -1, keepdims=True)
    scaled = v * gain
    part = dot_t(scaled.astype(BF16), wo[...]).astype(BF16)
    features = wz.shape[0]
    rows = z.shape[0]

    def put(ref):
        ref[0, :, :features] = part
        if not is_last:
            ref[0, :, features:] = lane_columns(three_parts(squares), rows).astype(BF16)

    @pl.when(step < 2)
    def _():
        put(send_ref)

    @pl.when(step >= 2)
    def _():
        put(keep_ref)

    if is_last:
        for at, slot in enumerate((1, 3, 0, 2)):

            @pl.when(step == at)
            def _():
                cot_ref[0] = cots[slot][...]

        d_gated = dot(cot_ref[0], wo[...])
        dg_ref[0] = d_gated.astype(BF16)
        cross = jnp.sum(d_gated * scaled, -1, keepdims=True)
        sums_ref[0] = lane_columns([squares, cross], rows).T[:8]


def gate_backward(n_o, meta_o, col_o, is_last, inner, t_ref, *refs):
    z_ref, y_ref, gain_ref = refs[:3]
    refs = refs[3:]
    if is_last:
        dg_ref, sums_ref = refs[:2]
        refs = refs[2:]
        dy_ref, dz_ref, gated_ref, gg_ref = refs
    else:
        cots, refs = refs[:4], refs[4:]
        o_parts, refs = refs[:n_o], refs[n_o:]
        dy_ref, dz_ref, gated_ref, gg_ref, cot_ref, wo, extra_s, sem_o = refs
    step = pl.program_id(0)

    @pl.when(step == 0)
    def _():
        gg_ref[...] = jnp.zeros_like(gg_ref)
        if not is_last:
            deep = wo.shape[0] // (t_ref.shape[0] - 1)
            wait_all(
                start_weight(o_parts, meta_o, col_o, wo.shape[1], deep, t_ref, wo, sem_o)
            )

    if is_last:
        d_gated = dg_ref[0].astype(F32)
        sums = sums_ref[0]
        cols = jnp.concatenate([sums, jnp.zeros((120, sums.shape[1]), F32)], 0).T
        scale = lax.rsqrt(cols[:, 0:1] / inner + EPS)
        cross = cols[:, 1:2]
    else:
        features = wo.shape[0]
        for at in range(4):

            @pl.when(step == at)
            def _():
                cot_ref[0] = cots[at][:, :features]
                extra_s[...] = cots[at][:, features:].astype(F32)

        d_gated = dot(cot_ref[0], wo[...])
        extra = extra_s[...]
        scale = extra[:, 0:1] + extra[:, 1:2] + extra[:, 2:3]
        cross = extra[:, 3:4] + extra[:, 4:5] + extra[:, 5:6]
    z, y, gain = z_ref[0].astype(F32), y_ref[0], gain_ref[0][6:7]
    sig = jax.nn.sigmoid(z)
    silu = z * sig
    v = y * silu
    normed = v * scale
    gated_ref[0] = (normed * gain).astype(BF16)
    gg_ref[6:7] += jnp.sum(d_gated * normed, 0, keepdims=True)
    dv = d_gated * gain * scale - v * (scale * scale * scale * cross / inner)
    dy_ref[0] = (dv * silu).astype(BF16)
    dz_ref[0] = (dv * y * (sig * (1.0 + z * (1.0 - sig)))).astype(BF16)


def layer_spec(array, k):
    return pl.BlockSpec((1,) + array.shape[1:], lambda at, t: (k,) + (0,) * (array.ndim - 1))


def whole_spec(shape):
    return pl.BlockSpec(shape, lambda at, t: (0,) * len(shape))


ANY = pl.BlockSpec(memory_space=pl.ANY)


def call(body, table, grid, ins, in_specs, outs, out_specs, scratch, flops, name, aliases=None):
    size = sum(item.size * item.dtype.itemsize for item in list(ins) + list(outs))
    return pl.pallas_call(
        body,
        grid_spec=pltpu.PrefetchScalarGridSpec(
            num_scalar_prefetch=1,
            grid=(grid,),
            in_specs=in_specs,
            out_specs=out_specs,
            scratch_shapes=scratch,
        ),
        out_shape=outs,
        compiler_params=pltpu.CompilerParams(
            dimension_semantics=("arbitrary",), vmem_limit_bytes=VMEM
        ),
        cost_estimate=pl.CostEstimate(flops=flops, bytes_accessed=size, transcendentals=0),
        name=name,
        input_output_aliases=aliases or {},
    )(table, *ins)


def run_project(k, table, slots, gain, w_bc, w_dt, lines, params, bc_params, spread, weight, col, norm):
    blocks = len(slots)
    rows, features = slots[0].shape
    wide = w_bc.shape[1]
    chan, head = params
    width = chan.shape[2]
    states = wide // 2
    last = blocks - 1

    def early(shape):
        return pl.BlockSpec((1,) + shape, lambda at, t: (jnp.minimum(at, last), 0, 0))

    def block(shape):
        return pl.BlockSpec((1,) + shape, lambda at, t: (jnp.maximum(at - blocks, 0), 0, 0))

    def slot(shape):
        return pl.BlockSpec((1,) + shape, lambda at, t: (jnp.maximum(at - blocks, 0) ^ t[0], 0, 0))

    ins = [*slots, gain, w_bc, w_dt, lines, chan, bc_params, head, spread, *weight[0]]
    in_specs = [whole_spec(item.shape) for item in slots]
    in_specs += [whole_spec(item.shape) for item in (gain, w_bc, w_dt)]
    in_specs += [block((8, rows)), layer_spec(chan, k), whole_spec(bc_params.shape)]
    in_specs += [layer_spec(head, k), whole_spec(spread.shape)] + [ANY] * len(weight[0])
    outs = [
        jax.ShapeDtypeStruct((blocks, rows, features), BF16),
        jax.ShapeDtypeStruct((blocks, rows, width), BF16),
        jax.ShapeDtypeStruct((blocks, rows, wide), F32),
        jax.ShapeDtypeStruct((blocks, HEAD_ROWS, rows), F32),
        jax.ShapeDtypeStruct((blocks, rows, width), F32),
        jax.ShapeDtypeStruct((blocks, states, width), F32),
    ]
    out_specs = [
        early((rows, features)), early((rows, width)), early((rows, wide)),
        early((HEAD_ROWS, rows)), slot((rows, width)), block((states, width)),
    ]
    scratch = [
        pltpu.VMEM((states, width), F32),
        pltpu.VMEM((8, width), F32),
        pltpu.VMEM((8, wide), F32),
        pltpu.VMEM((features, width), BF16),
        pltpu.VMEM((rows, features), BF16),
        pltpu.VMEM((blocks, rows, width), F32),
        pltpu.VMEM((blocks, rows, wide), F32),
        pltpu.VMEM((blocks, HEAD_ROWS, rows), F32),
        pltpu.SemaphoreType.DMA((len(weight[1]),)),
    ]
    body = partial(project_scan, len(weight[0]), weight[1], col, norm)
    return call(body, table, 2 * blocks, ins, in_specs, outs, out_specs, scratch, 10**10, "project_scan")


def run_gate_forward(k, table, rows, y, chan, cots, w_z, w_o, cols):
    blocks, count, features = rows.shape
    width = y.shape[2]
    is_last = cots is not None
    extra = 0 if is_last else 128

    def slot(shape):
        return pl.BlockSpec((1,) + shape, lambda at, t: (2 * at + 1 - 5 * (at // 2), 0, 0))

    cots = cots or []
    ins = [rows, y, chan, *cots, *w_z[0], *w_o[0]]
    in_specs = [slot((count, features)), slot((count, width)), layer_spec(chan, k)]
    in_specs += [whole_spec(item.shape) for item in cots] + [ANY] * (len(w_z[0]) + len(w_o[0]))
    half = jax.ShapeDtypeStruct((2, count, features + extra), BF16)
    outs = [jax.ShapeDtypeStruct((blocks, count, width), BF16), half, half]
    out_specs = [
        slot((count, width)),
        pl.BlockSpec((1, count, features + extra), lambda at, t: (jnp.minimum(at, 1), 0, 0)),
        pl.BlockSpec((1, count, features + extra), lambda at, t: (jnp.maximum(at - 2, 0), 0, 0)),
    ]
    if is_last:
        outs += [
            jax.ShapeDtypeStruct((blocks, count, features), BF16),
            jax.ShapeDtypeStruct((blocks, count, width), BF16),
            jax.ShapeDtypeStruct((blocks, 8, count), F32),
        ]
        out_specs += [slot((count, features)), slot((count, width)), slot((8, count))]
    scratch = [
        pltpu.VMEM((features, width), BF16),
        pltpu.VMEM((features, width), BF16),
        pltpu.SemaphoreType.DMA((len(w_z[1]),)),
        pltpu.SemaphoreType.DMA((len(w_o[1]),)),
    ]
    body = partial(gate_forward, len(w_z[0]), w_z[1], len(w_o[0]), w_o[1], cols, is_last)
    return call(body, table, blocks, ins, in_specs, outs, out_specs, scratch, 6 * 10**9, "gate_forward")


def run_gate_backward(k, table, z, y, chan, known, cots, w_o, col, inner):
    blocks, count, width = z.shape
    is_last = cots is None

    def slot(shape):
        return pl.BlockSpec((1,) + shape, lambda at, t: (at, 0, 0))

    ins = [z, y, chan]
    in_specs = [slot((count, width)), slot((count, width)), layer_spec(chan, k)]
    outs = [
        jax.ShapeDtypeStruct((blocks, count, width), BF16),
        jax.ShapeDtypeStruct((blocks, count, width), BF16),
        jax.ShapeDtypeStruct((blocks, count, width), BF16),
        jax.ShapeDtypeStruct((8, width), F32),
    ]
    out_specs = [slot((count, width))] * 3 + [whole_spec((8, width))]
    scratch = []
    if is_last:
        ins += list(known)
        in_specs += [slot((count, width)), slot((8, count))]
    else:
        features = cots[0].shape[1] - 128
        ins += [*cots, *w_o[0]]
        in_specs += [whole_spec(item.shape) for item in cots] + [ANY] * len(w_o[0])
        outs.append(jax.ShapeDtypeStruct((blocks, count, features), BF16))
        out_specs.append(slot((count, features)))
        scratch = [
            pltpu.VMEM((features, width), BF16),
            pltpu.VMEM((count, 128), F32),
            pltpu.SemaphoreType.DMA((len(w_o[1]),)),
        ]
    body = partial(gate_backward, len(w_o[0]), w_o[1], col, is_last, inner)
    return call(body, table, blocks, ins, in_specs, outs, out_specs, scratch, 3 * 10**9, "gate_backward")


def run_mix_backward(k, table, x, bc, u, lines, y, dy, state, params, bc_params, spread, heads_of, gg, top, steps, before):
    blocks, rows, width = x.shape
    wide = bc.shape[2]
    states = wide // 2
    chan, head = params

    def slot(shape):
        return pl.BlockSpec((1,) + shape, lambda at, t: ((top - at) ^ t[0], 0, 0))

    def earlier(shape):
        return pl.BlockSpec(
            (1,) + shape,
            lambda at, t: (jnp.maximum(top - at - 1, 0) ^ t[0], rows // shape[0] - 1, 0),
        )

    def straight(shape):
        return pl.BlockSpec((1,) + shape, lambda at, t: (top - at, 0, 0))

    ins = [x, x, bc, bc, u, lines, y, dy, state, chan, bc_params, head, spread, heads_of]
    in_specs = [
        slot((rows, width)), earlier((16, width)), slot((rows, wide)), earlier((8, wide)),
        slot((HEAD_ROWS, rows)), straight((8, rows)),
        slot((rows, width)), slot((rows, width)), straight((states, width)),
        layer_spec(chan, k), whole_spec(bc_params.shape), layer_spec(head, k),
        whole_spec(spread.shape), whole_spec(heads_of.shape),
    ]
    outs = [
        jax.ShapeDtypeStruct((blocks, rows, width), BF16),
        jax.ShapeDtypeStruct((blocks, rows, wide), BF16),
        jax.ShapeDtypeStruct((blocks, HEAD_ROWS, rows), F32),
        jax.ShapeDtypeStruct((8, width), F32),
        jax.ShapeDtypeStruct((8, wide), F32),
        jax.ShapeDtypeStruct((2, HEAD_ROWS, 128), F32),
        jax.ShapeDtypeStruct((states, width), F32),
        jax.ShapeDtypeStruct((3, 8, width), F32),
        jax.ShapeDtypeStruct((3, 8, wide), F32),
    ]
    out_specs = [slot((rows, width)), slot((rows, wide)), slot((HEAD_ROWS, rows))]
    out_specs += [whole_spec(item.shape) for item in outs[3:]]
    aliases = {}
    if before:
        aliases = {1 + len(ins) + at: at for at in range(3)}
        ins += list(before)
        in_specs += [ANY] * 3 + [whole_spec(item.shape) for item in outs[3:]]
    else:
        ins.append(gg)
        in_specs.append(whole_spec(gg.shape))
    body = partial(mix_backward, not before)
    return call(body, table, steps, ins, in_specs, outs, out_specs, [], 2 * 10**9 * steps, "mix_backward", aliases)


def run_input_backward(table, dx, dz, dbc, du, normed, w_bc, w_dt, w_x, w_z, cols):
    blocks, rows, width = dx.shape
    features = normed.shape[2]
    wide = dbc.shape[2]

    def slot(shape):
        return pl.BlockSpec((1,) + shape, lambda at, t: (2 * at + 1 - 5 * (at // 2), 0, 0))

    ins = [dx, dz, dbc, du, normed, w_bc, w_dt, *w_x[0], *w_z[0]]
    in_specs = [slot((rows, width)), slot((rows, width)), slot((rows, wide)), slot((HEAD_ROWS, rows))]
    in_specs += [slot((rows, features)), whole_spec(w_bc.shape), whole_spec(w_dt.shape)]
    in_specs += [ANY] * (len(w_x[0]) + len(w_z[0]))
    half = jax.ShapeDtypeStruct((2, rows, features), BF16)
    outs = [
        half, half,
        jax.ShapeDtypeStruct((HEAD_ROWS, features), F32),
        jax.ShapeDtypeStruct((1, features), F32),
    ]
    out_specs = [
        pl.BlockSpec((1, rows, features), lambda at, t: (jnp.minimum(at, 1), 0, 0)),
        pl.BlockSpec((1, rows, features), lambda at, t: (jnp.maximum(at - 2, 0), 0, 0)),
        whole_spec((HEAD_ROWS, features)), whole_spec((1, features)),
    ]
    scratch = [
        pltpu.VMEM((features, width), BF16),
        pltpu.VMEM((features, width), BF16),
        pltpu.SemaphoreType.DMA((len(w_x[1]),)),
        pltpu.SemaphoreType.DMA((len(w_z[1]),)),
    ]
    body = partial(input_backward, len(w_x[0]), w_x[1], len(w_z[0]), w_z[1], cols)
    return call(body, table, blocks, ins, in_specs, outs, out_specs, scratch, 7 * 10**9, "input_backward")


def segment_lines(segment, blocks):
    rows = segment.shape[0] // blocks
    cut = segment.reshape(blocks, rows)
    ends = cut[:, -1:]
    before = jnp.concatenate([cut[:1, :1], ends[:-1]], 0)
    kinds = [cut.astype(F32), (cut == before).astype(F32), (cut == ends).astype(F32)]
    for back in (1, 2, 3):
        earlier = jnp.pad(segment, (back, 0), constant_values=-1)[: segment.shape[0]]
        kinds.append((segment == earlier).astype(F32).reshape(blocks, rows))
    at = jnp.arange(8)[None, :, None]
    lines = jnp.zeros((blocks, 8, rows), F32)
    for index, kind in enumerate(kinds):
        lines = jnp.where(at == index, kind[:, None], lines)
    return lines


def head_tables(heads, width):
    owner = np.arange(width)[None, :] // (width // heads)
    at = np.arange(128)[:, None]
    spread_enter = (at == owner + HEAD_ROWS) | (at == owner + 3 * HEAD_ROWS)
    spread_tail = (at == owner + 2 * HEAD_ROWS) | (at == owner + 4 * HEAD_ROWS)
    spread = np.stack([spread_enter, spread_tail]).astype(np.float32)
    owners = (at[:HEAD_ROWS] == owner).astype(np.float32)
    return jnp.asarray(spread, BF16), jnp.asarray(owners, BF16)


def norm_scale_of(values):
    return lax.rsqrt(jnp.mean(values * values, -1, keepdims=True) + EPS)


def shards(
    hidden, segment_ids, cotangent, norm_gain, in_zx, in_dt, in_bc, conv_x, conv_x_bias,
    conv_bc, conv_bc_bias, dt_bias, a_log, skip_d, gated_gain, out_wt,
):
    layers = in_zx.shape[0]
    count = lax.axis_size("fsdp")
    tp_count = lax.axis_size("tp")
    tp_at = lax.axis_index("tp").astype(jnp.int32)
    own, features = hidden.shape
    deep = in_zx.shape[1]
    width = in_zx.shape[3]
    heads = in_dt.shape[2]
    wide = in_bc.shape[2]
    bc_deep = in_bc.shape[1]
    shared = conv_bc.shape[1]
    taps = conv_bc.shape[2]
    inner = width * tp_count
    dt_lines = -(-deep * heads // wide)
    dt_rest = dt_lines * wide - deep * heads
    lines = -(-(bc_deep + dt_lines + 1) // 16) * 16
    table = placement(tp_at)

    packs, weights, wholes = [], [], []
    for k in range(layers):
        tiny = [conv_bc[k].reshape(-1), conv_bc_bias[k]]
        tiny = jnp.concatenate(tiny + ([norm_gain.reshape(-1)] if k == 0 else []))
        tiny = jnp.pad(tiny, (0, wide - tiny.shape[0]))[None]
        dt = jnp.pad(in_dt[k].T.reshape(-1), (0, dt_rest)).reshape(dt_lines, wide)
        pack = jnp.concatenate([in_bc[k], dt, tiny], 0)
        packs.append(jnp.pad(pack, ((0, lines - pack.shape[0]), (0, 0))))

    ring_x = RingGather(in_zx[0, :, 1])
    over = permute(hidden, "tp", 2)
    beside = permute(hidden, "tp", 1)
    ring_x.step()
    walk = is_walk()
    pack = double(packs[0][None, None, None, None, None], "tp", 2, 3)
    for k in range(1, layers):
        whole = lax.all_gather(packs[k], ("fsdp", "tp"), axis=0, tiled=False)
        packs[k] = whole.reshape((count, tp_count) + packs[k].shape)

    def whole_of(k, source, out):
        return jnp.concatenate([source[k, :, 1], source[k, :, 0], out[k]], 1)

    if walk:
        steps = ring_x.steps
        in_zx_late, out_wt_late, *steps[0] = lax.optimization_barrier((in_zx, out_wt) + tuple(steps[0]))
        ring_zo = RingGather(jnp.concatenate([in_zx_late[0, :, 0], out_wt_late[0]], 1))
        ring_x.step(pack)
        pack = double(after(pack, *steps[0]), "fsdp", 4, 0)
        ring_x.step(pack)
        ring_zo.step(*steps[1])
        pack = double(after(pack, *steps[1]), "fsdp", 2, 1)
        ring_x.step(pack)
        pack = double(after(pack, *steps[2]), "fsdp", 1, 2)
        ring_zo.step(pack, *steps[3])
        over = after(over, pack)
    else:
        in_zx_late, out_wt_late = in_zx, out_wt
        ring_zo = RingGather(jnp.concatenate([in_zx[0, :, 0], out_wt[0]], 1))
        pack = lax.all_gather(pack[0], "fsdp", axis=0, tiled=False)[:, None]
    packs[0] = pack = double(pack, "tp", 1, 4).reshape(count, tp_count, lines, wide)
    slots = [hidden, beside, over, permute(over, "tp", 1)]
    cot_over = permute(after(cotangent, pack), "tp", 2)
    cot_beside = permute(after(cotangent, pack), "tp", 1)
    table = after(table, pack, *ring_zo.last())
    ring_zo.step(table)

    lines_of = segment_lines(segment_ids[0], tp_count)
    spread, heads_of = head_tables(heads, width)
    w_bc, w_dt, gains, bc_params = [], [], [], []
    skips = jnp.repeat(skip_d, width // heads, axis=1)
    chan = jnp.stack([conv_x_bias, skips, gated_gain], 1)
    chan = jnp.concatenate([jnp.swapaxes(conv_x, 1, 2), chan], 1)
    chan = jnp.pad(chan, ((0, 0), (0, 1), (0, 0))).astype(F32)
    head = jnp.pad(jnp.stack([dt_bias, a_log], 2), ((0, 0), (0, HEAD_ROWS - heads), (0, 126)))
    params = (chan, head.astype(F32))

    def unpack(k):
        part = packs[k]
        w_bc.append(part[:, :, :bc_deep].reshape(features, wide))
        dt = pick(part[:, :, bc_deep : bc_deep + dt_lines], tp_at, 1)
        dt = dt.reshape(count, -1)[:, : heads * deep]
        dt = dt.reshape(count, heads, deep).swapaxes(0, 1).reshape(heads, features)
        w_dt.append(jnp.pad(dt, ((0, 128 - heads), (0, 0))))
        tiny = part[:, :, bc_deep + dt_lines]
        if k == 0:
            first = shared * (taps + 1)
            every = tiny[:, :, first : first + layers * bc_deep]
            every = every.reshape(features // bc_deep, layers, bc_deep).swapaxes(0, 1)
            gains.extend(every.reshape(layers, 1, features).astype(F32))
        taps_bc = tiny[:, :, : shared * taps].reshape(wide, taps).astype(F32)
        bias_bc = tiny[:, :, shared * taps : shared * (taps + 1)].reshape(1, wide).astype(F32)
        bc_params.append(jnp.pad(jnp.concatenate([taps_bc.T, bias_bc], 0), ((0, 3), (0, 0))))

    unpack(0)
    running = hidden.astype(F32)
    saved = []
    for k in range(layers):
        if k:
            normed = (running * norm_scale_of(running) * gains[k]).astype(BF16)
            over = permute(normed, "tp", 2)
            beside = permute(normed, "tp", 1)
            if walk:
                ring_all.step(normed)
                over, *ring_all.steps[2] = lax.optimization_barrier((over,) + tuple(ring_all.steps[2]))
                behind, ahead = ring_all.steps[2]
                last_x = ring_last(behind[:, :width], ahead[:, :width])
                last_zo = ring_last(behind[:, width:], ahead[:, width:])
            slots = [normed, beside, over, permute(over, "tp", 1)]
        if k == 0:
            w_x = ring_x.weight()
        elif walk:
            w_x = walk_weight(ring_all.own, ring_all.steps[:3] + [last_x])
        else:
            w_x = ring_all.weight()
        rows, x, bc, u, y, state = run_project(
            k, table, slots, gains[k], w_bc[k], w_dt[k], lines_of, params, bc_params[k], spread, w_x, 0, k == 0
        )
        if k == 0:
            y, cot_over, *_ = lax.optimization_barrier((y, cot_over) + tuple(ring_zo.last()))
            ring_zo.step(y)
            cots_last = [cotangent, cot_beside, cot_over, permute(cot_over, "tp", 1)]
            w_zo, cols_zo = ring_zo.weight(), (0, 1)
        else:
            w_zo, cols_zo = w_x, (1, 2)
            if walk:
                y, *last_zo = lax.optimization_barrier((y,) + tuple(last_zo))
                w_zo = walk_weight(ring_all.own, ring_all.steps[:3] + [tuple(last_zo)], width)
        weights.append((w_x, w_zo, cols_zo))
        entry = dict(rows=rows, x=x, bc=bc, u=u, y=y, state=state, h=running)
        is_last = k == layers - 1
        if not is_last:
            next_ring = RingGather(whole_of(k + 1, in_zx_late, out_wt_late))
            next_ring.step(*(ring_zo.last() if k == 0 else (y,)))
        z, send, keep, *more = run_gate_forward(
            k, table, rows, y, chan, cots_last if is_last else None, w_zo, w_zo, cols_zo
        )
        if not is_last and walk:
            send, z, packs[k + 1], *next_ring.steps[0] = lax.optimization_barrier(
                (send, z, packs[k + 1]) + tuple(next_ring.steps[0])
            )
        entry["z"] = z
        entry["near"] = near = permute(send, "tp", 1)
        if not is_last:
            ring_all = next_ring
            going = plus(keep[1], near[1])
            far = permute(going, "tp", 2)
            unpack(k + 1)
            far = after(far, w_bc[k + 1], w_dt[k + 1], bc_params[k + 1])
            if walk:
                ring_all.step(going)
                far, *ring_all.steps[1] = lax.optimization_barrier((far,) + tuple(ring_all.steps[1]))
        else:
            cot, d_gated, sums = more
            sums = tp_sum_slots(sums)
            far = permute(plus(keep[1], near[1]), "tp", 2)
            entry.update(cot=cot, d_gated=d_gated, sums=sums, far=far, parts=keep[0].astype(F32) + near[0].astype(F32))
        if not is_last:
            branch = keep[0].astype(F32) + near[0].astype(F32) + far.astype(F32)
            squares = jnp.sum(branch[:, features:], -1, keepdims=True)
            branch = branch[:, :features]
            scale = lax.rsqrt(squares / inner + EPS)
            entry.update(branch=branch, scale=scale)
            running = running + branch * scale
        saved.append(entry)

    grad_run = cotangent.astype(F32)
    parts = [None] * layers

    def small_sum(parts):
        d_bc, g_norm, gbc, g_dt, gx = (jnp.stack(item) for item in zip(*parts))
        room = (layers, count, tp_count)
        d_norm = (g_norm / jnp.stack(gains)).reshape(room + (bc_deep,))
        d_conv = gbc[:, : taps + 1].reshape((layers, taps + 1) + room[1:] + (shared,))
        d_conv = d_conv.transpose(0, 2, 3, 1, 4).reshape(room + ((taps + 1) * shared,))
        d_tiny = jnp.concatenate([d_norm, d_conv], 3).astype(BF16)
        d_tiny = jnp.pad(d_tiny, ((0, 0), (0, 0), (0, 0), (0, wide - d_tiny.shape[3])))
        d_pack = jnp.concatenate([d_bc.reshape(room + (bc_deep, wide)), d_tiny[:, :, :, None]], 3)
        d_pack = d_pack.transpose(1, 2, 0, 3, 4).reshape(count, tp_count, -1, wide)
        d_dt = g_dt[:, :heads].reshape(layers, heads, count, deep).transpose(2, 0, 1, 3)
        d_dt = jnp.pad(d_dt.reshape(count, layers, -1), ((0, 0), (0, 0), (0, dt_rest))).astype(BF16)
        return SmallSum(d_pack, d_dt.reshape(count, -1, wide), gx.reshape(-1, wide))

    sums_of = [None] * layers
    for k in reversed(range(layers)):
        item = saved[k]
        rows, z, y = item["rows"], item["z"], item["y"]
        w_x, w_zo, cols_zo = weights[k]
        if k == layers - 1:
            cot = item["cot"]
            dy, dz, gated, g_gain = run_gate_backward(
                k, table, z, y, chan, (item["d_gated"], item["sums"]), None, w_zo, cols_zo[1], inner
            )
        else:
            low = grad_run.astype(BF16)
            cross = jnp.sum(low.astype(F32) * item["branch"], -1, keepdims=True)
            extra = three_parts(item["scale"]) + three_parts(cross)
            extra = jnp.concatenate(extra, 1).astype(BF16)
            low = jnp.concatenate([low, jnp.pad(extra, ((0, 0), (0, 128 - 6)))], 1)
            over, beside = permute(low, "tp", 2), permute(low, "tp", 1)
            if walk:
                last_x = sums_of[k + 1][2]
                over = after(over, *ring_step(sums_of[k + 1], low))
                (over,) = ring_pin(sums_of[k + 1], over)
                ring_step([last_x], over)
            cots = [low, beside, over, permute(over, "tp", 1)]
            dy, dz, gated, g_gain, cot = run_gate_backward(
                k, table, z, y, chan, None, cots, w_zo, cols_zo[1], inner
            )
            if walk:
                (dy,) = ring_pin([last_x], dy)

        def weight_grad(left, right):
            result = lax.dot_general(
                left, right, (((0, 1), (0, 1)), ((), ())), preferred_element_type=F32
            )
            return result.astype(BF16)

        ring_o = RingSum(weight_grad(cot, gated).reshape(count, deep, width), table)
        ring_z = RingSum(weight_grad(rows, dz).reshape(count, deep, width), table)
        early = [ring_o, ring_z]
        rounds = early + ([last_x] if k < layers - 1 and walk else [])
        dy = after(dy, *ring_step(rounds, dy), ring_o.terms, ring_z.terms)
        if k == layers - 1:
            dy = after(dy, saved[k]["near"])
        splits = (tp_count,) if k else (tp_count // 2, tp_count - tp_count // 2)
        done, top = None, tp_count - 1
        for steps in splits:
            done = run_mix_backward(
                k, table, item["x"], item["bc"], item["u"], lines_of, y, dy, item["state"], params,
                bc_params[k], spread, heads_of, g_gain, top, steps, done,
            )
            top -= steps
            if top >= 0:
                done = list(done)
                (done[6],) = ring_pin(rounds, done[6])
                done[6] = after(done[6], *ring_step(rounds))
        dx, dbc, du, gx, gbc, gh = done[:6]
        (dx,) = ring_pin(rounds, dx)
        if k == layers - 1:
            dx, far = lax.optimization_barrier((dx, item["far"]))
            scale = lax.rsqrt(item["sums"][0, 0] / inner + EPS)[:, None]
            running = running + (item["parts"] + far.astype(F32)) * scale
        every = [ring_o, ring_z]
        if k == 0:
            ring_x = RingSum(weight_grad(rows, dx).reshape(count, deep, width), table)
            every.append(ring_x)
            sent = ring_step(every)
            dx_now = after(dx, *sent) if walk else dx
        else:
            sent = ring_step(every)
            dx_now = after(dx, *sent) if walk else dx
        send, keep, g_dt, g_norm = run_input_backward(
            table, dx_now, dz, dbc, du, rows, w_bc[k], w_dt[k], w_x, w_zo, (0, cols_zo[0])
        )
        parts[k] = [weight_grad(rows, dbc) if k else None, g_norm, gbc, g_dt, gx]
        if k == 0:
            (send,) = ring_pin(every, send)
            near = permute(send, "tp", 1)
            going = plus(keep[1], near[1])
            far = permute(going, "tp", 2)
            ring_step(every, going)
            (far,) = ring_pin(every, far)
            ring_step([ring_x], far)
            parts[k][0] = weight_grad(rows, after(dbc, far))
            small = small_sum(parts)
            got = small.over_core()
            (got,) = ring_pin([ring_x], got)
            last_sent = ring_step([ring_x])
            if walk:
                got = after(got, *last_sent)
                far = after(far, *last_sent)
            got = small.over_z(small.over_x(small.over_y(got)))
        else:
            (send,) = ring_pin(every, send)
            near = permute(send, "tp", 1)
            going = plus(keep[1], near[1])
            far = permute(going, "tp", 2)
            ring_step(every, going)
            ring_x = RingSum(weight_grad(rows, after(dx, going)).reshape(count, deep, width), table)
            far, ring_x.terms, parts[k][0] = ring_pin(every, far, ring_x.terms, parts[k][0])
        sums_of[k] = (ring_o, ring_z, ring_x)
        d_normed = keep[0].astype(F32) + near[0].astype(F32) + far.astype(F32)
        h = item["h"]
        inv = norm_scale_of(h)
        scaled = d_normed * gains[k]
        grad_run = (
            grad_run
            + inv * scaled
            - h * (inv**3 * (jnp.sum(scaled * h, -1, keepdims=True) / features))
        )

    d_pack, vector = small.result(got)
    d_dt = d_pack[layers * (bc_deep + 1) :].reshape(layers, -1)[:, : heads * deep]
    d_pack = d_pack[: layers * (bc_deep + 1)].reshape(layers, -1, wide)
    vector = vector.reshape(layers, 8, width)
    tiny = d_pack[:, bc_deep]
    conv = tiny[:, bc_deep : bc_deep + (taps + 1) * shared].reshape(layers, taps + 1, shared)
    zx, out = ring_results([ring for rings in sums_of for ring in rings])
    return (
        running,
        grad_run,
        tiny[:, :bc_deep],
        zx,
        d_dt.reshape(layers, heads, deep).swapaxes(1, 2),
        d_pack[:, :bc_deep],
        vector[:, :taps].swapaxes(1, 2),
        vector[:, taps],
        conv[:, :taps].swapaxes(1, 2),
        conv[:, taps],
        vector[:, 7, :heads],
        vector[:, 7, HEAD_ROWS : HEAD_ROWS + heads],
        jnp.sum(vector[:, 5].reshape(layers, heads, -1), 2),
        vector[:, 6],
        out,
    )


def solution(mesh):
    tokens = P(("fsdp", "tp"), None)
    split = P(None, ("fsdp", "tp"))
    rows = P(None, ("fsdp", "tp"), None)
    weights = (
        split,
        P(None, "fsdp", None, "tp"),
        P(None, "fsdp", "tp"),
        rows,
        P(None, "tp", None),
        P(None, "tp"),
        rows,
        split,
        P(None, "tp"),
        P(None, "tp"),
        P(None, "tp"),
        P(None, "tp"),
        P(None, "fsdp", "tp"),
    )
    return jax.shard_map(
        shards,
        mesh=mesh,
        in_specs=(tokens, P("fsdp", None), tokens) + weights,
        out_specs=(tokens, tokens) + weights,
        check_vma=False,
    )
```

```python
from functools import partial

import jax
import jax.numpy as jnp
import numpy as np
from jax import lax
from jax.experimental import pallas as pl
from jax.experimental.pallas import tpu as pltpu
from jax.sharding import PartitionSpec as P

EPS = 1e-05
NEG = -1e30
F32 = jnp.float32
BF16 = jnp.bfloat16
WALK = (0, 2, 4, 6, 7, 5, 3, 1)
HEAD_ROWS = 16
VMEM = 48 * 1024 * 1024
SMALL = 24 * 1024 * 1024


def permute(value, axis, mask):
    size = lax.axis_size(axis)
    return lax.ppermute(value, axis, [(at, at ^ mask) for at in range(size)])


def tp_gather(value):
    across = permute(value, "tp", 2)
    core = permute(value, "tp", 1)
    return [value, core, across, permute(across, "tp", 1)]


def tp_reduce(send, keep):
    near = permute(send, "tp", 1)
    far = (keep[1].astype(F32) + near[1].astype(F32)).astype(keep.dtype)
    far = permute(far, "tp", 2)
    return keep[0].astype(F32) + near[0].astype(F32) + far.astype(F32)


def tp_sum_slots(value):
    near = permute(value, "tp", 1)
    value = value + jnp.stack([near[1], near[0], near[3], near[2]])
    far = permute(value, "tp", 2)
    return value + jnp.stack([far[2], far[3], far[0], far[1]])


def is_walk():
    return lax.axis_size("fsdp") == len(WALK)


def placement(tp_at):
    size = lax.axis_size("fsdp")
    if not is_walk():
        owners = jnp.arange(size, dtype=jnp.int32)
    else:
        all_owners = [[WALK[(WALK.index(f) + k) % size] for k in range(size)] for f in range(size)]
        owners = pick(jnp.array(all_owners, jnp.int32), lax.axis_index("fsdp"), 0)
    return jnp.concatenate([tp_at[None], owners])


def step_ring(value, by):
    size = len(WALK)
    return lax.ppermute(
        value, "fsdp", [(WALK[at], WALK[(at + by) % size]) for at in range(size)]
    )


def ring_pair(behind, ahead):
    return step_ring(behind, 1), step_ring(ahead, -1)


def ring_last(behind, ahead):
    half = behind.shape[0] // 2
    return step_ring(behind[:half], 1), step_ring(ahead[half:], -1)


def walk_weight(own, steps, lack=0):
    arrays = [own]
    rows = own.shape[0]
    meta = [(0, 0, rows, 0, 0, True, 0)]
    for at, (behind, ahead) in enumerate(steps):
        arrays += [behind, ahead]
        if at < 3:
            meta.append((len(arrays) - 2, 0, rows, 7 - at, 0, True, 0))
            meta.append((len(arrays) - 1, 0, rows, 1 + at, 0, True, 0))
        else:
            meta.append((len(arrays) - 2, 0, rows // 2, 4, 0, True, lack))
            meta.append((len(arrays) - 1, 0, rows // 2, 4, rows // 2, True, lack))
    return arrays, tuple(meta)


def natural_weight(array, count, deep, stride):
    return [array], tuple((0, at * stride, deep, at, 0, False, 0) for at in range(count))


def after(value, *earlier):
    return lax.optimization_barrier((value,) + earlier)[0]


class RingGather:
    def __init__(self, own):
        self.own = own
        self.steps = []

    def step(self, *earlier):
        if not is_walk():
            return
        behind, ahead = self.steps[-1] if self.steps else (self.own, self.own)
        if earlier:
            behind, ahead, *_ = lax.optimization_barrier((behind, ahead) + earlier)
        go = ring_last if len(self.steps) == 3 else ring_pair
        self.steps.append(go(behind, ahead))

    def last(self):
        return self.steps[-1] if self.steps else ()

    def weight(self):
        if is_walk():
            return walk_weight(self.own, self.steps)
        whole = lax.all_gather(self.own, "fsdp", axis=0, tiled=True)
        deep = self.own.shape[0]
        return natural_weight(whole, lax.axis_size("fsdp"), deep, deep)


def double(value, axis, mask, dim):
    other = permute(value, axis, mask)
    second = (lax.axis_index(axis) & mask) != 0
    low = jnp.where(second, other, value)
    high = jnp.where(second, value, other)
    return jnp.concatenate([low, high], dim)


def plus(left, right):
    return (left.astype(F32) + right.astype(F32)).astype(left.dtype)


def pick(value, at, axis):
    return lax.dynamic_index_in_dim(value, at, axis, keepdims=False, allow_negative_indices=False)


def two_parts(value):
    high = value.astype(BF16)
    return jnp.concatenate([high, (value - high.astype(F32)).astype(BF16)], 0)


def joined(parts):
    half = parts.shape[0] // 2
    return parts[:half].astype(F32) + parts[half:].astype(F32)


class SmallSum:
    def __init__(self, terms, own, vector):
        index = lax.axis_index("tp")
        self.core, self.y = index & 1, index >> 1
        self.terms = terms.reshape((terms.shape[0], 2, 2) + terms.shape[2:])
        self.own, self.vector = own, vector
        self.wide = vector.shape[1]

    def over_core(self):
        return permute(pick(self.terms, 1 - self.core, 2), "tp", 1)

    def over_y(self, got):
        self.terms = plus(pick(self.terms, self.core, 2), got)
        return permute(pick(self.terms, 1 - self.y, 1), "tp", 2)

    def over_x(self, got):
        terms = plus(pick(self.terms, self.y, 1), got)
        self.terms = terms = jnp.concatenate([terms, self.own], 1)
        self.rows = rows = terms.shape[1]
        if not is_walk():
            return ()
        index = lax.axis_index("fsdp")
        self.x, self.z = index & 1, index >> 1
        self.terms = terms = terms.reshape((4, 2) + terms.shape[1:])
        got = pick(terms, 1 - self.x, 1).reshape(4 * rows, self.wide)
        return permute(jnp.concatenate([got, two_parts(self.vector)], 0), "fsdp", 1)

    def over_z(self, got):
        if not is_walk():
            return ()
        rows, terms = self.rows, self.terms
        self.vector = self.vector + joined(got[4 * rows :])
        got = got[: 4 * rows].reshape(4, rows, self.wide)
        mine = pick(terms, self.x, 1)
        self.total = pick(mine, self.z, 0).astype(F32) + pick(got, self.z, 0).astype(F32)
        sent = two_parts(self.vector)
        parts = []
        for mask in (3, 2, 1):
            part = plus(pick(mine, self.z ^ mask, 0), pick(got, self.z ^ mask, 0))
            parts.append(permute(jnp.concatenate([part, sent], 0), "fsdp", 2 * mask))
        return tuple(parts)

    def result(self, parts):
        if not is_walk():
            own = lax.psum_scatter(self.terms, "fsdp", scatter_dimension=0, tiled=False)
            return own.astype(F32), lax.psum(self.vector, "fsdp")
        total, vector = self.total, self.vector
        for part in parts:
            total = total + part[: self.rows].astype(F32)
            vector = vector + joined(part[self.rows :])
        return total, vector


class RingSum:
    def __init__(self, terms, table):
        self.terms = terms
        self.table = table
        self.at = 0
        self.sent = ()
        self.first = 0


def ring_payload(steps, firsts, which, t_ref, *refs):
    del t_ref
    terms, refs = refs[: 2 * len(steps)], refs[2 * len(steps) :]
    forth_out, back_out = refs[-2:]
    row = 0
    for at, step in enumerate(steps):
        ahead, behind = terms[2 * at][0], terms[2 * at + 1][0]
        deep = ahead.shape[0]
        half = deep // 2
        if step == 0:
            forth_out[row : row + half] = ahead[:half]
            back_out[row : row + half] = behind[half:]
            row += half
            continue
        count = half if step == 1 else deep
        span = pl.ds(firsts[at], count)
        forth = refs[2 * which[at]][span, :].astype(F32)
        back = refs[2 * which[at] + 1][span, :].astype(F32)
        if step == 1:
            forth_out[row : row + half] = (ahead[:half].astype(F32) + forth).astype(BF16)
            forth_out[row + half : row + deep] = ahead[half:]
            back_out[row : row + half] = behind[:half]
            back_out[row + half : row + deep] = (behind[half:].astype(F32) + back).astype(BF16)
        else:
            forth_out[row : row + deep] = (ahead.astype(F32) + forth).astype(BF16)
            back_out[row : row + deep] = (behind.astype(F32) + back).astype(BF16)
        row += deep


def ring_final(firsts, which, t_ref, *refs):
    del t_ref
    count = len(firsts)
    terms, (zx_ref, out_ref) = refs[:count], refs[-2:]
    arrived = refs[count:-2]
    deep = out_ref.shape[1]
    for at in range(count):
        span = pl.ds(firsts[at], deep)
        total = (
            terms[at][0].astype(F32)
            + arrived[2 * which[at]][span, :].astype(F32)
            + arrived[2 * which[at] + 1][span, :].astype(F32)
        )
        if at % 3 == 0:
            out_ref[at // 3] = total
        else:
            zx_ref[at // 3, :, at % 3 - 1, :] = total


def term_spec(terms, slot):
    return pl.BlockSpec((1,) + terms.shape[1:], lambda at, t: (t[1 + slot], 0, 0))


def arrivals(rings):
    pairs, which = [], []
    for ring in rings:
        if not ring.sent:
            which.append(0)
            continue
        known = [at for at, pair in enumerate(pairs) if pair[0] is ring.sent[0]]
        which.append(known[0] if known else len(pairs))
        if not known:
            pairs.append(ring.sent)
    return [item for pair in pairs for item in pair], tuple(which)


def ring_step(rings, *earlier):
    if not is_walk():
        return ()
    arrived, which = arrivals(rings)
    if earlier and arrived:
        arrived = list(lax.optimization_barrier(tuple(arrived) + tuple(earlier))[: len(arrived)])
    table = rings[0].table
    if earlier and not arrived:
        table = after(table, *earlier)
    ins, in_specs, rows = [], [], 0
    firsts = []
    deep, width = rings[0].terms.shape[1:]
    for ring in rings:
        slots = ((4, 4), (3, 5), (2, 6), (1, 7))[ring.at]
        ins += [ring.terms, ring.terms]
        in_specs += [term_spec(ring.terms, slots[0]), term_spec(ring.terms, slots[1])]
        firsts.append(ring.first)
        ring.first = rows
        rows += deep if ring.at else deep // 2
    ins += arrived
    in_specs += [whole_spec(item.shape) for item in arrived]
    out = jax.ShapeDtypeStruct((rows, width), BF16)
    steps = tuple(ring.at for ring in rings)
    body = partial(ring_payload, steps, tuple(firsts), which)
    forth, back = call(
        body, table, 1, ins, in_specs, [out, out], [whole_spec(out.shape)] * 2, [], 10**6, "ring_payload"
    )
    sent = ring_pair(forth, back)
    for ring in rings:
        ring.sent = sent
        ring.at += 1
    return forth, back


def ring_pin(rings, *values):
    arrived, _ = arrivals(rings)
    if not arrived:
        return values
    olds = {id(item): at for at, item in enumerate(arrived)}
    done = lax.optimization_barrier(tuple(arrived) + tuple(values))
    for ring in rings:
        if ring.sent:
            ring.sent = tuple(done[olds[id(item)]] for item in ring.sent)
    return done[len(arrived) :]


def ring_results(rings):
    layers = len(rings) // 3
    deep, width = rings[0].terms.shape[1:]
    if not is_walk():
        sums = [
            lax.psum_scatter(ring.terms, "fsdp", scatter_dimension=0, tiled=False).astype(F32)
            for ring in rings
        ]
        zx = [jnp.stack(sums[3 * k + 1 : 3 * k + 3], 1) for k in range(layers)]
        return jnp.stack(zx), jnp.stack(sums[::3])
    arrived, which = arrivals(rings)
    ins = [ring.terms for ring in rings] + arrived
    in_specs = [term_spec(ring.terms, 0) for ring in rings]
    in_specs += [whole_spec(item.shape) for item in arrived]
    outs = [
        jax.ShapeDtypeStruct((layers, deep, 2, width), F32),
        jax.ShapeDtypeStruct((layers, deep, width), F32),
    ]
    out_specs = [whole_spec(item.shape) for item in outs]
    body = partial(ring_final, tuple(ring.first for ring in rings), which)
    return call(body, rings[0].table, 1, ins, in_specs, outs, out_specs, [], 10**6, "ring_final")


def dot(left, right):
    return jnp.dot(left, right, preferred_element_type=F32)


def dot_t(left, right):
    return lax.dot_general(left, right, (((1,), (1,)), ((), ())), preferred_element_type=F32)


def shifted_sum(value, sign):
    width = value.shape[1]
    lane = lax.broadcasted_iota(jnp.int32, value.shape, 1)
    by = 1
    while by < width:
        if sign > 0:
            value = value + jnp.where(lane >= by, pltpu.roll(value, by, 1), 0.0)
        else:
            value = value + jnp.where(lane < width - by, pltpu.roll(value, width - by, 1), 0.0)
        by *= 2
    return value


def conv_parts(cur, prev, weight, bias, marks):
    rows = cur.shape[0]
    ext = jnp.concatenate([prev, cur], 0)
    pre = bias + cur * weight[3:4]
    moved = []
    for back in (1, 2, 3):
        item = ext[8 - back : 8 - back + rows]
        moved.append(item)
        pre = pre + item * marks[back - 1] * weight[3 - back : 4 - back]
    return pre, moved


def rates(u, params, seg_rows):
    u = u + params[:, 0:1]
    rate = jnp.exp(params[:, 1:2])
    dt = jnp.maximum(u, 0.0) + jnp.log1p(jnp.exp(-jnp.abs(u)))
    log_dt = jnp.where(u < -15.0, u, jnp.log(dt))
    a = -dt * rate
    total = shifted_sum(a, 1)
    last = total[:, -1:]
    less = total - log_dt
    enter = jnp.exp(total) * seg_rows[1:2]
    tail = jnp.exp(last - less) * seg_rows[2:3]
    return u, dt, a, rate, total, less, enter, tail


def as_columns(first, enter, tail, lines):
    enter_hi = enter.astype(BF16).astype(F32)
    tail_hi = tail.astype(BF16).astype(F32)
    rest = jnp.zeros((128 - 5 * HEAD_ROWS - 8, enter.shape[1]), F32)
    stacked = jnp.concatenate(
        [first, enter_hi, tail_hi, enter - enter_hi, tail - tail_hi, lines, rest], 0
    )
    return stacked.T


SEG = 5 * HEAD_ROWS


def pair_masks(rows):
    lane = lax.broadcasted_iota(jnp.int32, (rows, 128), 1)
    return lane < 64, lane >= 64


def weight_copies(arrays, meta, column, width, deep, table, goal, sems):
    copies = []
    for at, (array, source, rows, slot, first, by_walk, lack) in enumerate(meta):
        row = slot * deep + first
        if by_walk:
            row = pl.multiple_of(table[1 + slot] * deep + first, 32)
        copy = pltpu.make_async_copy(
            arrays[array].at[pl.ds(source, rows), pl.ds(column * width - lack, width)],
            goal.at[pl.ds(row, rows)],
            sems.at[at],
        )
        copies.append(copy)
    return copies


def start_weight(*where):
    copies = weight_copies(*where)
    for copy in copies:
        copy.start()
    return copies


def wait_weight(*where):
    wait_all(weight_copies(*where))


def wait_all(copies):
    for copy in copies:
        copy.wait()


def scan_block(x, raw, raw_u, sr, cp, bp, hp, spread_ref, y_ref, state_ref, held, x_tail, bc_tail):
    rows = x.shape[0]
    pairs = x.shape[1] // 128
    _, _, _, _, total, less, enter, tail = rates(raw_u, hp, sr)
    cols = as_columns(total, enter, tail, sr)
    marks = [cols[:, SEG + at : SEG + at + 1] for at in (3, 4, 5)]
    pre, _ = conv_parts(x, x_tail[...], cp, cp[4:5], marks)
    xc = pre * jax.nn.sigmoid(pre)
    x_tail[...] = x[rows - 8 :]
    pre_bc, _ = conv_parts(raw, bc_tail[...], bp, bp[4:5], marks)
    bc = (pre_bc * jax.nn.sigmoid(pre_bc)).astype(BF16)
    bc_tail[...] = raw[rows - 8 :]
    states = bc.shape[1] // 2
    b_rows, c_rows = bc[:, :states], bc[:, states:]

    cols_low = cols.astype(BF16)
    enter_x = dot(cols_low, spread_ref[0])
    tail_x = dot(cols_low, spread_ref[1])

    at_t = lax.broadcasted_iota(jnp.int32, (rows, rows), 0)
    at_s = lax.broadcasted_iota(jnp.int32, (rows, rows), 1)
    bar = jnp.where((cols[:, SEG : SEG + 1] == sr[0:1]) & (at_t >= at_s), 0.0, NEG)
    scores = dot_t(c_rows, b_rows)
    state = held[...]
    state_ref[0] = state
    entering = dot(c_rows, state.astype(BF16)) * enter_x
    half = rows // 2
    xl = xc.astype(BF16)
    low_mask, high_mask = pair_masks(rows)
    zero = jnp.zeros((rows, 128), BF16)
    for pair in range(pairs):
        span = slice(pair * 128, pair * 128 + 128)
        part = xl[:, span]
        acc = entering[:, span] + xc[:, span] * cp[5:6, span]
        early, late = acc[:half], acc[half:]
        for side, mask in ((0, low_mask), (1, high_mask)):
            head = 2 * pair + side
            column, line = cols[:, head : head + 1], less[head : head + 1]
            own = jnp.where(mask, part, zero)
            first = jnp.exp(column[:half] - line[:, :half] + bar[:half, :half]) * scores[:half, :half]
            second = jnp.exp(column[half:] - line + bar[half:]) * scores[half:]
            early = early + dot(first.astype(BF16), own[:half])
            late = late + dot(second.astype(BF16), own)
        acc = jnp.concatenate([early, late], 0)
        y_ref[0, :, span] = acc
    keep = enter_x[rows - 1 : rows]
    held[...] = state * keep + dot(
        b_rows.astype(F32).T.astype(BF16), (xc * tail_x).astype(BF16)
    )


def mix_backward(is_first, t_ref, *refs):
    (
        x_ref, xp_ref, bc_ref, bcp_ref, u_ref, sr_ref, y_ref, dy_ref, state_ref,
        cp_ref, bp_ref, hp_ref, spread_ref, heads_ref,
    ) = refs[:14]
    dx_ref, dbc_ref, du_ref, *carried = refs[-9:]
    gx_ref, gbc_ref, gh_ref, held, x_next, bc_next = carried
    rows = x_ref.shape[1]
    width = x_ref.shape[2]
    pairs = width // 128

    @pl.when(pl.program_id(0) == 0)
    def _():
        for at, ref in enumerate(carried):
            if is_first:
                ref[...] = refs[14][...] if at == 0 else jnp.zeros_like(ref)
            else:
                ref[...] = refs[17 + at][...]

    sr = sr_ref[0]
    cp, bp = cp_ref[0], bp_ref[...]
    u, dt, a, rate, total, less, enter, tail = rates(u_ref[0], hp_ref[0], sr)
    cols = as_columns(less, enter, tail, sr)
    marks = [cols[:, SEG + at : SEG + at + 1] for at in (3, 4, 5)]
    x = x_ref[0].astype(F32)
    pre, x_moved = conv_parts(x, xp_ref[0][8:].astype(F32), cp, cp[4:5], marks)
    sig = jax.nn.sigmoid(pre)
    xc = pre * sig
    raw = bc_ref[0]
    pre_bc, bc_moved = conv_parts(raw, bcp_ref[0], bp, bp[4:5], marks)
    sig_bc = jax.nn.sigmoid(pre_bc)
    bc = (pre_bc * sig_bc).astype(BF16)
    states = bc.shape[1] // 2
    b_rows, c_rows = bc[:, :states], bc[:, states:]

    cols_low = cols.astype(BF16)
    enter_x = dot(cols_low, spread_ref[0])
    tail_x = dot(cols_low, spread_ref[1])
    keep = enter_x[rows - 1 : rows]

    at_s = lax.broadcasted_iota(jnp.int32, (rows, rows), 0)
    at_t = lax.broadcasted_iota(jnp.int32, (rows, rows), 1)
    bar = jnp.where((cols[:, SEG : SEG + 1] == sr[0:1]) & (at_t >= at_s), 0.0, NEG)
    scores = dot_t(b_rows, c_rows)

    dyl = dy_ref[0]
    dy = dyl.astype(F32)
    xl = xc.astype(BF16)
    state = state_ref[0]
    d_state = held[...]
    d_state_low = d_state.astype(BF16)
    entered = (dy * enter_x).astype(BF16)
    dc = dot_t(entered, state.astype(BF16))
    db = dot_t((xc * tail_x).astype(BF16), d_state_low)
    dx_tail = dot(b_rows, d_state_low) * tail_x
    x_round = xl.astype(F32)
    last_terms = jnp.sum(x_round * dx_tail, 0, keepdims=True) + keep * jnp.sum(
        state * d_state, 0, keepdims=True
    )
    held[...] = keep * d_state + dot(c_rows.astype(F32).T.astype(BF16), entered)

    low_mask, high_mask = pair_masks(rows)
    zero = jnp.zeros((rows, 128), BF16)
    half = rows // 2
    d_first = jnp.zeros((half, rows), F32)
    d_second = jnp.zeros((half, half), F32)
    d_scan = []
    for pair in range(pairs):
        span = slice(pair * 128, pair * 128 + 128)
        part, grad = xl[:, span], dyl[:, span]
        acc = dx_tail[:, span]
        early, late = acc[:half], acc[half:]
        for side, mask in ((0, low_mask), (1, high_mask)):
            head = 2 * pair + side
            column, line = cols[:, head : head + 1], total[head : head + 1]
            own, own_grad = jnp.where(mask, part, zero), jnp.where(mask, grad, zero)
            first = jnp.exp(line - column[:half] + bar[:half])
            second = jnp.exp(line[:, half:] - column[half:] + bar[half:, half:])
            d_first = d_first + first * dot_t(own[:half], grad)
            d_second = d_second + second * dot_t(own[half:], grad[half:])
            early = early + dot((first * scores[:half]).astype(BF16), own_grad)
            late = late + dot((second * scores[half:, half:]).astype(BF16), own_grad[half:])
        d_scan.append(jnp.concatenate([early, late], 0))
    d_scores = jnp.concatenate([jnp.zeros((half, half), F32), d_second], 1)
    d_scores = jnp.concatenate([d_first, d_scores], 0)
    d_scan = jnp.concatenate(d_scan, 1)
    db = db + dot(d_scores.astype(BF16), c_rows)
    dc = dc + dot(d_scores.T.astype(BF16), b_rows)

    skip = cp[5:6]
    from_x = x_round * d_scan
    from_t = dy * (y_ref[0] - skip * xc) - from_x
    row_at = lax.broadcasted_iota(jnp.int32, (rows, width), 0)
    from_t = from_t + jnp.where(row_at == rows - 1, last_terms, 0.0)

    def per_head(value):
        high = value.astype(BF16)
        return dot_t(heads_ref[...], high) + dot_t(
            heads_ref[...], (value - high.astype(F32)).astype(BF16)
        )

    q = per_head(from_x)
    da = shifted_sum(per_head(from_t), -1)
    slope = jax.nn.sigmoid(u)
    ratio = jnp.where(u < -15.0, 1.0, slope / dt)
    du = q * ratio - da * rate * slope
    du_ref[0] = du
    gh_ref[0] += jnp.sum(du, 1, keepdims=True)
    gh_ref[1] += jnp.sum(da * a, 1, keepdims=True)
    both = jnp.concatenate([gh_ref[0], gh_ref[1], jnp.zeros((128 - 2 * HEAD_ROWS, 128), F32)], 0)
    gx_ref[7:8, 0:128] = both.T[0:1]

    def conv_back(d_out, cur, moved, weight, carried, grads):
        grads[3:4] += jnp.sum(d_out * cur, 0, keepdims=True)
        grads[4:5] += jnp.sum(d_out, 0, keepdims=True)
        result = d_out * weight[3:4]
        for back in (1, 2, 3):
            kept = d_out * marks[back - 1]
            grads[3 - back : 4 - back] += jnp.sum(kept * moved[back - 1], 0, keepdims=True)
            ext = jnp.concatenate([kept, carried[back - 1]], 0)
            result = result + ext[back : back + rows] * weight[3 - back : 4 - back]
            carried[back - 1] = kept[:8]
        return result

    gx_ref[5:6] += jnp.sum(dy * xc, 0, keepdims=True)
    d_pre = (d_scan + skip * dy) * (sig * (1.0 + pre * (1.0 - sig)))
    dx_ref[0] = conv_back(d_pre, x, x_moved, cp, x_next, gx_ref).astype(BF16)
    d_bc = jnp.concatenate([db, dc], 1) * (sig_bc * (1.0 + pre_bc * (1.0 - sig_bc)))
    dbc_ref[0] = conv_back(d_bc, raw, bc_moved, bp, bc_next, gbc_ref).astype(BF16)


def input_backward(n_x, meta_x, n_z, meta_z, cols_xz, t_ref, *refs):
    dx_ref, dz_ref, dbc_ref, du_ref, rows_ref, wbc_ref, wdt_ref = refs[:7]
    x_parts, z_parts = refs[7 : 7 + n_x], refs[7 + n_x : 7 + n_x + n_z]
    send_ref, keep_ref, gdt_ref, gn_ref, wx, wz, sem_x, sem_z = refs[7 + n_x + n_z :]
    step = pl.program_id(0)
    width = wx.shape[1]
    deep = wx.shape[0] // (t_ref.shape[0] - 1)

    @pl.when(step == 0)
    def _():
        copies = start_weight(z_parts, meta_z, cols_xz[1], width, deep, t_ref, wz, sem_z)
        start_weight(x_parts, meta_x, cols_xz[0], width, deep, t_ref, wx, sem_x)
        wait_all(copies)
        gdt_ref[...] = jnp.zeros_like(gdt_ref)
        gn_ref[...] = jnp.zeros_like(gn_ref)

    normed = rows_ref[0]
    du = du_ref[0]
    gdt_ref[...] += dot(du.astype(BF16), normed)
    total = dot_t(dz_ref[0], wz[...]) + dot_t(dbc_ref[0], wbc_ref[...])

    @pl.when(step == 0)
    def _():
        wait_weight(x_parts, meta_x, cols_xz[0], width, deep, t_ref, wx, sem_x)

    total = total + dot_t(dx_ref[0], wx[...])
    du_cols = jnp.concatenate([du, jnp.zeros((128 - du.shape[0], du.shape[1]), F32)], 0).T
    total = total + dot(du_cols.astype(BF16), wdt_ref[...])
    gn_ref[...] += jnp.sum(total * normed.astype(F32), 0, keepdims=True)
    out = total.astype(BF16)

    @pl.when(step < 2)
    def _():
        send_ref[0] = out

    @pl.when(step >= 2)
    def _():
        keep_ref[0] = out


def project_scan(n_x, meta_x, col_x, with_norm, t_ref, *refs):
    slots, refs = refs[:4], refs[4:]
    gain_ref, wbc_ref, wdt_ref, sr_ref, cp_ref, bp_ref, hp_ref, spread_ref = refs[:8]
    refs = refs[8:]
    x_parts, refs = refs[:n_x], refs[n_x:]
    rows_ref, x_ref, bc_ref, u_ref, y_ref, state_ref = refs[:6]
    held, x_tail, bc_tail, wx, r_s, x_s, bc_s, u_s, sem_x = refs[6:]
    step = pl.program_id(0)
    blocks = x_s.shape[0]
    deep = wx.shape[0] // (t_ref.shape[0] - 1)

    def weights():
        return start_weight(x_parts, meta_x, col_x, wx.shape[1], deep, t_ref, wx, sem_x)

    for at in range(4):

        @pl.when(step == at)
        def _():
            copies = weights() if at == 0 else []
            value = slots[at][...]
            if with_norm:
                value = value.astype(F32)
                scale = lax.rsqrt(jnp.mean(value * value, -1, keepdims=True) + EPS)
                value = (value * scale * gain_ref[...]).astype(BF16)
            r_s[...] = value
            wait_all(copies)

    @pl.when(step < blocks)
    def _():
        value = r_s[...]
        rows_ref[0] = value
        x = dot(value, wx[...])
        bc = dot(value, wbc_ref[...])
        u = dot_t(wdt_ref[...][:HEAD_ROWS], value)
        x = x.astype(BF16)
        x_ref[0], bc_ref[0], u_ref[0] = x, bc, u
        x_s[step], bc_s[step], u_s[step] = x.astype(F32), bc, u

    @pl.when(step == blocks)
    def _():
        held[...] = jnp.zeros_like(held)
        x_tail[...] = jnp.zeros_like(x_tail)
        bc_tail[...] = jnp.zeros_like(bc_tail)

    @pl.when(step >= blocks)
    def _():
        slot = (step - blocks) ^ t_ref[0]
        scan_block(
            x_s[slot], bc_s[slot], u_s[slot], sr_ref[0], cp_ref[0], bp_ref[...], hp_ref[0], spread_ref,
            y_ref, state_ref, held, x_tail, bc_tail,
        )


def lane_columns(columns, rows):
    lane = lax.broadcasted_iota(jnp.int32, (rows, 128), 1)
    result = jnp.zeros((rows, 128), F32)
    for at, column in enumerate(columns):
        result = jnp.where(lane == at, column, result)
    return result


def three_parts(value):
    high = value.astype(BF16).astype(F32)
    rest = value - high
    middle = rest.astype(BF16).astype(F32)
    return [high, middle, rest - middle]


def gate_forward(n_z, meta_z, n_o, meta_o, cols_zo, is_last, t_ref, *refs):
    rows_ref, y_ref, gain_ref = refs[:3]
    refs = refs[3:]
    cots = ()
    if is_last:
        cots, refs = refs[:4], refs[4:]
    z_parts, refs = refs[:n_z], refs[n_z:]
    o_parts, refs = refs[:n_o], refs[n_o:]
    z_ref, send_ref, keep_ref = refs[:3]
    refs = refs[3:]
    if is_last:
        cot_ref, dg_ref, sums_ref = refs[:3]
        refs = refs[3:]
    wz, wo, sem_z, sem_o = refs
    step = pl.program_id(0)
    width = wz.shape[1]
    deep = wz.shape[0] // (t_ref.shape[0] - 1)

    @pl.when(step == 0)
    def _():
        copies = start_weight(z_parts, meta_z, cols_zo[0], width, deep, t_ref, wz, sem_z)
        start_weight(o_parts, meta_o, cols_zo[1], width, deep, t_ref, wo, sem_o)
        wait_all(copies)

    z = dot(rows_ref[0], wz[...]).astype(BF16)

    @pl.when(step == 0)
    def _():
        wait_weight(o_parts, meta_o, cols_zo[1], width, deep, t_ref, wo, sem_o)

    z_ref[0] = z
    z = z.astype(F32)
    v = y_ref[0] * (z * jax.nn.sigmoid(z))
    gain = gain_ref[0][6:7]
    squares = jnp.sum(v * v, -1, keepdims=True)
    scaled = v * gain
    part = dot_t(scaled.astype(BF16), wo[...]).astype(BF16)
    features = wz.shape[0]
    rows = z.shape[0]

    def put(ref):
        ref[0, :, :features] = part
        if not is_last:
            ref[0, :, features:] = lane_columns(three_parts(squares), rows).astype(BF16)

    @pl.when(step < 2)
    def _():
        put(send_ref)

    @pl.when(step >= 2)
    def _():
        put(keep_ref)

    if is_last:
        for at, slot in enumerate((1, 3, 0, 2)):

            @pl.when(step == at)
            def _():
                cot_ref[0] = cots[slot][...]

        d_gated = dot(cot_ref[0], wo[...])
        dg_ref[0] = d_gated.astype(BF16)
        cross = jnp.sum(d_gated * scaled, -1, keepdims=True)
        sums_ref[0] = lane_columns([squares, cross], rows).T[:8]


def gate_backward(n_o, meta_o, col_o, is_last, inner, t_ref, *refs):
    z_ref, y_ref, gain_ref = refs[:3]
    refs = refs[3:]
    if is_last:
        dg_ref, sums_ref = refs[:2]
        refs = refs[2:]
        dy_ref, dz_ref, gated_ref, gg_ref = refs
    else:
        cots, refs = refs[:4], refs[4:]
        o_parts, refs = refs[:n_o], refs[n_o:]
        dy_ref, dz_ref, gated_ref, gg_ref, cot_ref, wo, extra_s, sem_o = refs
    step = pl.program_id(0)

    @pl.when(step == 0)
    def _():
        gg_ref[...] = jnp.zeros_like(gg_ref)
        if not is_last:
            deep = wo.shape[0] // (t_ref.shape[0] - 1)
            wait_all(
                start_weight(o_parts, meta_o, col_o, wo.shape[1], deep, t_ref, wo, sem_o)
            )

    if is_last:
        d_gated = dg_ref[0].astype(F32)
        sums = sums_ref[0]
        cols = jnp.concatenate([sums, jnp.zeros((120, sums.shape[1]), F32)], 0).T
        scale = lax.rsqrt(cols[:, 0:1] / inner + EPS)
        cross = cols[:, 1:2]
    else:
        features = wo.shape[0]
        for at in range(4):

            @pl.when(step == at)
            def _():
                cot_ref[0] = cots[at][:, :features]
                extra_s[...] = cots[at][:, features:].astype(F32)

        d_gated = dot(cot_ref[0], wo[...])
        extra = extra_s[...]
        scale = extra[:, 0:1] + extra[:, 1:2] + extra[:, 2:3]
        cross = extra[:, 3:4] + extra[:, 4:5] + extra[:, 5:6]
    z, y, gain = z_ref[0].astype(F32), y_ref[0], gain_ref[0][6:7]
    sig = jax.nn.sigmoid(z)
    silu = z * sig
    v = y * silu
    normed = v * scale
    gated_ref[0] = (normed * gain).astype(BF16)
    gg_ref[6:7] += jnp.sum(d_gated * normed, 0, keepdims=True)
    dv = d_gated * gain * scale - v * (scale * scale * scale * cross / inner)
    dy_ref[0] = (dv * silu).astype(BF16)
    dz_ref[0] = (dv * y * (sig * (1.0 + z * (1.0 - sig)))).astype(BF16)


def layer_spec(array, k):
    return pl.BlockSpec((1,) + array.shape[1:], lambda at, t: (k,) + (0,) * (array.ndim - 1))


def whole_spec(shape):
    return pl.BlockSpec(shape, lambda at, t: (0,) * len(shape))


ANY = pl.BlockSpec(memory_space=pl.ANY)


def call(body, table, grid, ins, in_specs, outs, out_specs, scratch, flops, name, aliases=None):
    size = sum(item.size * item.dtype.itemsize for item in list(ins) + list(outs))
    return pl.pallas_call(
        body,
        grid_spec=pltpu.PrefetchScalarGridSpec(
            num_scalar_prefetch=1,
            grid=(grid,),
            in_specs=in_specs,
            out_specs=out_specs,
            scratch_shapes=scratch,
        ),
        out_shape=outs,
        compiler_params=pltpu.CompilerParams(
            dimension_semantics=("arbitrary",), vmem_limit_bytes=SMALL if grid == 1 else VMEM
        ),
        cost_estimate=pl.CostEstimate(flops=flops, bytes_accessed=size, transcendentals=0),
        name=name,
        input_output_aliases=aliases or {},
    )(table, *ins)


def run_project(k, table, slots, gain, w_bc, w_dt, lines, params, bc_params, spread, weight, col, norm):
    blocks = len(slots)
    rows, features = slots[0].shape
    wide = w_bc.shape[1]
    chan, head = params
    width = chan.shape[2]
    states = wide // 2
    last = blocks - 1

    def early(shape):
        return pl.BlockSpec((1,) + shape, lambda at, t: (jnp.minimum(at, last), 0, 0))

    def block(shape):
        return pl.BlockSpec((1,) + shape, lambda at, t: (jnp.maximum(at - blocks, 0), 0, 0))

    def slot(shape):
        return pl.BlockSpec((1,) + shape, lambda at, t: (jnp.maximum(at - blocks, 0) ^ t[0], 0, 0))

    ins = [*slots, gain, w_bc, w_dt, lines, chan, bc_params, head, spread, *weight[0]]
    in_specs = [whole_spec(item.shape) for item in slots]
    in_specs += [whole_spec(item.shape) for item in (gain, w_bc, w_dt)]
    in_specs += [block((8, rows)), layer_spec(chan, k), whole_spec(bc_params.shape)]
    in_specs += [layer_spec(head, k), whole_spec(spread.shape)] + [ANY] * len(weight[0])
    outs = [
        jax.ShapeDtypeStruct((blocks, rows, features), BF16),
        jax.ShapeDtypeStruct((blocks, rows, width), BF16),
        jax.ShapeDtypeStruct((blocks, rows, wide), F32),
        jax.ShapeDtypeStruct((blocks, HEAD_ROWS, rows), F32),
        jax.ShapeDtypeStruct((blocks, rows, width), F32),
        jax.ShapeDtypeStruct((blocks, states, width), F32),
    ]
    out_specs = [
        early((rows, features)), early((rows, width)), early((rows, wide)),
        early((HEAD_ROWS, rows)), slot((rows, width)), block((states, width)),
    ]
    scratch = [
        pltpu.VMEM((states, width), F32),
        pltpu.VMEM((8, width), F32),
        pltpu.VMEM((8, wide), F32),
        pltpu.VMEM((features, width), BF16),
        pltpu.VMEM((rows, features), BF16),
        pltpu.VMEM((blocks, rows, width), F32),
        pltpu.VMEM((blocks, rows, wide), F32),
        pltpu.VMEM((blocks, HEAD_ROWS, rows), F32),
        pltpu.SemaphoreType.DMA((len(weight[1]),)),
    ]
    body = partial(project_scan, len(weight[0]), weight[1], col, norm)
    return call(body, table, 2 * blocks, ins, in_specs, outs, out_specs, scratch, 10**10, "project_scan")


def run_gate_forward(k, table, rows, y, chan, cots, w_z, w_o, cols):
    blocks, count, features = rows.shape
    width = y.shape[2]
    is_last = cots is not None
    extra = 0 if is_last else 128

    def slot(shape):
        return pl.BlockSpec((1,) + shape, lambda at, t: (2 * at + 1 - 5 * (at // 2), 0, 0))

    cots = cots or []
    ins = [rows, y, chan, *cots, *w_z[0], *w_o[0]]
    in_specs = [slot((count, features)), slot((count, width)), layer_spec(chan, k)]
    in_specs += [whole_spec(item.shape) for item in cots] + [ANY] * (len(w_z[0]) + len(w_o[0]))
    half = jax.ShapeDtypeStruct((2, count, features + extra), BF16)
    outs = [jax.ShapeDtypeStruct((blocks, count, width), BF16), half, half]
    out_specs = [
        slot((count, width)),
        pl.BlockSpec((1, count, features + extra), lambda at, t: (jnp.minimum(at, 1), 0, 0)),
        pl.BlockSpec((1, count, features + extra), lambda at, t: (jnp.maximum(at - 2, 0), 0, 0)),
    ]
    if is_last:
        outs += [
            jax.ShapeDtypeStruct((blocks, count, features), BF16),
            jax.ShapeDtypeStruct((blocks, count, width), BF16),
            jax.ShapeDtypeStruct((blocks, 8, count), F32),
        ]
        out_specs += [slot((count, features)), slot((count, width)), slot((8, count))]
    scratch = [
        pltpu.VMEM((features, width), BF16),
        pltpu.VMEM((features, width), BF16),
        pltpu.SemaphoreType.DMA((len(w_z[1]),)),
        pltpu.SemaphoreType.DMA((len(w_o[1]),)),
    ]
    body = partial(gate_forward, len(w_z[0]), w_z[1], len(w_o[0]), w_o[1], cols, is_last)
    return call(body, table, blocks, ins, in_specs, outs, out_specs, scratch, 6 * 10**9, "gate_forward")


def run_gate_backward(k, table, z, y, chan, known, cots, w_o, col, inner):
    blocks, count, width = z.shape
    is_last = cots is None

    def slot(shape):
        return pl.BlockSpec((1,) + shape, lambda at, t: (at, 0, 0))

    ins = [z, y, chan]
    in_specs = [slot((count, width)), slot((count, width)), layer_spec(chan, k)]
    outs = [
        jax.ShapeDtypeStruct((blocks, count, width), BF16),
        jax.ShapeDtypeStruct((blocks, count, width), BF16),
        jax.ShapeDtypeStruct((blocks, count, width), BF16),
        jax.ShapeDtypeStruct((8, width), F32),
    ]
    out_specs = [slot((count, width))] * 3 + [whole_spec((8, width))]
    scratch = []
    if is_last:
        ins += list(known)
        in_specs += [slot((count, width)), slot((8, count))]
    else:
        features = cots[0].shape[1] - 128
        ins += [*cots, *w_o[0]]
        in_specs += [whole_spec(item.shape) for item in cots] + [ANY] * len(w_o[0])
        outs.append(jax.ShapeDtypeStruct((blocks, count, features), BF16))
        out_specs.append(slot((count, features)))
        scratch = [
            pltpu.VMEM((features, width), BF16),
            pltpu.VMEM((count, 128), F32),
            pltpu.SemaphoreType.DMA((len(w_o[1]),)),
        ]
    body = partial(gate_backward, len(w_o[0]), w_o[1], col, is_last, inner)
    return call(body, table, blocks, ins, in_specs, outs, out_specs, scratch, 3 * 10**9, "gate_backward")


def run_mix_backward(k, table, x, bc, u, lines, y, dy, state, params, bc_params, spread, heads_of, gg, top, steps, before):
    blocks, rows, width = x.shape
    wide = bc.shape[2]
    states = wide // 2
    chan, head = params

    def slot(shape):
        return pl.BlockSpec((1,) + shape, lambda at, t: ((top - at) ^ t[0], 0, 0))

    def earlier(shape):
        return pl.BlockSpec(
            (1,) + shape,
            lambda at, t: (jnp.maximum(top - at - 1, 0) ^ t[0], rows // shape[0] - 1, 0),
        )

    def straight(shape):
        return pl.BlockSpec((1,) + shape, lambda at, t: (top - at, 0, 0))

    ins = [x, x, bc, bc, u, lines, y, dy, state, chan, bc_params, head, spread, heads_of]
    in_specs = [
        slot((rows, width)), earlier((16, width)), slot((rows, wide)), earlier((8, wide)),
        slot((HEAD_ROWS, rows)), straight((8, rows)),
        slot((rows, width)), slot((rows, width)), straight((states, width)),
        layer_spec(chan, k), whole_spec(bc_params.shape), layer_spec(head, k),
        whole_spec(spread.shape), whole_spec(heads_of.shape),
    ]
    outs = [
        jax.ShapeDtypeStruct((blocks, rows, width), BF16),
        jax.ShapeDtypeStruct((blocks, rows, wide), BF16),
        jax.ShapeDtypeStruct((blocks, HEAD_ROWS, rows), F32),
        jax.ShapeDtypeStruct((8, width), F32),
        jax.ShapeDtypeStruct((8, wide), F32),
        jax.ShapeDtypeStruct((2, HEAD_ROWS, 128), F32),
        jax.ShapeDtypeStruct((states, width), F32),
        jax.ShapeDtypeStruct((3, 8, width), F32),
        jax.ShapeDtypeStruct((3, 8, wide), F32),
    ]
    out_specs = [slot((rows, width)), slot((rows, wide)), slot((HEAD_ROWS, rows))]
    out_specs += [whole_spec(item.shape) for item in outs[3:]]
    aliases = {}
    if before:
        aliases = {1 + len(ins) + at: at for at in range(3)}
        ins += list(before)
        in_specs += [ANY] * 3 + [whole_spec(item.shape) for item in outs[3:]]
    else:
        ins.append(gg)
        in_specs.append(whole_spec(gg.shape))
    body = partial(mix_backward, not before)
    return call(body, table, steps, ins, in_specs, outs, out_specs, [], 2 * 10**9 * steps, "mix_backward", aliases)


def run_input_backward(table, dx, dz, dbc, du, normed, w_bc, w_dt, w_x, w_z, cols):
    blocks, rows, width = dx.shape
    features = normed.shape[2]
    wide = dbc.shape[2]

    def slot(shape):
        return pl.BlockSpec((1,) + shape, lambda at, t: (2 * at + 1 - 5 * (at // 2), 0, 0))

    ins = [dx, dz, dbc, du, normed, w_bc, w_dt, *w_x[0], *w_z[0]]
    in_specs = [slot((rows, width)), slot((rows, width)), slot((rows, wide)), slot((HEAD_ROWS, rows))]
    in_specs += [slot((rows, features)), whole_spec(w_bc.shape), whole_spec(w_dt.shape)]
    in_specs += [ANY] * (len(w_x[0]) + len(w_z[0]))
    half = jax.ShapeDtypeStruct((2, rows, features), BF16)
    outs = [
        half, half,
        jax.ShapeDtypeStruct((HEAD_ROWS, features), F32),
        jax.ShapeDtypeStruct((1, features), F32),
    ]
    out_specs = [
        pl.BlockSpec((1, rows, features), lambda at, t: (jnp.minimum(at, 1), 0, 0)),
        pl.BlockSpec((1, rows, features), lambda at, t: (jnp.maximum(at - 2, 0), 0, 0)),
        whole_spec((HEAD_ROWS, features)), whole_spec((1, features)),
    ]
    scratch = [
        pltpu.VMEM((features, width), BF16),
        pltpu.VMEM((features, width), BF16),
        pltpu.SemaphoreType.DMA((len(w_x[1]),)),
        pltpu.SemaphoreType.DMA((len(w_z[1]),)),
    ]
    body = partial(input_backward, len(w_x[0]), w_x[1], len(w_z[0]), w_z[1], cols)
    return call(body, table, blocks, ins, in_specs, outs, out_specs, scratch, 7 * 10**9, "input_backward")


def segment_lines(segment, blocks):
    rows = segment.shape[0] // blocks
    cut = segment.reshape(blocks, rows)
    ends = cut[:, -1:]
    before = jnp.concatenate([cut[:1, :1], ends[:-1]], 0)
    kinds = [cut.astype(F32), (cut == before).astype(F32), (cut == ends).astype(F32)]
    for back in (1, 2, 3):
        earlier = jnp.pad(segment, (back, 0), constant_values=-1)[: segment.shape[0]]
        kinds.append((segment == earlier).astype(F32).reshape(blocks, rows))
    at = jnp.arange(8)[None, :, None]
    lines = jnp.zeros((blocks, 8, rows), F32)
    for index, kind in enumerate(kinds):
        lines = jnp.where(at == index, kind[:, None], lines)
    return lines


def head_tables(heads, width):
    owner = np.arange(width)[None, :] // (width // heads)
    at = np.arange(128)[:, None]
    spread_enter = (at == owner + HEAD_ROWS) | (at == owner + 3 * HEAD_ROWS)
    spread_tail = (at == owner + 2 * HEAD_ROWS) | (at == owner + 4 * HEAD_ROWS)
    spread = np.stack([spread_enter, spread_tail]).astype(np.float32)
    owners = (at[:HEAD_ROWS] == owner).astype(np.float32)
    return jnp.asarray(spread, BF16), jnp.asarray(owners, BF16)


def norm_scale_of(values):
    return lax.rsqrt(jnp.mean(values * values, -1, keepdims=True) + EPS)


def shards(
    hidden, segment_ids, cotangent, norm_gain, in_zx, in_dt, in_bc, conv_x, conv_x_bias,
    conv_bc, conv_bc_bias, dt_bias, a_log, skip_d, gated_gain, out_wt,
):
    layers = in_zx.shape[0]
    count = lax.axis_size("fsdp")
    tp_count = lax.axis_size("tp")
    tp_at = lax.axis_index("tp").astype(jnp.int32)
    own, features = hidden.shape
    deep = in_zx.shape[1]
    width = in_zx.shape[3]
    heads = in_dt.shape[2]
    wide = in_bc.shape[2]
    bc_deep = in_bc.shape[1]
    shared = conv_bc.shape[1]
    taps = conv_bc.shape[2]
    inner = width * tp_count
    dt_lines = -(-deep * heads // wide)
    dt_rest = dt_lines * wide - deep * heads
    lines = -(-(bc_deep + dt_lines + 1) // 16) * 16
    table = placement(tp_at)

    packs, weights, wholes = [], [], []
    for k in range(layers):
        tiny = [conv_bc[k].reshape(-1), conv_bc_bias[k]]
        tiny = jnp.concatenate(tiny + ([norm_gain.reshape(-1)] if k == 0 else []))
        tiny = jnp.pad(tiny, (0, wide - tiny.shape[0]))[None]
        dt = jnp.pad(in_dt[k].T.reshape(-1), (0, dt_rest)).reshape(dt_lines, wide)
        pack = jnp.concatenate([in_bc[k], dt, tiny], 0)
        packs.append(jnp.pad(pack, ((0, lines - pack.shape[0]), (0, 0))))

    ring_x = RingGather(in_zx[0, :, 1])
    over = permute(hidden, "tp", 2)
    beside = permute(hidden, "tp", 1)
    ring_x.step()
    walk = is_walk()
    pack = double(packs[0][None, None, None, None, None], "tp", 2, 3)
    for k in range(1, layers):
        whole = lax.all_gather(packs[k], ("fsdp", "tp"), axis=0, tiled=False)
        packs[k] = whole.reshape((count, tp_count) + packs[k].shape)

    def whole_of(k, source, out):
        return jnp.concatenate([source[k, :, 1], source[k, :, 0], out[k]], 1)

    if walk:
        steps = ring_x.steps
        in_zx_late, out_wt_late, *steps[0] = lax.optimization_barrier((in_zx, out_wt) + tuple(steps[0]))
        ring_zo = RingGather(jnp.concatenate([in_zx_late[0, :, 0], out_wt_late[0]], 1))
        ring_x.step(pack)
        pack = double(after(pack, *steps[0]), "fsdp", 4, 0)
        ring_x.step(pack)
        ring_zo.step(*steps[1])
        pack = double(after(pack, *steps[1]), "fsdp", 2, 1)
        ring_x.step(pack)
        pack = double(after(pack, *steps[2]), "fsdp", 1, 2)
        ring_zo.step(pack, *steps[3])
        over = after(over, pack)
    else:
        in_zx_late, out_wt_late = in_zx, out_wt
        ring_zo = RingGather(jnp.concatenate([in_zx[0, :, 0], out_wt[0]], 1))
        pack = lax.all_gather(pack[0], "fsdp", axis=0, tiled=False)[:, None]
    packs[0] = pack = double(pack, "tp", 1, 4).reshape(count, tp_count, lines, wide)
    slots = [hidden, beside, over, permute(over, "tp", 1)]
    cot_over = permute(after(cotangent, pack), "tp", 2)
    cot_beside = permute(after(cotangent, pack), "tp", 1)
    table = after(table, pack, *ring_zo.last())
    ring_zo.step(table)

    lines_of = segment_lines(segment_ids[0], tp_count)
    spread, heads_of = head_tables(heads, width)
    w_bc, w_dt, gains, bc_params = [], [], [], []
    skips = jnp.repeat(skip_d, width // heads, axis=1)
    chan = jnp.stack([conv_x_bias, skips, gated_gain], 1)
    chan = jnp.concatenate([jnp.swapaxes(conv_x, 1, 2), chan], 1)
    chan = jnp.pad(chan, ((0, 0), (0, 1), (0, 0))).astype(F32)
    head = jnp.pad(jnp.stack([dt_bias, a_log], 2), ((0, 0), (0, HEAD_ROWS - heads), (0, 126)))
    params = (chan, head.astype(F32))

    def unpack(k):
        part = packs[k]
        w_bc.append(part[:, :, :bc_deep].reshape(features, wide))
        dt = pick(part[:, :, bc_deep : bc_deep + dt_lines], tp_at, 1)
        dt = dt.reshape(count, -1)[:, : heads * deep]
        dt = dt.reshape(count, heads, deep).swapaxes(0, 1).reshape(heads, features)
        w_dt.append(jnp.pad(dt, ((0, 128 - heads), (0, 0))))
        tiny = part[:, :, bc_deep + dt_lines]
        if k == 0:
            first = shared * (taps + 1)
            every = tiny[:, :, first : first + layers * bc_deep]
            every = every.reshape(features // bc_deep, layers, bc_deep).swapaxes(0, 1)
            gains.extend(every.reshape(layers, 1, features).astype(F32))
        taps_bc = tiny[:, :, : shared * taps].reshape(wide, taps).astype(F32)
        bias_bc = tiny[:, :, shared * taps : shared * (taps + 1)].reshape(1, wide).astype(F32)
        bc_params.append(jnp.pad(jnp.concatenate([taps_bc.T, bias_bc], 0), ((0, 3), (0, 0))))

    unpack(0)
    running = hidden.astype(F32)
    saved = []
    for k in range(layers):
        if k:
            normed = (running * norm_scale_of(running) * gains[k]).astype(BF16)
            over = permute(normed, "tp", 2)
            beside = permute(normed, "tp", 1)
            if walk:
                ring_all.step(normed)
                over, *ring_all.steps[2] = lax.optimization_barrier((over,) + tuple(ring_all.steps[2]))
                behind, ahead = ring_all.steps[2]
                last_x = ring_last(behind[:, :width], ahead[:, :width])
                last_zo = ring_last(behind[:, width:], ahead[:, width:])
            slots = [normed, beside, over, permute(over, "tp", 1)]
        if k == 0:
            w_x = ring_x.weight()
        elif walk:
            w_x = walk_weight(ring_all.own, ring_all.steps[:3] + [last_x])
        else:
            w_x = ring_all.weight()
        rows, x, bc, u, y, state = run_project(
            k, table, slots, gains[k], w_bc[k], w_dt[k], lines_of, params, bc_params[k], spread, w_x, 0, k == 0
        )
        if k == 0:
            y, cot_over, *_ = lax.optimization_barrier((y, cot_over) + tuple(ring_zo.last()))
            ring_zo.step(y)
            cots_last = [cotangent, cot_beside, cot_over, permute(cot_over, "tp", 1)]
            w_zo, cols_zo = ring_zo.weight(), (0, 1)
        else:
            w_zo, cols_zo = w_x, (1, 2)
            if walk:
                y, *last_zo = lax.optimization_barrier((y,) + tuple(last_zo))
                w_zo = walk_weight(ring_all.own, ring_all.steps[:3] + [tuple(last_zo)], width)
        weights.append((w_x, w_zo, cols_zo))
        entry = dict(rows=rows, x=x, bc=bc, u=u, y=y, state=state, h=running)
        is_last = k == layers - 1
        if not is_last:
            next_ring = RingGather(whole_of(k + 1, in_zx_late, out_wt_late))
            next_ring.step(*(ring_zo.last() if k == 0 else (y,)))
        z, send, keep, *more = run_gate_forward(
            k, table, rows, y, chan, cots_last if is_last else None, w_zo, w_zo, cols_zo
        )
        if not is_last and walk:
            send, z, packs[k + 1], *next_ring.steps[0] = lax.optimization_barrier(
                (send, z, packs[k + 1]) + tuple(next_ring.steps[0])
            )
        entry["z"] = z
        entry["near"] = near = permute(send, "tp", 1)
        if not is_last:
            ring_all = next_ring
            going = plus(keep[1], near[1])
            far = permute(going, "tp", 2)
            unpack(k + 1)
            far = after(far, w_bc[k + 1], w_dt[k + 1], bc_params[k + 1])
            if walk:
                ring_all.step(going)
                far, *ring_all.steps[1] = lax.optimization_barrier((far,) + tuple(ring_all.steps[1]))
        else:
            cot, d_gated, sums = more
            sums = tp_sum_slots(sums)
            far = permute(plus(keep[1], near[1]), "tp", 2)
            entry.update(cot=cot, d_gated=d_gated, sums=sums, far=far, parts=keep[0].astype(F32) + near[0].astype(F32))
        if not is_last:
            branch = keep[0].astype(F32) + near[0].astype(F32) + far.astype(F32)
            squares = jnp.sum(branch[:, features:], -1, keepdims=True)
            branch = branch[:, :features]
            scale = lax.rsqrt(squares / inner + EPS)
            entry.update(branch=branch, scale=scale)
            running = running + branch * scale
        saved.append(entry)

    grad_run = cotangent.astype(F32)
    parts = [None] * layers

    def small_sum(parts):
        d_bc, g_norm, gbc, g_dt, gx = (jnp.stack(item) for item in zip(*parts))
        room = (layers, count, tp_count)
        d_norm = (g_norm / jnp.stack(gains)).reshape(room + (bc_deep,))
        d_conv = gbc[:, : taps + 1].reshape((layers, taps + 1) + room[1:] + (shared,))
        d_conv = d_conv.transpose(0, 2, 3, 1, 4).reshape(room + ((taps + 1) * shared,))
        d_tiny = jnp.concatenate([d_norm, d_conv], 3).astype(BF16)
        d_tiny = jnp.pad(d_tiny, ((0, 0), (0, 0), (0, 0), (0, wide - d_tiny.shape[3])))
        d_pack = jnp.concatenate([d_bc.reshape(room + (bc_deep, wide)), d_tiny[:, :, :, None]], 3)
        d_pack = d_pack.transpose(1, 2, 0, 3, 4).reshape(count, tp_count, -1, wide)
        d_dt = g_dt[:, :heads].reshape(layers, heads, count, deep).transpose(2, 0, 1, 3)
        d_dt = jnp.pad(d_dt.reshape(count, layers, -1), ((0, 0), (0, 0), (0, dt_rest))).astype(BF16)
        return SmallSum(d_pack, d_dt.reshape(count, -1, wide), gx.reshape(-1, wide))

    sums_of = [None] * layers
    for k in reversed(range(layers)):
        item = saved[k]
        rows, z, y = item["rows"], item["z"], item["y"]
        w_x, w_zo, cols_zo = weights[k]
        if k == layers - 1:
            cot = item["cot"]
            dy, dz, gated, g_gain = run_gate_backward(
                k, table, z, y, chan, (item["d_gated"], item["sums"]), None, w_zo, cols_zo[1], inner
            )
        else:
            low = grad_run.astype(BF16)
            cross = jnp.sum(low.astype(F32) * item["branch"], -1, keepdims=True)
            extra = three_parts(item["scale"]) + three_parts(cross)
            extra = jnp.concatenate(extra, 1).astype(BF16)
            low = jnp.concatenate([low, jnp.pad(extra, ((0, 0), (0, 128 - 6)))], 1)
            over, beside = permute(low, "tp", 2), permute(low, "tp", 1)
            if walk:
                last_x = sums_of[k + 1][2]
                over = after(over, *ring_step(sums_of[k + 1], low))
                (over,) = ring_pin(sums_of[k + 1], over)
                ring_step([last_x], over)
            cots = [low, beside, over, permute(over, "tp", 1)]
            dy, dz, gated, g_gain, cot = run_gate_backward(
                k, table, z, y, chan, None, cots, w_zo, cols_zo[1], inner
            )
            if walk:
                (dy,) = ring_pin([last_x], dy)

        def weight_grad(left, right):
            result = lax.dot_general(
                left, right, (((0, 1), (0, 1)), ((), ())), preferred_element_type=F32
            )
            return result.astype(BF16)

        ring_o = RingSum(weight_grad(cot, gated).reshape(count, deep, width), table)
        ring_z = RingSum(weight_grad(rows, dz).reshape(count, deep, width), table)
        early = [ring_o, ring_z]
        rounds = early + ([last_x] if k < layers - 1 and walk else [])
        dy = after(dy, *ring_step(rounds, dy), ring_o.terms, ring_z.terms)
        if k == layers - 1:
            dy = after(dy, saved[k]["near"])
        splits = (tp_count,) if k else (tp_count // 2, tp_count - tp_count // 2)
        done, top = None, tp_count - 1
        for steps in splits:
            done = run_mix_backward(
                k, table, item["x"], item["bc"], item["u"], lines_of, y, dy, item["state"], params,
                bc_params[k], spread, heads_of, g_gain, top, steps, done,
            )
            top -= steps
            if top >= 0:
                done = list(done)
                (done[6],) = ring_pin(rounds, done[6])
                done[6] = after(done[6], *ring_step(rounds))
        dx, dbc, du, gx, gbc, gh = done[:6]
        (dx,) = ring_pin(rounds, dx)
        if k == layers - 1:
            dx, far = lax.optimization_barrier((dx, item["far"]))
            scale = lax.rsqrt(item["sums"][0, 0] / inner + EPS)[:, None]
            running = running + (item["parts"] + far.astype(F32)) * scale
        every = [ring_o, ring_z]
        if k == 0:
            ring_x = RingSum(weight_grad(rows, dx).reshape(count, deep, width), table)
            every.append(ring_x)
            sent = ring_step(every)
            dx_now = after(dx, *sent) if walk else dx
        else:
            sent = ring_step(every)
            dx_now = after(dx, *sent) if walk else dx
        send, keep, g_dt, g_norm = run_input_backward(
            table, dx_now, dz, dbc, du, rows, w_bc[k], w_dt[k], w_x, w_zo, (0, cols_zo[0])
        )
        parts[k] = [weight_grad(rows, dbc) if k else None, g_norm, gbc, g_dt, gx]
        if k == 0:
            (send,) = ring_pin(every, send)
            near = permute(send, "tp", 1)
            going = plus(keep[1], near[1])
            far = permute(going, "tp", 2)
            ring_step(every, going)
            (far,) = ring_pin(every, far)
            ring_step([ring_x], far)
            parts[k][0] = weight_grad(rows, after(dbc, far))
            small = small_sum(parts)
            got = small.over_core()
            (got,) = ring_pin([ring_x], got)
            last_sent = ring_step([ring_x])
            if walk:
                got = after(got, *last_sent)
                far = after(far, *last_sent)
            got = small.over_z(small.over_x(small.over_y(got)))
        else:
            (send,) = ring_pin(every, send)
            near = permute(send, "tp", 1)
            going = plus(keep[1], near[1])
            far = permute(going, "tp", 2)
            ring_step(every, going)
            ring_x = RingSum(weight_grad(rows, after(dx, going)).reshape(count, deep, width), table)
            far, ring_x.terms, parts[k][0] = ring_pin(every, far, ring_x.terms, parts[k][0])
        sums_of[k] = (ring_o, ring_z, ring_x)
        d_normed = keep[0].astype(F32) + near[0].astype(F32) + far.astype(F32)
        h = item["h"]
        inv = norm_scale_of(h)
        scaled = d_normed * gains[k]
        grad_run = (
            grad_run
            + inv * scaled
            - h * (inv**3 * (jnp.sum(scaled * h, -1, keepdims=True) / features))
        )

    d_pack, vector = small.result(got)
    d_dt = d_pack[layers * (bc_deep + 1) :].reshape(layers, -1)[:, : heads * deep]
    d_pack = d_pack[: layers * (bc_deep + 1)].reshape(layers, -1, wide)
    vector = vector.reshape(layers, 8, width)
    tiny = d_pack[:, bc_deep]
    conv = tiny[:, bc_deep : bc_deep + (taps + 1) * shared].reshape(layers, taps + 1, shared)
    zx, out = ring_results([ring for rings in sums_of for ring in rings])
    return (
        running,
        grad_run,
        tiny[:, :bc_deep],
        zx,
        d_dt.reshape(layers, heads, deep).swapaxes(1, 2),
        d_pack[:, :bc_deep],
        vector[:, :taps].swapaxes(1, 2),
        vector[:, taps],
        conv[:, :taps].swapaxes(1, 2),
        conv[:, taps],
        vector[:, 7, :heads],
        vector[:, 7, HEAD_ROWS : HEAD_ROWS + heads],
        jnp.sum(vector[:, 5].reshape(layers, heads, -1), 2),
        vector[:, 6],
        out,
    )


def solution(mesh):
    tokens = P(("fsdp", "tp"), None)
    split = P(None, ("fsdp", "tp"))
    rows = P(None, ("fsdp", "tp"), None)
    weights = (
        split,
        P(None, "fsdp", None, "tp"),
        P(None, "fsdp", "tp"),
        rows,
        P(None, "tp", None),
        P(None, "tp"),
        rows,
        split,
        P(None, "tp"),
        P(None, "tp"),
        P(None, "tp"),
        P(None, "tp"),
        P(None, "fsdp", "tp"),
    )
    return jax.shard_map(
        shards,
        mesh=mesh,
        in_specs=(tokens, P("fsdp", None), tokens) + weights,
        out_specs=(tokens, tokens) + weights,
        check_vma=False,
    )
```
